32 devices in a mesh: frame: 8 (over y, x, core), tile: 4 (over z).
Axes of the slice: x: 2, y: 2, z: 4, core: 2. Of those that a mesh axis runs over, the one named last changes fastest.
Arguments:
- tokens: bfloat16 [32, 256, 1024], P('frame', 'tile'), may hold values from -6 to 6
- out_grad: bfloat16 [32, 256, 1024], P('frame', 'tile'), may hold values from -6 to 6
- actions: int32 [32], P('frame'), may hold values from 0 to 7
- segments: int32 [32], replicated, may hold values from 0 to 3, never falling along the last dimension, each value on 1 to 16 neighbouring positions
- frame_mask: int32 [32], replicated, may hold values 0 or 1
- embed: float32 [8, 1024], replicated, may hold values from -3 to 3
- ln1_gain: float32 [1024], replicated, may hold values from 0.1 to 1.9
- ln1_shift: float32 [1024], replicated, may hold values from -1.5 to 1.5
- spatial_qkv: bfloat16 [1024, 3072], P('frame'), may hold values from -0.25 to 0.25
- spatial_out: bfloat16 [1024, 1024], P('frame'), may hold values from -0.5 to 0.5
- ln2_gain: float32 [1024], replicated, may hold values from 0.1 to 1.9
- ln2_shift: float32 [1024], replicated, may hold values from -1.5 to 1.5
- temporal_qkv: bfloat16 [1024, 3072], P('frame'), may hold values from -0.25 to 0.25
- temporal_out: bfloat16 [1024, 1024], P('frame'), may hold values from -0.25 to 0.25
- ln3_gain: float32 [1024], replicated, may hold values from 0.1 to 1.9
- ln3_shift: float32 [1024], replicated, may hold values from -1.5 to 1.5
- ffn_in: bfloat16 [1024, 4096], P('frame'), may hold values from -0.1875 to 0.1875
- ffn_in_bias: float32 [4096], replicated, may hold values from -2.5 to 2.5
- ffn_out: bfloat16 [4096, 1024], P('frame'), may hold values from -0.125 to 0.125
- ffn_out_bias: float32 [1024], replicated, may hold values from -1.5 to 1.5
Outputs:
- result: bfloat16 [32, 256, 1024], P('frame', 'tile')
- tokens_grad: bfloat16 [32, 256, 1024], P('frame', 'tile')
- embed_grad: float32 [8, 1024], replicated
- ln1_gain_grad: float32 [1024], replicated
- ln1_shift_grad: float32 [1024], replicated
- spatial_qkv_grad: float32 [1024, 3072], P('frame')
- spatial_out_grad: float32 [1024, 1024], P('frame')
- ln2_gain_grad: float32 [1024], replicated
- ln2_shift_grad: float32 [1024], replicated
- temporal_qkv_grad: float32 [1024, 3072], P('frame')
- temporal_out_grad: float32 [1024, 1024], P('frame')
- ln3_gain_grad: float32 [1024], replicated
- ln3_shift_grad: float32 [1024], replicated
- ffn_in_grad: float32 [1024, 4096], P('frame')
- ffn_in_bias_grad: float32 [4096], replicated
- ffn_out_grad: float32 [4096, 1024], P('frame')
- ffn_out_bias_grad: float32 [1024], replicated
The draws below stay inside these ranges and needn't reach their ends.
Inputs may be any that keep to these rules, and one draw needn't show every extreme that they name: `segments`: clip numbers never fall along the frames; each clip holds 1 to 16 consecutive frames and one holds exactly 16.
All inputs are finite; a program needn't handle non-finite values.
Results may differ from the reference program's by a relative error of at most 0.023.
Values may be sent and summed in bfloat16 or wider, within the bound.
A program may use at most 256 MiB of HBM per device.

```python
import math
import jax
import jax.numpy as jnp
import numpy as np
from jax import lax

D = 1024
HD = 64
FF = 4096
ACTS = 8
FRAME_TOK = 256
MAXLEN = 16
FRAMES = 32
CLIPS = 4


def plant(entries, own_key, least, top_value):
    index_at = [jax.random.randint(jax.random.fold_in(own_key, axis), (), 0, length) for axis, length in enumerate(entries.shape)]
    longest = entries.shape.index(max(entries.shape))
    next_to = index_at[:longest] + [(index_at[longest] + 1) % entries.shape[longest]] + index_at[longest + 1:]
    return entries.at[tuple(index_at)].set(least).at[tuple(next_to)].set(top_value)


def block_levels(key, dims, cuts, low, top_value):
    level = 1.0
    for axis_at, shards_of in cuts:
        heights = jax.random.uniform(jax.random.fold_in(jax.random.fold_in(key, 6), axis_at), (shards_of,), jnp.float32, low / len(cuts), top_value / len(cuts))
        level = level * jnp.repeat(jnp.exp(heights), dims[axis_at] // shards_of).reshape((-1,) + (1,) * (len(dims) - 1 - axis_at))
    return level


def split_up(count, total, reach, slope):
    weights = [(1 << 20) // math.isqrt(rank ** slope) + 1 for rank in range(2, count + 1)]
    rest, holding = total - reach - (count - 1), [1] * (count - 1)
    while rest > 0:
        candidates = [i for i in range(count - 1) if holding[i] < reach]
        mass, left = sum([weights[i] for i in candidates]), rest
        for i in candidates:
            more = min(reach - holding[i], max(1, left * weights[i] // mass), rest)
            holding[i] = holding[i] + more
            rest = rest - more
    return np.array([reach] + holding)


def uneven(own_key, amount, total, most, slope):
    if amount == 2:
        one = jax.random.randint(own_key, (), max(1, total - most), min(most, total - 1) + 1)
        return jnp.stack([one, total - one])
    sizes = jnp.asarray(split_up(amount, total, most, slope), jnp.int32)
    couples = (amount - 1) // 2
    source_of, sink = sizes[1:1 + 2 * couples:2], sizes[2:2 + 2 * couples:2]
    margin = jnp.minimum(source_of - 1, most - sink)
    passed = jax.random.randint(jax.random.fold_in(own_key, 1), (couples,), 0, 1 << 20) % (margin + 1)
    sizes = sizes.at[1:1 + 2 * couples:2].set(source_of - passed).at[2:2 + 2 * couples:2].set(sink + passed)
    return sizes[jax.random.permutation(jax.random.fold_in(own_key, 2), amount)]


def gaussian(key, extent, width, limit, cuts=(), held_as=jnp.bfloat16):
    result = jax.random.normal(key, extent, jnp.float32) * width
    if len(cuts) > 0:
        result = block_levels(key, extent, cuts, -0.22, 0.18) * result
    return jnp.clip(result, min=-limit, max=limit).astype(held_as)


def setup_inputs(seed: int = 0) -> dict:
    streams_of = jax.random.split(jax.random.key(seed), 21)
    tokens = gaussian(streams_of[0], (FRAMES, FRAME_TOK, D), 1.0, 6.0, ((0, 8), (1, 4)))
    out_grad = gaussian(streams_of[1], (FRAMES, FRAME_TOK, D), 1.0, 6.0, ((0, 8), (1, 4)))
    actions = plant(jax.random.randint(streams_of[2], (FRAMES,), 0, ACTS), jax.random.fold_in(streams_of[2], 1), 0, ACTS - 1).astype(jnp.int32)
    segments = jnp.searchsorted(jnp.cumsum(uneven(streams_of[3], CLIPS, FRAMES, MAXLEN, 1)), jnp.arange(FRAMES), side="right").astype(jnp.int32)
    frame_mask = plant((jax.random.randint(streams_of[4], (FRAMES,), 0, 4) < 3).astype(jnp.int32), jax.random.fold_in(streams_of[4], 1), 0, 1)
    embed = gaussian(streams_of[5], (ACTS, D), 0.5, 3.0, (), jnp.float32)
    ln1_gain = jnp.clip(1.0 + 0.18 * jax.random.normal(streams_of[6], (D,), jnp.float32), 0.1, 1.9)
    ln1_shift = gaussian(streams_of[7], (D,), 0.3, 1.5, (), jnp.float32)
    spatial_qkv = gaussian(streams_of[8], (D, 3 * D), (D // 2) ** -0.5, 0.25, ((0, 8),))
    spatial_out = gaussian(streams_of[9], (D, D), (D // 8) ** -0.5, 0.5, ((0, 8),))
    ln2_gain = jnp.clip(1.0 + 0.18 * jax.random.normal(streams_of[10], (D,), jnp.float32), 0.1, 1.9)
    ln2_shift = gaussian(streams_of[11], (D,), 0.3, 1.5, (), jnp.float32)
    temporal_qkv = gaussian(streams_of[12], (D, 3 * D), (D // 2) ** -0.5, 0.25, ((0, 8),))
    temporal_out = gaussian(streams_of[13], (D, D), (D // 2) ** -0.5, 0.25, ((0, 8),))
    ln3_gain = jnp.clip(1.0 + 0.18 * jax.random.normal(streams_of[14], (D,), jnp.float32), 0.1, 1.9)
    ln3_shift = gaussian(streams_of[15], (D,), 0.3, 1.5, (), jnp.float32)
    ffn_in = gaussian(streams_of[16], (D, FF), D ** -0.5, 0.1875, ((0, 8),))
    ffn_in_bias = gaussian(streams_of[17], (FF,), 0.5, 2.5, (), jnp.float32)
    ffn_out = gaussian(streams_of[18], (FF, D), (FF // 2) ** -0.5, 0.125, ((0, 8),))
    ffn_out_bias = gaussian(streams_of[19], (D,), 0.3, 1.5, (), jnp.float32)
    return dict(tokens=tokens, out_grad=out_grad, actions=actions, segments=segments, frame_mask=frame_mask, embed=embed, ln1_gain=ln1_gain, ln1_shift=ln1_shift, spatial_qkv=spatial_qkv, spatial_out=spatial_out, ln2_gain=ln2_gain, ln2_shift=ln2_shift, temporal_qkv=temporal_qkv, temporal_out=temporal_out, ln3_gain=ln3_gain, ln3_shift=ln3_shift, ffn_in=ffn_in, ffn_in_bias=ffn_in_bias, ffn_out=ffn_out, ffn_out_bias=ffn_out_bias)


highest = lax.Precision.HIGHEST

@jax.custom_vjp
def low(v):
    return lax.optimization_barrier(v.astype(jnp.bfloat16)).astype(jnp.float32)

@jax.custom_vjp
def low_back(v):
    return v

def low_keep(v):
    return (low(v), None)

def low_pass(kept, grad):
    return (grad,)

def back_keep(v):
    return (v, None)

def back_low(kept, grad):
    return (low(grad),)
low.defvjp(low_keep, low_pass)
low_back.defvjp(back_keep, back_low)

def layer_norm(hidden, gain, shift):
    mean_row = lax.optimization_barrier(jnp.mean(hidden, -1, keepdims=True))
    centred = hidden - mean_row
    variance = lax.optimization_barrier(jnp.mean(centred * centred, -1, keepdims=True))
    return centred * lax.rsqrt(variance + 1e-05) * gain + shift

def project(hidden, weight):
    return jnp.einsum('abd,de->abe', hidden, weight, precision=highest)

def spatial_block(hidden, gain, shift, w_qkv, w_out):
    frame_count, token_count, model_width = hidden.shape
    head_count = model_width // HD
    unit = low(layer_norm(hidden, gain, shift))
    packed = low_back(low(project(unit, w_qkv)))
    query = packed[..., :model_width].reshape(frame_count, token_count, head_count, HD)
    keys = packed[..., model_width:2 * model_width].reshape(frame_count, token_count, head_count, HD)
    values = packed[..., 2 * model_width:].reshape(frame_count, token_count, head_count, HD)
    scores = low_back(jnp.einsum('fqhd,fkhd->fhqk', query, keys, precision=highest) * HD ** (-0.5))
    weights_low = low(jax.nn.softmax(scores, axis=-1))
    mixed = jnp.einsum('fhqk,fkhd->fqhd', weights_low, values, precision=highest)
    mixed = low(low_back(mixed.reshape(frame_count, token_count, model_width)))
    return hidden + low_back(project(mixed, w_out))

def temporal_block(hidden, allowed, gain, shift, w_qkv, w_out):
    pos_count, frame_count, model_width = hidden.shape
    head_count = model_width // HD
    unit = low(layer_norm(hidden, gain, shift))
    packed = low_back(low(project(unit, w_qkv)))
    query = packed[..., :model_width].reshape(pos_count, frame_count, head_count, HD)
    keys = packed[..., model_width:2 * model_width].reshape(pos_count, frame_count, head_count, HD)
    values = packed[..., 2 * model_width:].reshape(pos_count, frame_count, head_count, HD)
    scores = low_back(jnp.einsum('pihd,pjhd->phij', query, keys, precision=highest) * HD ** (-0.5))
    masked = jnp.where(allowed[None, None], scores, -1e+30)
    weights_low = low(jax.nn.softmax(masked, axis=-1))
    mixed = jnp.einsum('phij,pjhd->pihd', weights_low, values, precision=highest)
    mixed = low(low_back(mixed.reshape(pos_count, frame_count, model_width)))
    return hidden + low_back(project(mixed, w_out))

def ffn_block(hidden, gain, shift, w_in, in_bias, w_out, out_bias):
    unit = low(layer_norm(hidden, gain, shift))
    pre = low_back(project(unit, w_in) + in_bias)
    active = low(jax.nn.gelu(pre, approximate=True))
    return hidden + low_back(project(active, w_out) + out_bias)

def reference(tokens, out_grad, actions, segments, frame_mask, embed, ln1_gain, ln1_shift, spatial_qkv, spatial_out, ln2_gain, ln2_shift, temporal_qkv, temporal_out, ln3_gain, ln3_shift, ffn_in, ffn_in_bias, ffn_out, ffn_out_bias):
    frame_total, frame_tokens, model_width = tokens.shape
    block_frames = math.gcd(frame_total, 16)
    pos_block = 16
    one_hot = (actions[:, None] == jnp.arange(ACTS, dtype=jnp.int32)[None, :]).astype(jnp.float32)
    index_frames = jnp.arange(frame_total, dtype=jnp.int32)
    allowed = (segments[:, None] == segments[None, :]) & (index_frames[None, :] <= index_frames[:, None])
    allowed = allowed & ((frame_mask[None, :] == 1) | (index_frames[None, :] == index_frames[:, None]))

    def forward(xf, emb, g1, s1, wqs, wos, g2, s2, wqt, wot, g3, s3, win, bin_, wout, bout):
        start = xf + jnp.dot(one_hot, emb, precision=highest)[:, None, :]
        blocks = start.reshape(frame_total // block_frames, block_frames, frame_tokens, model_width)
        after1 = lax.map(jax.checkpoint(lambda blk: spatial_block(blk, g1, s1, wqs, wos)), blocks)
        after1 = after1.reshape(frame_total, frame_tokens, model_width)
        turned = after1.transpose(1, 0, 2).reshape(frame_tokens // pos_block, pos_block, frame_total, model_width)
        after2 = lax.map(jax.checkpoint(lambda blk: temporal_block(blk, allowed, g2, s2, wqt, wot)), turned)
        after2 = after2.reshape(frame_tokens, frame_total, model_width).transpose(1, 0, 2)
        blocks = after2.reshape(frame_total // block_frames, block_frames, frame_tokens, model_width)
        final = lax.map(jax.checkpoint(lambda blk: ffn_block(blk, g3, s3, win, bin_, wout, bout)), blocks)
        return final.reshape(frame_total, frame_tokens, model_width)
    primals = (tokens.astype(jnp.float32), embed, ln1_gain, ln1_shift, spatial_qkv.astype(jnp.float32), spatial_out.astype(jnp.float32), ln2_gain, ln2_shift, temporal_qkv.astype(jnp.float32), temporal_out.astype(jnp.float32), ln3_gain, ln3_shift, ffn_in.astype(jnp.float32), ffn_in_bias, ffn_out.astype(jnp.float32), ffn_out_bias)
    output, pull = jax.vjp(forward, *primals)
    grads = pull(out_grad.astype(jnp.float32))
    return (output.astype(jnp.bfloat16), grads[0].astype(jnp.bfloat16), grads[1], grads[2], grads[3], grads[4], grads[5], grads[6], grads[7], grads[8], grads[9], grads[10], grads[11], grads[12], grads[13], grads[14], grads[15])
```

```python
import functools

import jax
import jax.numpy as jnp
from jax import lax
from jax.experimental import pallas as pl
from jax.experimental.pallas import tpu as pltpu
from jax.sharding import PartitionSpec as P

HD = 64
LANES = 128
EPS = 1e-5
MESH = pl.DeviceIdType.MESH
F32 = jnp.float32
BF16 = jnp.bfloat16
VMEM_SPEC = pl.BlockSpec(memory_space=pltpu.VMEM)
HBM_SPEC = pl.BlockSpec(memory_space=pltpu.HBM)


def params(**kw):
    return pltpu.CompilerParams(vmem_limit_bytes=58 * 1024 * 1024, **kw)


def at(j, size):
    return pl.ds(pl.multiple_of(j * size, size), size)


def each(n, fn):
    def step(i, carry):
        fn(i)
        return carry

    lax.fori_loop(0, n, step, 0)


def dot(a, b):
    return jnp.dot(a, b, preferred_element_type=F32)


def dot_nt(a, b):
    return lax.dot_general(a, b, (((1,), (1,)), ((), ())), preferred_element_type=F32)


def dot_tn(a, b):
    return lax.dot_general(a, b, (((0,), (0,)), ((), ())), preferred_element_type=F32)


def normed(h):
    cen = h - jnp.mean(h, -1, keepdims=True)
    inv = lax.rsqrt(jnp.mean(cen * cen, -1, keepdims=True) + EPS)
    return cen * inv, inv


ROWS = 32


def norm_rows(load, gain_ref, shift_ref, unit_ref):
    def step(i):
        rows = at(i, ROWS)
        xhat, _ = normed(load(rows))
        unit_ref[rows, :] = (xhat * gain_ref[...] + shift_ref[...]).astype(BF16)

    each(unit_ref.shape[0] // ROWS, step)


def fold(x):
    return jnp.sum(x.reshape(x.shape[0] // 8, 8, x.shape[1]), 0)


def norm_back(load, du_ref, gain_ref, dgain_ref, dshift_ref, acc_ref, store):
    acc_ref[...] = jnp.zeros_like(acc_ref)

    def step(i):
        rows = at(i, ROWS)
        xhat, inv = normed(load(rows))
        du = du_ref[rows, :]
        acc_ref[0] += fold(du * xhat)
        acc_ref[1] += fold(du)
        dx = du * gain_ref[...]
        dh = inv * (
            dx - jnp.mean(dx, -1, keepdims=True) - xhat * jnp.mean(dx * xhat, -1, keepdims=True)
        )
        store(rows, dh)

    each(du_ref.shape[0] // ROWS, step)
    dgain_ref[...] = jnp.sum(acc_ref[0], 0, keepdims=True)
    dshift_ref[...] = jnp.sum(acc_ref[1], 0, keepdims=True)


def head_masks():
    lane = lax.broadcasted_iota(jnp.int32, (1, LANES), 1)
    low = jnp.where(lane < HD, 1.0, 0.0)
    return low.astype(BF16), (1.0 - low).astype(BF16)


def head_probs(qm, k, bias_ref):
    s = dot_nt(qm, k) * (HD**-0.5)
    if bias_ref is not None:
        s = s + bias_ref[...]
    e = jnp.exp(s - jnp.max(s, -1, keepdims=True))
    return e * (1.0 / jnp.sum(e, -1, keepdims=True))


def attention(qkv_ref, bias_ref, mixed_ref):
    width = mixed_ref.shape[1]
    per = width // LANES
    masks = head_masks()

    def pair(p):
        q, k, v = (qkv_ref[:, at(p + i * per, LANES)] for i in range(3))
        out = 0.0
        for m in masks:
            out = out + dot(head_probs(q * m, k, bias_ref).astype(BF16), v * m)
        mixed_ref[:, at(p, LANES)] = out.astype(BF16)

    each(per, pair)


def attention_back(qkv_ref, bias_ref, dmix_ref, dqkv_ref):
    width = dmix_ref.shape[1]
    per = width // LANES
    masks = head_masks()
    scale = HD**-0.5

    def pair(p):
        q, k, v = (qkv_ref[:, at(p + i * per, LANES)] for i in range(3))
        dm = dmix_ref[:, at(p, LANES)]
        dq = dk = dv = 0.0
        for m in masks:
            qm = q * m
            dmm = dm * m
            probs = head_probs(qm, k, bias_ref)
            dp = dot_nt(dmm, v)
            ds = probs * (dp - jnp.sum(probs * dp, -1, keepdims=True))
            ds = ds.astype(BF16)
            dq = dq + dot(ds, k * m)
            dk = dk + dot_tn(ds, qm)
            dv = dv + dot_tn(probs.astype(BF16), dmm)
        dqkv_ref[:, at(p, LANES)] = (dq * scale).astype(BF16)
        dqkv_ref[:, at(p + per, LANES)] = (dk * scale).astype(BF16)
        dqkv_ref[:, at(p + 2 * per, LANES)] = dv.astype(BF16)

    each(per, pair)


def matmul(x_ref, w_ref, block, store):
    def step(j):
        cols = at(j, block)
        store(cols, dot(x_ref[...], w_ref[:, cols]))

    each(w_ref.shape[1] // block, step)


def matmul_nt(x_ref, w_ref, block, store):
    def step(j):
        rows = at(j, block)
        store(rows, dot_nt(x_ref[...], w_ref[rows, :]))

    each(w_ref.shape[0] // block, step)


def attn_fwd_kernel(masked, base_ref, added_ref, gain_ref, shift_ref, wqkv_ref, wo_ref, *rest):
    if masked:
        bias_ref, unit_ref, qkv_ref, mixed_ref, after_ref = rest
    else:
        bias_ref = None
        unit_ref, qkv_ref, mixed_ref, after_ref = rest

    def load(rows):
        return base_ref[rows, :].astype(F32) + added_ref[...]

    norm_rows(load, gain_ref, shift_ref, unit_ref)

    def put_qkv(cols, y):
        qkv_ref[:, cols] = y.astype(BF16)

    matmul(unit_ref, wqkv_ref, 512, put_qkv)
    attention(qkv_ref, bias_ref, mixed_ref)

    def put_after(cols, y):
        y = y + base_ref[:, cols].astype(F32) + added_ref[:, cols]
        after_ref[:, cols] = y.astype(after_ref.dtype)

    matmul(mixed_ref, wo_ref, 512, put_after)


def attn_fwd(base, added, gain, shift, wqkv, wo, bias, out_type, name):
    rows, width = base.shape
    ins = [base, added, gain, shift, wqkv, wo] + ([bias] if bias is not None else [])
    shapes = [(width, BF16), (3 * width, BF16), (width, BF16), (width, out_type)]
    return pl.pallas_call(
        functools.partial(attn_fwd_kernel, bias is not None),
        out_shape=[jax.ShapeDtypeStruct((rows, w), d) for w, d in shapes],
        in_specs=[VMEM_SPEC] * len(ins),
        out_specs=[VMEM_SPEC] * 4,
        compiler_params=params(),
        name=name,
    )(*ins)


def attn_bwd_kernel(masked, base_ref, added_ref, gain_ref, wqkv_ref, wo_ref, dout_ref, qkv_ref, *rest):
    if masked:
        bias_ref, *rest = rest
    else:
        bias_ref = None
    dlow_ref, dqkv_ref, dbase_ref, dgain_ref, dshift_ref, dmix_ref, du_ref, acc_ref = rest

    def cast(i):
        rows = at(i, ROWS)
        dlow_ref[rows, :] = dout_ref[rows, :].astype(BF16)

    each(dlow_ref.shape[0] // ROWS, cast)

    def put_mix(rows, y):
        dmix_ref[:, rows] = y.astype(BF16)

    matmul_nt(dlow_ref, wo_ref, 512, put_mix)
    attention_back(qkv_ref, bias_ref, dmix_ref, dqkv_ref)

    def put_du(rows, y):
        du_ref[:, rows] = y

    matmul_nt(dqkv_ref, wqkv_ref, 256, put_du)

    def load(rows):
        return base_ref[rows, :].astype(F32) + added_ref[...]

    def store(rows, dh):
        dbase_ref[rows, :] = (dout_ref[rows, :].astype(F32) + dh).astype(dbase_ref.dtype)

    norm_back(load, du_ref, gain_ref, dgain_ref, dshift_ref, acc_ref, store)


def attn_bwd(base, added, gain, wqkv, wo, dout, qkv, bias, out_type, name):
    rows, width = base.shape
    ins = [base, added, gain, wqkv, wo, dout, qkv] + ([bias] if bias is not None else [])
    outs = [
        jax.ShapeDtypeStruct((rows, width), BF16),
        jax.ShapeDtypeStruct((rows, 3 * width), BF16),
        jax.ShapeDtypeStruct((rows, width), out_type),
        jax.ShapeDtypeStruct((1, width), F32),
        jax.ShapeDtypeStruct((1, width), F32),
    ]
    return pl.pallas_call(
        functools.partial(attn_bwd_kernel, bias is not None),
        out_shape=outs,
        in_specs=[VMEM_SPEC] * len(ins),
        out_specs=[VMEM_SPEC] * len(outs),
        scratch_shapes=[
            pltpu.VMEM((rows, width), BF16),
            pltpu.VMEM((rows, width), F32),
            pltpu.VMEM((2, 8, width), F32),
        ],
        compiler_params=params(),
        name=name,
    )(*ins)


GELU_A = 0.7978845608
GELU_B = 0.044715


def ffn_fwd_kernel(after_ref, gain_ref, shift_ref, win_ref, bin_ref, wout_ref, bout_ref,
                   unit_ref, pre_ref, act_ref, res_ref):
    norm_rows(lambda rows: after_ref[rows, :], gain_ref, shift_ref, unit_ref)

    def put_pre(cols, y):
        v = y + bin_ref[:, cols]
        pre_ref[:, cols] = v
        act = 0.5 * v * (1.0 + jnp.tanh(GELU_A * (v + GELU_B * v * v * v)))
        act_ref[:, cols] = act.astype(BF16)

    matmul(unit_ref, win_ref, 512, put_pre)

    def put_res(cols, y):
        res_ref[:, cols] = (after_ref[:, cols] + y + bout_ref[:, cols]).astype(BF16)

    matmul(act_ref, wout_ref, 256, put_res)


def ffn_fwd(after, gain, shift, win, b_in, wout, b_out):
    rows, width = after.shape
    ff = win.shape[1]
    return pl.pallas_call(
        ffn_fwd_kernel,
        out_shape=[
            jax.ShapeDtypeStruct((rows, width), BF16),
            jax.ShapeDtypeStruct((rows, ff), F32),
            jax.ShapeDtypeStruct((rows, ff), BF16),
            jax.ShapeDtypeStruct((rows, width), BF16),
        ],
        in_specs=[VMEM_SPEC] * 7,
        out_specs=[VMEM_SPEC] * 4,
        compiler_params=params(),
        name="ffn_forward",
    )(after, gain, shift, win, b_in, wout, b_out)


def ffn_bwd_kernel(g_ref, pre_ref, after_ref, gain_ref, win_ref, wout_ref,
                   dpre_ref, dafter_ref, dgain_ref, dshift_ref, dbin_ref, dbout_ref, du_ref, acc_ref):
    def put_dpre(rows, y):
        v = pre_ref[:, rows]
        t = jnp.tanh(GELU_A * (v + GELU_B * v * v * v))
        slope = 0.5 * (1.0 + t) + 0.5 * v * (1.0 - t * t) * GELU_A * (1.0 + 3.0 * GELU_B * v * v)
        d = (y * slope).astype(BF16)
        dpre_ref[:, rows] = d
        dbin_ref[:, rows] = jnp.sum(d.astype(F32), 0, keepdims=True)

    matmul_nt(g_ref, wout_ref, 512, put_dpre)

    def put_du(rows, y):
        du_ref[:, rows] = y

    matmul_nt(dpre_ref, win_ref, 256, put_du)
    dbout_ref[...] = jnp.zeros_like(dbout_ref)

    def store(rows, dh):
        g = g_ref[rows, :].astype(F32)
        dafter_ref[rows, :] = g + dh
        dbout_ref[...] += jnp.sum(g, 0, keepdims=True)

    norm_back(lambda rows: after_ref[rows, :], du_ref, gain_ref, dgain_ref, dshift_ref, acc_ref, store)


def ffn_bwd(g, pre, after, gain, win, wout):
    rows, width = after.shape
    ff = win.shape[1]
    row = lambda n: jax.ShapeDtypeStruct((1, n), F32)
    return pl.pallas_call(
        ffn_bwd_kernel,
        out_shape=[
            jax.ShapeDtypeStruct((rows, ff), BF16),
            jax.ShapeDtypeStruct((rows, width), F32),
            row(width), row(width), row(ff), row(width),
        ],
        in_specs=[VMEM_SPEC] * 6,
        out_specs=[VMEM_SPEC] * 6,
        scratch_shapes=[pltpu.VMEM((rows, width), F32), pltpu.VMEM((2, 8, width), F32)],
        compiler_params=params(),
        name="ffn_backward",
    )(g, pre, after, gain, win, wout)


def wgrad_kernel(shard, left_ref, left2_ref, right_ref, right2_ref, out_ref, lt_ref):
    tok = left_ref.shape[0]
    lt_ref[:, :tok] = left_ref[...].T
    lt_ref[:, tok:] = left2_ref[...].T
    col_blocks = right_ref.shape[1] // 1024
    for rb in range(shard // 128):
        for cb in range(col_blocks):
            def step(j, rb=rb, cb=cb):
                cols = pl.ds(pl.multiple_of(cb * 1024 + j * 512, 512), 512)
                a = jnp.concatenate(
                    [lt_ref[q * shard + rb * 128 : q * shard + (rb + 1) * 128, :] for q in range(4)], 0
                )
                y = dot(a[:, :tok], right_ref[:, cols]) + dot(a[:, tok:], right2_ref[:, cols])
                y = y.astype(BF16)
                for q in range(4):
                    out_ref[rb * col_blocks + cb, q, :, at(j, 512)] = y[q * 128 : (q + 1) * 128]

            each(2, step)


def wgrad_units(left, right, shard, core, name):
    tok = left.shape[0]
    parts = left.reshape(tok, 4, 2, shard)
    mine = lax.dynamic_index_in_dim(parts, core, 2, False).reshape(tok, 4 * shard)
    other = lax.dynamic_index_in_dim(parts, 1 - core, 2, False).reshape(tok, 4 * shard)
    swap = [(i, i ^ 1) for i in range(8)]
    other = lax.ppermute(other, "frame", swap)
    right2 = lax.ppermute(right, "frame", swap)
    units = (shard // 128) * (right.shape[1] // 1024)
    return pl.pallas_call(
        functools.partial(wgrad_kernel, shard),
        out_shape=jax.ShapeDtypeStruct((units, 4, 128, 1024), BF16),
        in_specs=[VMEM_SPEC] * 4,
        out_specs=VMEM_SPEC,
        scratch_shapes=[pltpu.VMEM((4 * shard, 2 * tok), BF16)],
        compiler_params=params(),
        name=name,
    )(mine, other, right, right2)


def xor(a, b):
    bit = lax.rem(a // b, 2)
    return a + b - 2 * b * bit


def greet(partners):
    barrier = pltpu.get_barrier_semaphore()
    for p in partners:
        pl.semaphore_signal(barrier, inc=1, device_id=p, device_id_type=MESH)
    pl.semaphore_wait(barrier, len(partners))


def remote(src, dst, ssem, rsem, dev):
    return pltpu.make_async_remote_copy(
        src_ref=src, dst_ref=dst, send_sem=ssem, recv_sem=rsem, device_id=dev, device_id_type=MESH
    )


def xor_any(a, bits):
    for b in (1, 2, 4, 8, 16):
        if bits & b:
            a = xor(a, b)
    return a


def swap_kernel(axes, src_of, dst_of, src_ref, dst_ref, ssem, rsem, lsem):
    f = lax.axis_index("frame")
    t = lax.axis_index("tile")
    nf = 8 if "frame" in axes else 1
    nt = 4 if "tile" in axes else 1
    todo = [(a, b) for a in range(nf) for b in range(nt) if (a, b) != (0, 0)]
    devs = [(xor_any(f, a), xor_any(t, b)) for a, b in todo]
    greet(devs)
    own = pltpu.make_async_copy(src_ref.at[src_of(f, t)], dst_ref.at[dst_of(f, t)], lsem)
    own.start()
    for i, d in enumerate(devs):
        remote(src_ref.at[src_of(*d)], dst_ref.at[dst_of(f, t)], ssem.at[i], rsem.at[i], d).start()
    own.wait()
    for i, d in enumerate(devs):
        remote(src_ref.at[src_of(*d)], dst_ref.at[dst_of(*d)], ssem.at[i], rsem.at[i], d).wait()


def swap_blocks(x, shape, axes, src_of, dst_of, cid, name):
    n = (8 if "frame" in axes else 1) * (4 if "tile" in axes else 1)
    return pl.pallas_call(
        functools.partial(swap_kernel, axes, src_of, dst_of),
        out_shape=jax.ShapeDtypeStruct(shape, x.dtype),
        in_specs=[HBM_SPEC],
        out_specs=HBM_SPEC,
        scratch_shapes=[
            pltpu.SemaphoreType.DMA((n - 1,)),
            pltpu.SemaphoreType.DMA((n - 1,)),
            pltpu.SemaphoreType.DMA,
        ],
        compiler_params=params(collective_id=cid, has_side_effects=True),
        name=name,
    )(x)


def gather_chunks(shapes):
    out = []
    for i, (rows, cols) in enumerate(shapes):
        step = rows
        while step * cols > 200 * 1024 and step % 32 == 0:
            step //= 2
        out += [(i, r, step) for r in range(0, rows, step)]
    return out


def gather_kernel(n_arr, chunks, *refs):
    ins = refs[:n_arr]
    outs = refs[n_arr : 2 * n_arr]
    ssem, rsem, lsem = refs[2 * n_arr :]
    f = lax.axis_index("frame")
    t = lax.axis_index("tile")
    odd = lax.rem(t, 2)
    fx, fy = xor(f, 2), xor(f, 4)
    first = fx + (fy - fx) * odd
    second = fy + (fx - fy) * odd
    diag = xor_any(f, 6)
    tz = xor(t, 1)
    sib = xor(f, 1)
    to_sib, to_first, to_second, to_z = (sib, t), (first, t), (second, t), (f, tz)
    greet([to_sib, (fx, t), (fy, t), to_z])

    def piece(k, owner, chunk_only=True):
        a, r, n = chunks[k]
        return outs[a].at[pl.ds(pl.multiple_of(owner * ins[a].shape[0] + r, 16), n)]

    def own(k):
        a, r, n = chunks[k]
        return ins[a].at[pl.ds(r, n)]

    def copy(k, kind):
        dev = (to_first, to_second, to_z, to_sib, to_sib, to_sib, to_sib)[kind]
        owner = (f, first, first, f, first, diag, second)[kind]
        src = own(k) if kind in (0, 3) else piece(k, owner)
        return remote(src, piece(k, owner), ssem.at[k, kind], rsem.at[k, kind], dev)

    def arrived(k, kind):
        owner = (first, diag, second, sib, xor(first, 1), xor(diag, 1), xor(second, 1))[kind]
        dst = piece(k, owner)
        remote(dst, dst, ssem.at[k, kind], rsem.at[k, kind], to_sib).wait_recv()

    n = len(chunks)
    for k in range(n):
        pltpu.make_async_copy(own(k), piece(k, f), lsem.at[k]).start()
    for k in range(min(2, n)):
        copy(k, 0).start()
    for k in range(n + 1):
        if k < n:
            copy(k, 3).start()
            arrived(k, 0)
            if k + 2 < n:
                copy(k + 2, 0).start()
            for kind in (1, 2, 4):
                copy(k, kind).start()
        if k >= 1:
            for kind in (1, 2):
                arrived(k - 1, kind)
                copy(k - 1, kind + 4).start()
    for k in range(n):
        for kind in (3, 4, 5, 6):
            arrived(k, kind)
        for kind in range(7):
            copy(k, kind).wait_send()
        pltpu.make_async_copy(own(k), piece(k, f), lsem.at[k]).wait()


def gather_weights(mats):
    chunks = gather_chunks([m.shape for m in mats])
    n = len(mats)
    return pl.pallas_call(
        functools.partial(gather_kernel, n, chunks),
        out_shape=[jax.ShapeDtypeStruct((8 * m.shape[0], m.shape[1]), m.dtype) for m in mats],
        in_specs=[HBM_SPEC] * n,
        out_specs=[HBM_SPEC] * n,
        scratch_shapes=[
            pltpu.SemaphoreType.DMA((len(chunks), 7)),
            pltpu.SemaphoreType.DMA((len(chunks), 7)),
            pltpu.SemaphoreType.DMA((len(chunks),)),
        ],
        compiler_params=params(collective_id=0, has_side_effects=True),
        name="gather_weights",
    )(*mats)


def add_into(dst, a, b, rows):
    def step(i):
        r = at(i, 16)
        dst[r, :] = (a[r, :].astype(F32) + b[r, :].astype(F32)).astype(dst.dtype)

    each(rows // 16, step)


def reduce_kernel(units, n_arr, *refs):
    grads = refs[:n_arr]
    small_ref = refs[n_arr]
    out_ref, small_out = refs[n_arr + 1 : n_arr + 3]
    (g_ref, r1, r2, zin, zpeer, sm, smr, lsem, s1s, s1r, s2s, s2r, zs, zr, zps, zpr, sms, smrs) = refs[n_arr + 3 :]
    f = lax.axis_index("frame")
    t = lax.axis_index("tile")
    q = f // 2
    leaf = (t == 0) | (t == 3)
    inner = jnp.logical_not(leaf)
    fx, fy, sib = xor(f, 2), xor(f, 4), xor(f, 1)
    qx, qy, qd = xor(q, 1), xor(q, 2), xor_any(q, 3)
    to_x, to_y, to_sib, to_z, to_peer = (fx, t), (fy, t), (sib, t), (f, xor(t, 1)), (f, 3 - t)
    greet([to_x, to_y, to_sib, to_z, to_peer])
    n = len(units)

    def hop(u):
        return (to_x, qx, to_y, qy) if u % 2 == 0 else (to_y, qy, to_x, qx)

    def src(u, piece):
        a, i = units[u]
        return grads[a].at[i, piece]

    def local(u):
        dev1, p1, dev2, p2 = hop(u)
        return (
            pltpu.make_async_copy(src(u, q), g_ref.at[u, 0], lsem.at[u, 0]),
            pltpu.make_async_copy(src(u, p2), g_ref.at[u, 1], lsem.at[u, 1]),
        )

    def step1(u):
        dev1, p1, dev2, p2 = hop(u)
        return (
            remote(src(u, p1), r1.at[u, 0], s1s.at[u, 0], s1r.at[u, 0], dev1),
            remote(src(u, qd), r1.at[u, 1], s1s.at[u, 1], s1r.at[u, 1], dev1),
        )

    def step2(u):
        return remote(g_ref.at[u, 1], r2.at[u], s2s.at[u], s2r.at[u], hop(u)[2])

    def to_inner(u):
        return remote(g_ref.at[u, 0], zin.at[u], zs.at[u], zr.at[u], to_z)

    def across(u):
        return remote(g_ref.at[u, 0], zpeer.at[u], zps.at[u], zpr.at[u], to_peer)

    def to_leaf(u):
        return remote(r2.at[u], zin.at[u], zs.at[u], zr.at[u], to_z)

    def emit(u, ref):
        def step(i):
            r = at(i, 16)
            out_ref[u, r, :] = ref[u, r, :].astype(F32)

        each(8, step)

    for u in range(n):
        for c in local(u):
            c.start()
    for u in range(min(4, n)):
        for c in step1(u):
            c.start()
    sm[0] = small_ref[...]

    def small_copy(i, dev):
        return remote(sm.at[i], smr.at[i], sms.at[i], smrs.at[i], dev)

    hops = (to_sib, to_x, to_y)
    small_copy(0, to_sib).start()
    for s in range(n + 4):
        if s < 3:
            small_copy(s, hops[s]).wait()
            sm[s + 1] = sm[s] + smr[s]
            if s < 2:
                small_copy(s + 1, hops[s + 1]).start()
            else:
                @pl.when(leaf)
                def _():
                    small_copy(3, to_z).start()
        if s == 4:
            @pl.when(inner)
            def _():
                small_copy(3, to_z).wait_recv()
                sm[4] = sm[3] + smr[3]
                small_copy(4, to_peer).start()
        if s == 6:
            @pl.when(inner)
            def _():
                small_copy(4, to_peer).wait()
                sm[5] = sm[4] + smr[4]
                remote(sm.at[5], smr.at[3], sms.at[3], smrs.at[3], to_z).start()
                small_out[...] = sm[5]
        if s == 8:
            @pl.when(leaf)
            def _():
                small_copy(3, to_z).wait()
                small_out[...] = smr[3]

        if s < n:
            u = s
            for c in step1(u):
                c.wait_recv()
            for c in local(u):
                c.wait()
            add_into(g_ref.at[u, 1], g_ref.at[u, 1], r1.at[u, 1], 128)
            step2(u).start()
            if u + 4 < n:
                for c in step1(u + 4):
                    c.start()
            add_into(g_ref.at[u, 0], g_ref.at[u, 0], r1.at[u, 0], 128)
        u = s - 1
        if 0 <= u < n:
            step2(u).wait_recv()
            add_into(g_ref.at[u, 0], g_ref.at[u, 0], r2.at[u], 128)

            @pl.when(leaf)
            def _(u=u):
                to_inner(u).start()

        u = s - 2
        if 0 <= u < n:
            @pl.when(inner)
            def _(u=u):
                to_inner(u).wait_recv()
                add_into(g_ref.at[u, 0], g_ref.at[u, 0], zin.at[u], 128)
                across(u).start()

        u = s - 3
        if 0 <= u < n:
            @pl.when(inner)
            def _(u=u):
                across(u).wait_recv()
                add_into(r2.at[u], g_ref.at[u, 0], zpeer.at[u], 128)
                to_leaf(u).start()
                emit(u, r2)

        u = s - 4
        if 0 <= u < n:
            @pl.when(leaf)
            def _(u=u):
                to_leaf(u).wait_recv()
                emit(u, zin)

    for u in range(n):
        for c in step1(u):
            c.wait_send()
        step2(u).wait_send()
        to_inner(u).wait_send()

    @pl.when(inner)
    def _():
        for u in range(n):
            across(u).wait_send()
        remote(sm.at[5], smr.at[3], sms.at[3], smrs.at[3], to_z).wait_send()


def reduce_units(grads, small):
    units = [(i, u) for i, g in enumerate(grads) for u in range(g.shape[0])]
    n = len(units)
    unit = grads[0].shape[2:]
    dma = pltpu.SemaphoreType.DMA
    return pl.pallas_call(
        functools.partial(reduce_kernel, units, len(grads)),
        out_shape=[
            jax.ShapeDtypeStruct((n,) + unit, F32),
            jax.ShapeDtypeStruct(small.shape, F32),
        ],
        in_specs=[HBM_SPEC] * len(grads) + [VMEM_SPEC],
        out_specs=[VMEM_SPEC] * 2,
        scratch_shapes=[
            pltpu.VMEM((n, 2) + unit, BF16),
            pltpu.VMEM((n, 2) + unit, BF16),
            pltpu.VMEM((n,) + unit, BF16),
            pltpu.VMEM((n,) + unit, BF16),
            pltpu.VMEM((n,) + unit, BF16),
            pltpu.VMEM((6,) + small.shape, F32),
            pltpu.VMEM((5,) + small.shape, F32),
            dma((n, 2)), dma((n, 2)), dma((n, 2)), dma((n,)), dma((n,)),
            dma((n,)), dma((n,)), dma((n,)), dma((n,)), dma((6,)), dma((6,)),
        ],
        compiler_params=params(collective_id=1, has_side_effects=True),
        name="reduce_gradients",
    )(*grads, small)


def per_device(on_boxes, tokens, out_grad, actions, segments, frame_mask, embed,
               ln1_gain, ln1_shift, spatial_qkv, spatial_out,
               ln2_gain, ln2_shift, temporal_qkv, temporal_out,
               ln3_gain, ln3_shift, ffn_in, ffn_in_bias, ffn_out, ffn_out_bias):
    frames_dev, tile_tokens, width = tokens.shape
    n_frame = lax.axis_size("frame")
    n_tile = lax.axis_size("tile")
    f = lax.axis_index("frame")
    t = lax.axis_index("tile")
    frames = frames_dev * n_frame
    place = tile_tokens // n_frame
    rows = frames_dev * tile_tokens
    row = lambda v: v[None, :]

    mats = (spatial_qkv, spatial_out, temporal_qkv, temporal_out, ffn_in, ffn_out)

    grad4 = out_grad.reshape(frames_dev, n_frame, place, width)
    if on_boxes:
        w_qs, w_os, w_qt, w_ot, w_in, w_out = gather_weights(mats)
        base1 = swap_blocks(tokens, tokens.shape, ("tile",),
                            lambda f, t: t, lambda f, t: t, 2, "tokens_to_frames")
        g = swap_blocks(grad4, (n_frame, frames_dev, place, width), ("frame",),
                        lambda f, t: (slice(None), f), lambda f, t: f, 3, "grad_to_places")
    else:
        w_qs, w_os, w_qt, w_ot, w_in, w_out = (lax.all_gather(m, "frame", axis=0, tiled=True) for m in mats)
        base1 = lax.all_to_all(tokens, "tile", 0, 0, tiled=True)
        g = lax.all_to_all(grad4.transpose(1, 0, 2, 3), "frame", 0, 0, tiled=True)
    base1 = base1.reshape(rows, width)
    g = g.reshape(rows, width)

    action = lax.dynamic_index_in_dim(actions, t, keepdims=False)
    added = lax.dynamic_slice_in_dim(embed, action, 1, 0)

    unit1, qkv1, mixed1, after1 = attn_fwd(
        base1, added, row(ln1_gain), row(ln1_shift), w_qs, w_os, None, BF16, "spatial_forward")

    blocks = n_frame * n_tile

    def turn(x, forward, cid, name):
        x = x.reshape(blocks, rows // blocks, width)
        if on_boxes:
            by_place = lambda f, t: 8 * t + f
            by_frame = lambda f, t: 4 * f + t
            a, b = (by_place, by_frame) if forward else (by_frame, by_place)
            y = swap_blocks(x, x.shape, ("frame", "tile"), a, b, cid, name)
        else:
            if forward:
                y = x.reshape(n_tile, n_frame, -1, width).transpose(1, 0, 2, 3)
                y = lax.all_to_all(y.reshape(x.shape), ("frame", "tile"), 0, 0, tiled=True)
            else:
                y = lax.all_to_all(x, ("frame", "tile"), 0, 0, tiled=True)
                y = y.reshape(n_frame, n_tile, -1, width).transpose(1, 0, 2, 3)
        return y.reshape(rows, width)

    base2 = turn(after1, True, 4, "frames_to_places")

    number = jnp.arange(rows, dtype=jnp.int32)
    of_frame, of_place = number // place, number % place
    seg_row = jnp.repeat(segments, place)
    open_row = jnp.repeat(frame_mask, place)
    allowed = (
        (seg_row[:, None] == seg_row[None, :])
        & (of_place[:, None] == of_place[None, :])
        & (of_frame[None, :] <= of_frame[:, None])
        & ((open_row[None, :] == 1) | (of_frame[None, :] == of_frame[:, None]))
    )
    bias = jnp.where(allowed, 0.0, -1e30).astype(F32)
    nothing = jnp.zeros((1, width), F32)
    unit2, qkv2, mixed2, after2 = attn_fwd(
        base2, nothing, row(ln2_gain), row(ln2_shift), w_qt, w_ot, bias, F32, "temporal_forward")
    unit3, pre, act, result = ffn_fwd(
        after2, row(ln3_gain), row(ln3_shift), w_in, row(ffn_in_bias), w_out, row(ffn_out_bias))
    d_pre, d_after2, dg3, ds3, d_bin, d_bout = ffn_bwd(g, pre, after2, row(ln3_gain), w_in, w_out)
    low2, d_qkv2, d_after1, dg2, ds2 = attn_bwd(
        base2, nothing, row(ln2_gain), w_qt, w_ot, d_after2, qkv2, bias, BF16, "temporal_backward")
    d_out1 = turn(d_after1, False, 5, "places_to_frames")
    low1, d_qkv1, d_start, dg1, ds1 = attn_bwd(
        base1, added, row(ln1_gain), w_qs, w_os, d_out1, qkv1, None, F32, "spatial_backward")

    tokens_grad = d_start.astype(BF16).reshape(n_tile, tile_tokens, width)
    result = result.reshape(n_frame, frames_dev, place, width)
    if on_boxes:
        tokens_grad = swap_blocks(tokens_grad, tokens.shape, ("tile",),
                                  lambda f, t: t, lambda f, t: t, 6, "tokens_grad_to_tiles")
        result = swap_blocks(result, grad4.shape, ("frame",),
                             lambda f, t: f, lambda f, t: (slice(None), f), 7, "result_to_tiles")
    else:
        tokens_grad = lax.all_to_all(tokens_grad, "tile", 0, 0, tiled=True)
        result = lax.all_to_all(result, "frame", 0, 0, tiled=True).transpose(1, 0, 2, 3)
    result = result.reshape(tokens.shape)

    one_hot = (action == jnp.arange(embed.shape[0], dtype=jnp.int32)).astype(F32)
    d_embed = one_hot[:, None] * jnp.sum(d_start, 0, keepdims=True)

    pairs = (
        (unit1, d_qkv1, "spatial_qkv_grad"),
        (mixed1, low1, "spatial_out_grad"),
        (unit2, d_qkv2, "temporal_qkv_grad"),
        (mixed2, low2, "temporal_out_grad"),
        (unit3, d_pre, "ffn_in_grad"),
        (act, g, "ffn_out_grad"),
    )
    if on_boxes:
        small = jnp.concatenate(
            [d_embed, dg1, ds1, dg2, ds2, dg3, ds3, d_bout, d_bin.reshape(-1, width)], 0)
        small = jnp.pad(small, ((0, -small.shape[0] % 8), (0, 0)))
        core = lax.rem(f, 2)
        grads = [wgrad_units(a, b, a.shape[1] // 8, core, name) for a, b, name in pairs]
        order = (5, 4, 3, 2, 1, 0)
        out, small = reduce_units([grads[i] for i in order], small)
        summed = [None] * 6
        first = 0
        for i in order:
            n_row = pairs[i][0].shape[1] // 8 // 128
            n_col = pairs[i][1].shape[1] // 1024
            part = out[first : first + n_row * n_col].reshape(n_row, n_col, 128, 1024)
            summed[i] = part.transpose(0, 2, 1, 3).reshape(n_row * 128, n_col * 1024)
            first += n_row * n_col
        n_act = embed.shape[0]
        d_embed, vecs = small[:n_act], small[n_act:]
        dg1, ds1, dg2, ds2, dg3, ds3, d_bout = (vecs[i] for i in range(7))
        d_bin = vecs[7 : 7 + d_bin.shape[1] // width].reshape(-1)
    else:
        summed = []
        for a, b, _ in pairs:
            part = lax.dot_general(a, b, (((0,), (0,)), ((), ())), preferred_element_type=F32)
            part = lax.psum_scatter(part, "frame", scatter_dimension=0, tiled=True)
            summed.append(lax.psum(part.astype(BF16), "tile").astype(F32))
        d_embed, dg1, ds1, dg2, ds2, dg3, ds3, d_bin, d_bout = lax.psum(
            (d_embed, dg1[0], ds1[0], dg2[0], ds2[0], dg3[0], ds3[0], d_bin[0], d_bout[0]), ("frame", "tile"))

    return (result, tokens_grad, d_embed, dg1, ds1, summed[0], summed[1], dg2, ds2, summed[2], summed[3],
            dg3, ds3, summed[4], d_bin, summed[5], d_bout)


def solution(mesh):
    shard = P("frame", "tile", None)
    mat = P("frame", None)
    rep = P()
    in_specs = (shard, shard, P("frame"), rep, rep, rep, rep, rep, mat, mat, rep, rep, mat, mat,
                rep, rep, mat, rep, mat, rep)
    out_specs = (shard, shard, rep, rep, rep, mat, mat, rep, rep, mat, mat, rep, rep, mat, rep, mat, rep)
    on_boxes = mesh.shape["frame"] == 8 and mesh.shape["tile"] == 4
    return jax.shard_map(
        functools.partial(per_device, on_boxes),
        mesh=mesh, in_specs=in_specs, out_specs=out_specs, check_vma=False)
```

```python
import functools

import jax
import jax.numpy as jnp
from jax import lax
from jax.experimental import pallas as pl
from jax.experimental.pallas import tpu as pltpu
from jax.sharding import PartitionSpec as P

HD = 64
LANES = 128
EPS = 1e-5
MESH = pl.DeviceIdType.MESH
F32 = jnp.float32
BF16 = jnp.bfloat16
VMEM_SPEC = pl.BlockSpec(memory_space=pltpu.VMEM)
HBM_SPEC = pl.BlockSpec(memory_space=pltpu.HBM)


def params(**kw):
    return pltpu.CompilerParams(vmem_limit_bytes=58 * 1024 * 1024, **kw)


def at(j, size):
    return pl.ds(pl.multiple_of(j * size, size), size)


def each(n, fn):
    def step(i, carry):
        fn(i)
        return carry

    lax.fori_loop(0, n, step, 0)


def dot(a, b):
    return jnp.dot(a, b, preferred_element_type=F32)


def dot_nt(a, b):
    return lax.dot_general(a, b, (((1,), (1,)), ((), ())), preferred_element_type=F32)


def dot_tn(a, b):
    return lax.dot_general(a, b, (((0,), (0,)), ((), ())), preferred_element_type=F32)


def normed(h):
    cen = h - jnp.mean(h, -1, keepdims=True)
    inv = lax.rsqrt(jnp.mean(cen * cen, -1, keepdims=True) + EPS)
    return cen * inv, inv


ROWS = 32


def norm_rows(load, gain_ref, shift_ref, unit_ref):
    def step(i):
        rows = at(i, ROWS)
        xhat, _ = normed(load(rows))
        unit_ref[rows, :] = (xhat * gain_ref[...] + shift_ref[...]).astype(BF16)

    each(unit_ref.shape[0] // ROWS, step)


def fold(x):
    return jnp.sum(x.reshape(x.shape[0] // 8, 8, x.shape[1]), 0)


def norm_back(load, du_ref, gain_ref, dgain_ref, dshift_ref, acc_ref, store):
    acc_ref[...] = jnp.zeros_like(acc_ref)

    def step(i):
        rows = at(i, ROWS)
        xhat, inv = normed(load(rows))
        du = du_ref[rows, :]
        acc_ref[0] += fold(du * xhat)
        acc_ref[1] += fold(du)
        dx = du * gain_ref[...]
        dh = inv * (
            dx - jnp.mean(dx, -1, keepdims=True) - xhat * jnp.mean(dx * xhat, -1, keepdims=True)
        )
        store(rows, dh)

    each(du_ref.shape[0] // ROWS, step)
    dgain_ref[...] = jnp.sum(acc_ref[0], 0, keepdims=True)
    dshift_ref[...] = jnp.sum(acc_ref[1], 0, keepdims=True)


def head_masks():
    lane = lax.broadcasted_iota(jnp.int32, (1, LANES), 1)
    low = jnp.where(lane < HD, 1.0, 0.0)
    return low.astype(BF16), (1.0 - low).astype(BF16)


def head_probs(qm, k, bias_ref):
    s = dot_nt(qm, k) * (HD**-0.5)
    if bias_ref is not None:
        s = s + bias_ref[...]
    e = jnp.exp(s - jnp.max(s, -1, keepdims=True))
    return e * (1.0 / jnp.sum(e, -1, keepdims=True))


def attention(qkv_ref, bias_ref, mixed_ref):
    width = mixed_ref.shape[1]
    per = width // LANES
    masks = head_masks()

    def pair(p):
        q, k, v = (qkv_ref[:, at(p + i * per, LANES)] for i in range(3))
        out = 0.0
        for m in masks:
            out = out + dot(head_probs(q * m, k, bias_ref).astype(BF16), v * m)
        mixed_ref[:, at(p, LANES)] = out.astype(BF16)

    each(per, pair)


def attention_back(qkv_ref, bias_ref, dmix_ref, dqkv_ref):
    width = dmix_ref.shape[1]
    per = width // LANES
    masks = head_masks()
    scale = HD**-0.5

    def pair(p):
        q, k, v = (qkv_ref[:, at(p + i * per, LANES)] for i in range(3))
        dm = dmix_ref[:, at(p, LANES)]
        dq = dk = dv = 0.0
        for m in masks:
            qm = q * m
            dmm = dm * m
            probs = head_probs(qm, k, bias_ref)
            dp = dot_nt(dmm, v)
            ds = probs * (dp - jnp.sum(probs * dp, -1, keepdims=True))
            ds = ds.astype(BF16)
            dq = dq + dot(ds, k * m)
            dk = dk + dot_tn(ds, qm)
            dv = dv + dot_tn(probs.astype(BF16), dmm)
        dqkv_ref[:, at(p, LANES)] = (dq * scale).astype(BF16)
        dqkv_ref[:, at(p + per, LANES)] = (dk * scale).astype(BF16)
        dqkv_ref[:, at(p + 2 * per, LANES)] = dv.astype(BF16)

    each(per, pair)


def matmul(x_ref, w_ref, block, store):
    def step(j):
        cols = at(j, block)
        store(cols, dot(x_ref[...], w_ref[:, cols]))

    each(w_ref.shape[1] // block, step)


def matmul_nt(x_ref, w_ref, block, store):
    def step(j):
        rows = at(j, block)
        store(rows, dot_nt(x_ref[...], w_ref[rows, :]))

    each(w_ref.shape[0] // block, step)


def attn_fwd_kernel(masked, base_ref, added_ref, gain_ref, shift_ref, wqkv_ref, wo_ref, *rest):
    if masked:
        bias_ref, unit_ref, qkv_ref, mixed_ref, after_ref = rest
    else:
        bias_ref = None
        unit_ref, qkv_ref, mixed_ref, after_ref = rest

    def load(rows):
        return base_ref[rows, :].astype(F32) + added_ref[...]

    norm_rows(load, gain_ref, shift_ref, unit_ref)

    def put_qkv(cols, y):
        qkv_ref[:, cols] = y.astype(BF16)

    matmul(unit_ref, wqkv_ref, 512, put_qkv)
    attention(qkv_ref, bias_ref, mixed_ref)

    def put_after(cols, y):
        y = y + base_ref[:, cols].astype(F32) + added_ref[:, cols]
        after_ref[:, cols] = y.astype(after_ref.dtype)

    matmul(mixed_ref, wo_ref, 512, put_after)


def attn_fwd(base, added, gain, shift, wqkv, wo, bias, out_type, name):
    rows, width = base.shape
    ins = [base, added, gain, shift, wqkv, wo] + ([bias] if bias is not None else [])
    shapes = [(width, BF16), (3 * width, BF16), (width, BF16), (width, out_type)]
    return pl.pallas_call(
        functools.partial(attn_fwd_kernel, bias is not None),
        out_shape=[jax.ShapeDtypeStruct((rows, w), d) for w, d in shapes],
        in_specs=[VMEM_SPEC] * len(ins),
        out_specs=[VMEM_SPEC] * 4,
        compiler_params=params(),
        name=name,
    )(*ins)


def attn_bwd_kernel(masked, base_ref, added_ref, gain_ref, wqkv_ref, wo_ref, dout_ref, qkv_ref, *rest):
    if masked:
        bias_ref, *rest = rest
    else:
        bias_ref = None
    dlow_ref, dqkv_ref, dbase_ref, dgain_ref, dshift_ref, dmix_ref, du_ref, acc_ref = rest

    def cast(i):
        rows = at(i, ROWS)
        dlow_ref[rows, :] = dout_ref[rows, :].astype(BF16)

    each(dlow_ref.shape[0] // ROWS, cast)

    def put_mix(rows, y):
        dmix_ref[:, rows] = y.astype(BF16)

    matmul_nt(dlow_ref, wo_ref, 512, put_mix)
    attention_back(qkv_ref, bias_ref, dmix_ref, dqkv_ref)

    def put_du(rows, y):
        du_ref[:, rows] = y

    matmul_nt(dqkv_ref, wqkv_ref, 256, put_du)

    def load(rows):
        return base_ref[rows, :].astype(F32) + added_ref[...]

    def store(rows, dh):
        dbase_ref[rows, :] = (dout_ref[rows, :].astype(F32) + dh).astype(dbase_ref.dtype)

    norm_back(load, du_ref, gain_ref, dgain_ref, dshift_ref, acc_ref, store)


def attn_bwd(base, added, gain, wqkv, wo, dout, qkv, bias, out_type, name):
    rows, width = base.shape
    ins = [base, added, gain, wqkv, wo, dout, qkv] + ([bias] if bias is not None else [])
    outs = [
        jax.ShapeDtypeStruct((rows, width), BF16),
        jax.ShapeDtypeStruct((rows, 3 * width), BF16),
        jax.ShapeDtypeStruct((rows, width), out_type),
        jax.ShapeDtypeStruct((1, width), F32),
        jax.ShapeDtypeStruct((1, width), F32),
    ]
    return pl.pallas_call(
        functools.partial(attn_bwd_kernel, bias is not None),
        out_shape=outs,
        in_specs=[VMEM_SPEC] * len(ins),
        out_specs=[VMEM_SPEC] * len(outs),
        scratch_shapes=[
            pltpu.VMEM((rows, width), BF16),
            pltpu.VMEM((rows, width), F32),
            pltpu.VMEM((2, 8, width), F32),
        ],
        compiler_params=params(),
        name=name,
    )(*ins)


GELU_A = 0.7978845608
GELU_B = 0.044715


def ffn_bwd_kernel(g_ref, slope_ref, after_ref, gain_ref, win_ref, wout_ref,
                   dslope_ref, dafter_ref, dgain_ref, dshift_ref, dbin_ref, dbout_ref, du_ref, acc_ref):
    def put_dpre(rows, y):
        d = (y * slope_ref[:, rows].astype(F32)).astype(BF16)
        dslope_ref[:, rows] = d
        dbin_ref[:, rows] = jnp.sum(d.astype(F32), 0, keepdims=True)

    matmul_nt(g_ref, wout_ref, 512, put_dpre)

    def put_du(rows, y):
        du_ref[:, rows] = y

    matmul_nt(dslope_ref, win_ref, 256, put_du)
    dbout_ref[...] = jnp.zeros_like(dbout_ref)

    def store(rows, dh):
        g = g_ref[rows, :].astype(F32)
        dafter_ref[rows, :] = g + dh
        dbout_ref[...] += jnp.sum(g, 0, keepdims=True)

    norm_back(lambda rows: after_ref[rows, :], du_ref, gain_ref, dgain_ref, dshift_ref, acc_ref, store)


def ffn_bwd(g, slope, after, gain, win, wout):
    rows, width = after.shape
    ff = win.shape[1]
    row = lambda n: jax.ShapeDtypeStruct((1, n), F32)
    return pl.pallas_call(
        ffn_bwd_kernel,
        out_shape=[
            jax.ShapeDtypeStruct((rows, ff), BF16),
            jax.ShapeDtypeStruct((rows, width), F32),
            row(width), row(width), row(ff), row(width),
        ],
        in_specs=[VMEM_SPEC] * 6,
        out_specs=[VMEM_SPEC] * 6,
        scratch_shapes=[pltpu.VMEM((rows, width), F32), pltpu.VMEM((2, 8, width), F32)],
        compiler_params=params(),
        name="ffn_backward",
    )(g, slope, after, gain, win, wout)


def wgrad_kernel(shard, left_ref, left2_ref, right_ref, right2_ref, out_ref, lt_ref):
    tok = left_ref.shape[0]
    lt_ref[:, :tok] = left_ref[...].T
    lt_ref[:, tok:] = left2_ref[...].T
    col_blocks = right_ref.shape[1] // 1024
    for rb in range(shard // 128):
        for cb in range(col_blocks):
            def step(j, rb=rb, cb=cb):
                cols = pl.ds(pl.multiple_of(cb * 1024 + j * 512, 512), 512)
                a = jnp.concatenate(
                    [lt_ref[q * shard + rb * 128 : q * shard + (rb + 1) * 128, :] for q in range(4)], 0
                )
                y = dot(a[:, :tok], right_ref[:, cols]) + dot(a[:, tok:], right2_ref[:, cols])
                y = y.astype(BF16)
                for q in range(4):
                    out_ref[rb * col_blocks + cb, q, :, at(j, 512)] = y[q * 128 : (q + 1) * 128]

            each(2, step)


def wgrad_units(left, right, shard, core, name):
    tok = left.shape[0]
    parts = left.reshape(tok, 4, 2, shard)
    mine = lax.dynamic_index_in_dim(parts, core, 2, False).reshape(tok, 4 * shard)
    other = lax.dynamic_index_in_dim(parts, 1 - core, 2, False).reshape(tok, 4 * shard)
    swap = [(i, i ^ 1) for i in range(8)]
    other = lax.ppermute(other, "frame", swap)
    right2 = lax.ppermute(right, "frame", swap)
    units = (shard // 128) * (right.shape[1] // 1024)
    return pl.pallas_call(
        functools.partial(wgrad_kernel, shard),
        out_shape=jax.ShapeDtypeStruct((units, 4, 128, 1024), BF16),
        in_specs=[VMEM_SPEC] * 4,
        out_specs=VMEM_SPEC,
        scratch_shapes=[pltpu.VMEM((4 * shard, 2 * tok), BF16)],
        compiler_params=params(),
        name=name,
    )(mine, other, right, right2)


def wgrad(core, shard, left, left_x, right, right_x, out, lt):
    tok = left.shape[0]
    col_blocks = right.shape[1] // TILE
    for rb in range(shard // 128):
        for q in range(4):
            cols = pl.ds(pl.multiple_of((2 * q + core) * shard + rb * 128, 128), 128)
            lt[q * 128 : (q + 1) * 128, :tok] = left[:, cols].T
            cols = pl.ds(q * shard + rb * 128, 128)
            lt[q * 128 : (q + 1) * 128, tok:] = left_x[:, cols].T

        def step(j, rb=rb):
            cols = at(j, 512)
            y = dot(lt[:, :tok], right[:, cols]) + dot(lt[:, tok:], right_x[:, cols])
            y = y.astype(BF16)
            unit = rb * col_blocks + j // 2
            half = pl.ds(pl.multiple_of(lax.rem(j, 2) * 512, 512), 512)
            for q in range(4):
                out[unit, q, :, half] = y[q * 128 : (q + 1) * 128]

        each(2 * col_blocks, step)


def xor(a, b):
    bit = lax.rem(a // b, 2)
    return a + b - 2 * b * bit


def greet(partners):
    barrier = pltpu.get_barrier_semaphore()
    for p in partners:
        pl.semaphore_signal(barrier, inc=1, device_id=p, device_id_type=MESH)
    pl.semaphore_wait(barrier, len(partners))


def remote(src, dst, ssem, rsem, dev):
    return pltpu.make_async_remote_copy(
        src_ref=src, dst_ref=dst, send_sem=ssem, recv_sem=rsem, device_id=dev, device_id_type=MESH
    )


def xor_any(a, bits):
    for b in (1, 2, 4, 8, 16):
        if bits & b:
            a = xor(a, b)
    return a


def swap_kernel(axes, src_of, dst_of, src_ref, dst_ref, ssem, rsem, lsem):
    f = lax.axis_index("frame")
    t = lax.axis_index("tile")
    nf = 8 if "frame" in axes else 1
    nt = 4 if "tile" in axes else 1
    todo = [(a, b) for a in range(nf) for b in range(nt) if (a, b) != (0, 0)]
    devs = [(xor_any(f, a), xor_any(t, b)) for a, b in todo]
    greet(devs)
    own = pltpu.make_async_copy(src_ref.at[src_of(f, t)], dst_ref.at[dst_of(f, t)], lsem)
    own.start()
    for i, d in enumerate(devs):
        remote(src_ref.at[src_of(*d)], dst_ref.at[dst_of(f, t)], ssem.at[i], rsem.at[i], d).start()
    own.wait()
    for i, d in enumerate(devs):
        remote(src_ref.at[src_of(*d)], dst_ref.at[dst_of(*d)], ssem.at[i], rsem.at[i], d).wait()


def swap_blocks(x, shape, axes, src_of, dst_of, cid, name):
    n = (8 if "frame" in axes else 1) * (4 if "tile" in axes else 1)
    return pl.pallas_call(
        functools.partial(swap_kernel, axes, src_of, dst_of),
        out_shape=jax.ShapeDtypeStruct(shape, x.dtype),
        in_specs=[HBM_SPEC],
        out_specs=HBM_SPEC,
        scratch_shapes=[
            pltpu.SemaphoreType.DMA((n - 1,)),
            pltpu.SemaphoreType.DMA((n - 1,)),
            pltpu.SemaphoreType.DMA,
        ],
        compiler_params=params(collective_id=cid, has_side_effects=True),
        name=name,
    )(x)


TILE = 1024
SLOTS = 6
AHEAD = 3


def gather_chunks(shapes):
    out = []
    for i, (rows, cols) in enumerate(shapes):
        step = rows
        while step * cols > 128 * 1024 and step % 32 == 0:
            step //= 2
        out += [(i, r, step) for r in range(0, rows, step)]
    return out


def weight_tiles(shapes):
    return [
        (i, r, c)
        for i, (rows, cols) in enumerate(shapes)
        for r in range(0, rows, TILE)
        for c in range(0, cols, TILE)
    ]


def forward_kernel(chunks, tiles, *refs):
    shards = refs[:6]
    (tokens, grad4, added, g1, s1, g2, s2, g3, s3, b_in, b_out, bias) = refs[6:18]
    full = refs[18:24]
    (base1, unit1, qkv1, mixed1, base2, unit2, qkv2, mixed2, after2, unit3, slope, act, g2d, gout, result) = refs[24:39]
    (wt, base_in, out1, in2, g_in, y_ref, res_out, act_x, g_x, lt, ssem, rsem, bsem, tsem, z3s, z3r, z3l,
     f7s, f7r, f7l, turn_s, turn_r, turn_l, x_s, x_r, o7s, o7r, o7l) = refs[39:]
    f = lax.axis_index("frame")
    t = lax.axis_index("tile")
    core = lax.rem(f, 2)
    odd = lax.rem(t, 2)
    fx, fy = xor(f, 2), xor(f, 4)
    first = fx + (fy - fx) * odd
    second = fy + (fx - fy) * odd
    diag = xor_any(f, 6)
    sib = xor(f, 1)
    to_sib, to_first, to_second, to_z = (sib, t), (first, t), (second, t), (f, xor(t, 1))
    greet([(xor_any(f, a), xor_any(t, b)) for a in range(8) for b in range(4) if a or b])

    def piece(k, owner):
        a, r, n = chunks[k]
        return full[a].at[pl.ds(pl.multiple_of(owner * shards[a].shape[0] + r, 16), n)]

    def own(k):
        a, r, n = chunks[k]
        return shards[a].at[pl.ds(r, n)]

    def copy(k, kind):
        dev = (to_first, to_second, to_z, to_sib, to_sib, to_sib, to_sib)[kind]
        owner = (f, first, first, f, first, diag, second)[kind]
        src = own(k) if kind in (0, 3) else piece(k, owner)
        return remote(src, piece(k, owner), ssem.at[k, kind], rsem.at[k, kind], dev)

    def arrived(k, kind):
        owner = (first, diag, second, sib, xor(first, 1), xor(diag, 1), xor(second, 1))[kind]
        dst = piece(k, owner)
        remote(dst, dst, ssem.at[k, kind], rsem.at[k, kind], to_sib).wait_recv()

    n = len(chunks)

    def hop(k):
        copy(k, 3).start()
        arrived(k, 0)
        if k + AHEAD < n:
            copy(k + AHEAD, 0).start()
        for kind in (1, 2, 4):
            copy(k, kind).start()

    def relay(k):
        for kind in (1, 2):
            arrived(k, kind)
            copy(k, kind + 4).start()

    progress = [0, 0]

    def advance(hops):
        while progress[0] < min(hops, n):
            hop(progress[0])
            progress[0] += 1
            if progress[0] >= 2:
                relay(progress[1])
                progress[1] += 1
        if hops > n and progress[1] < n:
            relay(progress[1])
            progress[1] += 1

    bounce = []
    for a, shard in enumerate(shards):
        for r in range(0, shard.shape[0], 128):
            for c in range(0, shard.shape[1], TILE):
                i = len(bounce)
                bounce.append((a, r, c, wt.at[4 + i // 8, pl.ds(i % 8 * 128, 128)]))

    def bounce_in(i):
        a, r, c, via = bounce[i]
        return pltpu.make_async_copy(shards[a].at[pl.ds(r, 128), pl.ds(c, TILE)], via, bsem.at[i])

    def bounce_out(i):
        a, r, c, via = bounce[i]
        row = pl.multiple_of(f * shards[a].shape[0] + r, 128)
        return pltpu.make_async_copy(via, full[a].at[pl.ds(row, 128), pl.ds(c, TILE)], bsem.at[i])

    def tile_load(i):
        a, r, c = tiles[i]
        src = full[a].at[pl.ds(r, TILE), pl.ds(c, TILE)]
        return pltpu.make_async_copy(src, wt.at[i % SLOTS], tsem.at[i])

    def tile(i):
        return wt.at[i % SLOTS]

    def tiles_of(a):
        return [i for i, x in enumerate(tiles) if x[0] == a]

    def complete(a):
        ks = [k for k in range(n) if chunks[k][0] == a]
        advance(ks[-1] + 2)
        for k in ks:
            for kind in (3, 4, 5, 6):
                arrived(k, kind)

    def load(ids):
        for i in ids:
            tile_load(i).start()

    def ready(ids):
        for i in ids:
            tile_load(i).wait()

    def token_copy(i):
        d = xor_any(t, i)
        return remote(tokens.at[d], base_in.at[pl.ds(pl.multiple_of(t * 64, 64), 64)], z3s.at[i - 1], z3r.at[i - 1], (f, d))

    def token_arrived(i):
        d = xor_any(t, i)
        dst = base_in.at[pl.ds(pl.multiple_of(d * 64, 64), 64)]
        remote(tokens.at[d], dst, z3s.at[i - 1], z3r.at[i - 1], (f, d)).wait()

    own_tokens = pltpu.make_async_copy(tokens.at[t], base_in.at[pl.ds(pl.multiple_of(t * 64, 64), 64)], z3l)
    own_tokens.start()
    for i in (1, 2, 3):
        token_copy(i).start()
    for k in range(AHEAD):
        copy(k, 0).start()
    for i in range(len(bounce)):
        bounce_in(i).start()

    def grad_copy(i, dst_slot):
        d = xor_any(f, i)
        return remote(grad4.at[:, d], g_in.at[pl.ds(4 * dst_slot, 4)], f7s.at[i - 1], f7r.at[i - 1], (d, t))

    own_grad = pltpu.make_async_copy(grad4.at[:, f], g_in.at[pl.ds(4 * f, 4)], f7l)

    advance(1)
    for i in range(len(bounce)):
        bounce_in(i).wait()
        bounce_out(i).start()
    own_tokens.wait()
    for i in (1, 2, 3):
        token_arrived(i)

    def plain(i):
        rows = at(i, ROWS)
        base1[rows, :] = base_in[rows, :]

    each(base1.shape[0] // ROWS, plain)
    norm_rows(lambda rows: base1[rows, :].astype(F32) + added[...], g1, s1, unit1)
    own_grad.start()
    for i in range(1, 8):
        grad_copy(i, f).start()
    for i in range(len(bounce)):
        bounce_out(i).wait()

    def project(unit, ids, out_ref):
        for j, i in enumerate(ids):
            def put(cols, y, j=j):
                start = pl.multiple_of(cols.start + j * TILE, 512)
                out_ref[:, pl.ds(start, 512)] = y.astype(BF16)

            matmul(unit, tile(i), 512, put)

    complete(0)
    load(tiles_of(0))
    ready(tiles_of(0))
    project(unit1, tiles_of(0), qkv1)
    complete(1)
    load(tiles_of(1))
    attention(qkv1, None, mixed1)
    ready(tiles_of(1))

    def put_after1(cols, y):
        y = y + base1[:, cols].astype(F32) + added[:, cols]
        y_ref[:, cols] = y

    matmul(mixed1, tile(tiles_of(1)[0]), 512, put_after1)

    def split(i):
        rows = at(i, ROWS)
        out1[pl.ds(4 * i, 4)] = y_ref[rows, :].reshape(4, 8, TILE).astype(BF16)

    each(y_ref.shape[0] // ROWS, split)

    slot = 4 * f + t
    others = [(a, b) for a in range(8) for b in range(4) if a or b]

    def turn_copy(i, d, dst_slot):
        return remote(out1.at[8 * d[1] + d[0]], in2.at[dst_slot], turn_s.at[i], turn_r.at[i], d)

    own_turn = pltpu.make_async_copy(out1.at[8 * t + f], in2.at[slot], turn_l)
    own_turn.start()
    for i, (a, b) in enumerate(others):
        turn_copy(i, (xor_any(f, a), xor_any(t, b)), slot).start()
    complete(2)
    load(tiles_of(2))
    complete(3)
    load(tiles_of(3))
    own_turn.wait()
    for i, (a, b) in enumerate(others):
        d = (xor_any(f, a), xor_any(t, b))
        turn_copy(i, d, 4 * d[0] + d[1]).wait()

    def join(i):
        base2[at(i, ROWS), :] = in2[pl.ds(4 * i, 4)].astype(F32).reshape(ROWS, TILE).astype(BF16)

    each(base2.shape[0] // ROWS, join)
    norm_rows(lambda rows: base2[rows, :].astype(F32), g2, s2, unit2)
    ready(tiles_of(2))
    project(unit2, tiles_of(2), qkv2)
    advance(12)
    attention(qkv2, bias, mixed2)
    advance(14)
    ready(tiles_of(3))

    def put_after2(cols, y):
        after2[:, cols] = y + base2[:, cols].astype(F32)

    matmul(mixed2, tile(tiles_of(3)[0]), 512, put_after2)
    norm_rows(lambda rows: after2[rows, :], g3, s3, unit3)
    complete(4)
    load(tiles_of(4))

    own_grad.wait()
    for i in range(1, 8):
        grad_copy(i, xor_any(f, i)).wait()

    def join_grad(i):
        g2d[at(i, ROWS), :] = g_in[pl.ds(4 * i, 4)].astype(F32).reshape(ROWS, TILE).astype(BF16)

    each(g2d.shape[0] // ROWS, join_grad)

    for j, i in enumerate(tiles_of(4)):
        tile_load(i).wait()

        def put_pre(cols, y, j=j):
            cols = pl.ds(pl.multiple_of(cols.start + j * TILE, 256), 256)
            v = y + b_in[:, cols]
            th = jnp.tanh(GELU_A * (v + GELU_B * v * v * v))
            act[:, cols] = (0.5 * v * (1.0 + th)).astype(BF16)
            rise = 0.5 * (1.0 + th) + 0.5 * v * (1.0 - th * th) * GELU_A * (1.0 + 3.0 * GELU_B * v * v)
            slope[:, cols] = rise.astype(BF16)

        matmul(unit3, tile(i), 256, put_pre)

    shard = shards[5].shape[0]
    swaps = [
        remote(act.at[:, pl.ds(pl.multiple_of((2 * q + 1 - core) * shard, shard), shard)],
               act_x.at[:, pl.ds(q * shard, shard)], x_s.at[q], x_r.at[q], to_sib)
        for q in range(4)
    ]
    swaps.append(remote(g2d, g_x, x_s.at[4], x_r.at[4], to_sib))
    for c in swaps:
        c.start()
    advance(16)
    for c in swaps:
        c.wait()
    wgrad(core, shard, act, act_x, g2d, g_x, gout, lt)
    complete(5)
    ids = tiles_of(5)
    load(ids)
    for j, i in enumerate(ids):
        tile_load(i).wait()

        def part(h, i=i, j=j):
            cols = at(h, 512)
            y = dot(act[:, j * TILE : (j + 1) * TILE], wt[i % SLOTS, :, cols])
            y_ref[:, cols] = y + (after2[:, cols] + b_out[:, cols] if j == 0 else y_ref[:, cols])

        each(2, part)

    def split_res(i):
        res_out[pl.ds(4 * i, 4)] = y_ref[at(i, ROWS), :].reshape(4, 8, TILE).astype(BF16)

    each(y_ref.shape[0] // ROWS, split_res)

    def res_copy(i, dst):
        d = xor_any(f, i)
        return remote(res_out.at[pl.ds(4 * d, 4)], result.at[:, dst], o7s.at[i - 1], o7r.at[i - 1], (d, t))

    own_res = pltpu.make_async_copy(res_out.at[pl.ds(4 * f, 4)], result.at[:, f], o7l)
    own_res.start()
    for i in range(1, 8):
        res_copy(i, f).start()
    for k in range(n):
        for kind in range(7):
            copy(k, kind).wait_send()
    own_res.wait()
    for i in range(1, 8):
        res_copy(i, xor_any(f, i)).wait()


def forward(mats, tokens, grad4, added, vecs, bias):
    width = tokens.shape[2]
    rows = tokens.shape[0] * tokens.shape[1]
    ff = mats[4].shape[1]
    fulls = [(8 * m.shape[0], m.shape[1]) for m in mats]
    chunks = gather_chunks([m.shape for m in mats])
    tiles = weight_tiles(fulls)
    n = len(chunks)
    dma = pltpu.SemaphoreType.DMA
    act_shapes = [
        (width, BF16), (width, BF16), (3 * width, BF16), (width, BF16),
        (width, BF16), (width, BF16), (3 * width, BF16), (width, BF16),
        (width, F32), (width, BF16), (ff, BF16), (ff, BF16), (width, BF16),
    ]
    units = mats[5].shape[0] // 128
    outs = [jax.ShapeDtypeStruct(s, BF16) for s in fulls]
    outs += [jax.ShapeDtypeStruct((rows, w), d) for w, d in act_shapes]
    outs += [jax.ShapeDtypeStruct((units, 4, 128, TILE), BF16), jax.ShapeDtypeStruct(grad4.shape, BF16)]
    blocks = (32, 8, width)
    return pl.pallas_call(
        functools.partial(forward_kernel, chunks, tiles),
        out_shape=outs,
        in_specs=[HBM_SPEC] * 8 + [VMEM_SPEC] * 10,
        out_specs=[HBM_SPEC] * 6 + [VMEM_SPEC] * 14 + [HBM_SPEC],
        scratch_shapes=[
            pltpu.VMEM((SLOTS, TILE, TILE), BF16),
            pltpu.VMEM((rows, width), BF16),
            pltpu.VMEM(blocks, BF16), pltpu.VMEM(blocks, BF16), pltpu.VMEM(blocks, BF16),
            pltpu.VMEM((rows, width), F32),
            pltpu.VMEM(blocks, BF16),
            pltpu.VMEM((rows, ff // 2), BF16), pltpu.VMEM((rows, width), BF16),
            pltpu.VMEM((512, 2 * rows), BF16),
            dma((n, 7)), dma((n, 7)), dma((16,)), dma((len(tiles),)),
            dma((3,)), dma((3,)), dma, dma((7,)), dma((7,)), dma,
            dma((31,)), dma((31,)), dma, dma((5,)), dma((5,)), dma((7,)), dma((7,)), dma,
        ],
        compiler_params=params(collective_id=0, has_side_effects=True),
        name="forward",
    )(*mats, tokens, grad4, added, *vecs, bias)


def add_into(dst, a, b, rows):
    def step(i):
        r = at(i, 16)
        dst[r, :] = (a[r, :].astype(F32) + b[r, :].astype(F32)).astype(dst.dtype)

    each(rows // 16, step)


def reduce_kernel(units, n_arr, *refs):
    grads = refs[:n_arr]
    small_ref = refs[n_arr]
    out_ref, small_out = refs[n_arr + 1 : n_arr + 3]
    (g_ref, r1, r2, zin, zpeer, sm, smr, lsem, s1s, s1r, s2s, s2r, zs, zr, zps, zpr, sms, smrs) = refs[n_arr + 3 :]
    f = lax.axis_index("frame")
    t = lax.axis_index("tile")
    q = f // 2
    leaf = (t == 0) | (t == 3)
    inner = jnp.logical_not(leaf)
    fx, fy, sib = xor(f, 2), xor(f, 4), xor(f, 1)
    qx, qy, qd = xor(q, 1), xor(q, 2), xor_any(q, 3)
    to_x, to_y, to_sib, to_z, to_peer = (fx, t), (fy, t), (sib, t), (f, xor(t, 1)), (f, 3 - t)
    greet([to_x, to_y, to_sib, to_z, to_peer])
    n = len(units)

    def hop(u):
        return (to_x, qx, to_y, qy) if u % 2 == 0 else (to_y, qy, to_x, qx)

    def src(u, piece):
        a, i = units[u]
        return grads[a].at[i, piece]

    def local(u):
        dev1, p1, dev2, p2 = hop(u)
        return (
            pltpu.make_async_copy(src(u, q), g_ref.at[u, 0], lsem.at[u, 0]),
            pltpu.make_async_copy(src(u, p2), g_ref.at[u, 1], lsem.at[u, 1]),
        )

    def step1(u):
        dev1, p1, dev2, p2 = hop(u)
        return (
            remote(src(u, p1), r1.at[u, 0], s1s.at[u, 0], s1r.at[u, 0], dev1),
            remote(src(u, qd), r1.at[u, 1], s1s.at[u, 1], s1r.at[u, 1], dev1),
        )

    def step2(u):
        return remote(g_ref.at[u, 1], r2.at[u], s2s.at[u], s2r.at[u], hop(u)[2])

    def to_inner(u):
        return remote(g_ref.at[u, 0], zin.at[u], zs.at[u], zr.at[u], to_z)

    def across(u):
        return remote(g_ref.at[u, 0], zpeer.at[u], zps.at[u], zpr.at[u], to_peer)

    def to_leaf(u):
        return remote(r2.at[u], zin.at[u], zs.at[u], zr.at[u], to_z)

    def emit(u, ref):
        def step(i):
            r = at(i, 16)
            out_ref[u, r, :] = ref[u, r, :].astype(F32)

        each(8, step)

    for u in range(n):
        for c in local(u):
            c.start()
    for u in range(min(4, n)):
        for c in step1(u):
            c.start()
    sm[0] = small_ref[...]

    def small_copy(i, dev):
        return remote(sm.at[i], smr.at[i], sms.at[i], smrs.at[i], dev)

    hops = (to_sib, to_x, to_y)
    small_copy(0, to_sib).start()
    for s in range(n + 4):
        if s < 3:
            small_copy(s, hops[s]).wait()
            sm[s + 1] = sm[s] + smr[s]
            if s < 2:
                small_copy(s + 1, hops[s + 1]).start()
            else:
                @pl.when(leaf)
                def _():
                    small_copy(3, to_z).start()
        if s == 4:
            @pl.when(inner)
            def _():
                small_copy(3, to_z).wait_recv()
                sm[4] = sm[3] + smr[3]
                small_copy(4, to_peer).start()
        if s == 6:
            @pl.when(inner)
            def _():
                small_copy(4, to_peer).wait()
                sm[5] = sm[4] + smr[4]
                remote(sm.at[5], smr.at[3], sms.at[3], smrs.at[3], to_z).start()
                small_out[...] = sm[5]
        if s == 8:
            @pl.when(leaf)
            def _():
                small_copy(3, to_z).wait()
                small_out[...] = smr[3]

        if s < n:
            u = s
            for c in step1(u):
                c.wait_recv()
            for c in local(u):
                c.wait()
            add_into(g_ref.at[u, 1], g_ref.at[u, 1], r1.at[u, 1], 128)
            step2(u).start()
            if u + 4 < n:
                for c in step1(u + 4):
                    c.start()
            add_into(g_ref.at[u, 0], g_ref.at[u, 0], r1.at[u, 0], 128)
        u = s - 1
        if 0 <= u < n:
            step2(u).wait_recv()
            add_into(g_ref.at[u, 0], g_ref.at[u, 0], r2.at[u], 128)

            @pl.when(leaf)
            def _(u=u):
                to_inner(u).start()

        u = s - 2
        if 0 <= u < n:
            @pl.when(inner)
            def _(u=u):
                to_inner(u).wait_recv()
                add_into(g_ref.at[u, 0], g_ref.at[u, 0], zin.at[u], 128)
                across(u).start()

        u = s - 3
        if 0 <= u < n:
            @pl.when(inner)
            def _(u=u):
                across(u).wait_recv()
                add_into(r2.at[u], g_ref.at[u, 0], zpeer.at[u], 128)
                to_leaf(u).start()
                emit(u, r2)

        u = s - 4
        if 0 <= u < n:
            @pl.when(leaf)
            def _(u=u):
                to_leaf(u).wait_recv()
                emit(u, zin)

    for u in range(n):
        for c in step1(u):
            c.wait_send()
        step2(u).wait_send()
        to_inner(u).wait_send()

    @pl.when(inner)
    def _():
        for u in range(n):
            across(u).wait_send()
        remote(sm.at[5], smr.at[3], sms.at[3], smrs.at[3], to_z).wait_send()


def reduce_units(grads, small):
    units = [(i, u) for i, g in enumerate(grads) for u in range(g.shape[0])]
    n = len(units)
    unit = grads[0].shape[2:]
    dma = pltpu.SemaphoreType.DMA
    return pl.pallas_call(
        functools.partial(reduce_kernel, units, len(grads)),
        out_shape=[
            jax.ShapeDtypeStruct((n,) + unit, F32),
            jax.ShapeDtypeStruct(small.shape, F32),
        ],
        in_specs=[HBM_SPEC] * len(grads) + [VMEM_SPEC],
        out_specs=[VMEM_SPEC] * 2,
        scratch_shapes=[
            pltpu.VMEM((n, 2) + unit, BF16),
            pltpu.VMEM((n, 2) + unit, BF16),
            pltpu.VMEM((n,) + unit, BF16),
            pltpu.VMEM((n,) + unit, BF16),
            pltpu.VMEM((n,) + unit, BF16),
            pltpu.VMEM((6,) + small.shape, F32),
            pltpu.VMEM((5,) + small.shape, F32),
            dma((n, 2)), dma((n, 2)), dma((n, 2)), dma((n,)), dma((n,)),
            dma((n,)), dma((n,)), dma((n,)), dma((n,)), dma((6,)), dma((6,)),
        ],
        compiler_params=params(collective_id=1, has_side_effects=True),
        name="reduce_gradients",
    )(*grads, small)


def plain_norm(h, gain, shift):
    cen = h - jnp.mean(h, -1, keepdims=True)
    inv = lax.rsqrt(jnp.mean(cen * cen, -1, keepdims=True) + EPS)
    return cen * inv * gain + shift


def per_device(on_boxes, tokens, out_grad, actions, segments, frame_mask, embed,
               ln1_gain, ln1_shift, spatial_qkv, spatial_out,
               ln2_gain, ln2_shift, temporal_qkv, temporal_out,
               ln3_gain, ln3_shift, ffn_in, ffn_in_bias, ffn_out, ffn_out_bias):
    frames_dev, tile_tokens, width = tokens.shape
    n_frame = lax.axis_size("frame")
    n_tile = lax.axis_size("tile")
    f = lax.axis_index("frame")
    t = lax.axis_index("tile")
    frames = frames_dev * n_frame
    place = tile_tokens // n_frame
    rows = frames_dev * tile_tokens
    row = lambda v: v[None, :]

    mats = (spatial_qkv, spatial_out, temporal_qkv, temporal_out, ffn_in, ffn_out)

    grad4 = out_grad.reshape(frames_dev, n_frame, place, width)
    action = lax.dynamic_index_in_dim(actions, t, keepdims=False)
    added = lax.dynamic_slice_in_dim(embed, action, 1, 0)

    blocks = n_frame * n_tile

    def turn(x, forward, cid, name):
        x = x.reshape(blocks, rows // blocks, width)
        if on_boxes:
            by_place = lambda f, t: 8 * t + f
            by_frame = lambda f, t: 4 * f + t
            a, b = (by_place, by_frame) if forward else (by_frame, by_place)
            y = swap_blocks(x, x.shape, ("frame", "tile"), a, b, cid, name)
        else:
            if forward:
                y = x.reshape(n_tile, n_frame, -1, width).transpose(1, 0, 2, 3)
                y = lax.all_to_all(y.reshape(x.shape), ("frame", "tile"), 0, 0, tiled=True)
            else:
                y = lax.all_to_all(x, ("frame", "tile"), 0, 0, tiled=True)
                y = y.reshape(n_frame, n_tile, -1, width).transpose(1, 0, 2, 3)
        return y.reshape(rows, width)

    number = jnp.arange(rows, dtype=jnp.int32)
    of_frame, of_place = number // place, number % place
    seg_row = jnp.repeat(segments, place)
    open_row = jnp.repeat(frame_mask, place)
    allowed = (
        (seg_row[:, None] == seg_row[None, :])
        & (of_place[:, None] == of_place[None, :])
        & (of_frame[None, :] <= of_frame[:, None])
        & ((open_row[None, :] == 1) | (of_frame[None, :] == of_frame[:, None]))
    )
    bias = jnp.where(allowed, 0.0, -1e30).astype(F32)
    nothing = jnp.zeros((1, width), F32)
    vecs = [row(v) for v in (ln1_gain, ln1_shift, ln2_gain, ln2_shift, ln3_gain, ln3_shift, ffn_in_bias, ffn_out_bias)]
    if on_boxes:
        (w_qs, w_os, w_qt, w_ot, w_in, w_out, base1, unit1, qkv1, mixed1, base2, unit2, qkv2, mixed2,
         after2, unit3, slope, act, g, g_out, result) = forward(mats, tokens, grad4, added, vecs, bias)
    else:
        w_qs, w_os, w_qt, w_ot, w_in, w_out = (lax.all_gather(m, "frame", axis=0, tiled=True) for m in mats)
        base1 = lax.all_to_all(tokens, "tile", 0, 0, tiled=True).reshape(rows, width)
        g = lax.all_to_all(grad4.transpose(1, 0, 2, 3), "frame", 0, 0, tiled=True).reshape(rows, width)
        unit1, qkv1, mixed1, after1 = attn_fwd(
            base1, added, vecs[0], vecs[1], w_qs, w_os, None, BF16, "spatial_forward")
        base2 = turn(after1, True, 4, "frames_to_places")
        unit2, qkv2, mixed2, after2 = attn_fwd(
            base2, nothing, vecs[2], vecs[3], w_qt, w_ot, bias, F32, "temporal_forward")
        unit3 = plain_norm(after2, ln3_gain, ln3_shift).astype(BF16)
        pre = jnp.dot(unit3, w_in, preferred_element_type=F32) + ffn_in_bias
        th = jnp.tanh(GELU_A * (pre + GELU_B * pre * pre * pre))
        act = (0.5 * pre * (1.0 + th)).astype(BF16)
        slope = 0.5 * (1.0 + th) + 0.5 * pre * (1.0 - th * th) * GELU_A * (1.0 + 3.0 * GELU_B * pre * pre)
        slope = slope.astype(BF16)
        result = after2 + jnp.dot(act, w_out, preferred_element_type=F32) + ffn_out_bias
        result = result.astype(BF16).reshape(n_frame, frames_dev, place, width)
        result = lax.all_to_all(result, "frame", 0, 0, tiled=True).transpose(1, 0, 2, 3)
    d_pre, d_after2, dg3, ds3, d_bin, d_bout = ffn_bwd(g, slope, after2, row(ln3_gain), w_in, w_out)
    low2, d_qkv2, d_after1, dg2, ds2 = attn_bwd(
        base2, nothing, row(ln2_gain), w_qt, w_ot, d_after2, qkv2, bias, BF16, "temporal_backward")
    d_out1 = turn(d_after1, False, 5, "places_to_frames")
    low1, d_qkv1, d_start, dg1, ds1 = attn_bwd(
        base1, added, row(ln1_gain), w_qs, w_os, d_out1, qkv1, None, F32, "spatial_backward")

    tokens_grad = d_start.astype(BF16).reshape(n_tile, tile_tokens, width)
    if on_boxes:
        tokens_grad = swap_blocks(tokens_grad, tokens.shape, ("tile",),
                                  lambda f, t: t, lambda f, t: t, 6, "tokens_grad_to_tiles")
    else:
        tokens_grad = lax.all_to_all(tokens_grad, "tile", 0, 0, tiled=True)
    result = result.reshape(tokens.shape)

    one_hot = (action == jnp.arange(embed.shape[0], dtype=jnp.int32)).astype(F32)
    d_embed = one_hot[:, None] * jnp.sum(d_start, 0, keepdims=True)

    pairs = (
        (unit1, d_qkv1, "spatial_qkv_grad"),
        (mixed1, low1, "spatial_out_grad"),
        (unit2, d_qkv2, "temporal_qkv_grad"),
        (mixed2, low2, "temporal_out_grad"),
        (unit3, d_pre, "ffn_in_grad"),
        (act, g, "ffn_out_grad"),
    )
    if on_boxes:
        small = jnp.concatenate(
            [d_embed, dg1, ds1, dg2, ds2, dg3, ds3, d_bout, d_bin.reshape(-1, width)], 0)
        small = jnp.pad(small, ((0, -small.shape[0] % 8), (0, 0)))
        core = lax.rem(f, 2)
        grads = [wgrad_units(a, b, a.shape[1] // 8, core, name) for a, b, name in pairs[:5]] + [g_out]
        order = (5, 4, 3, 2, 1, 0)
        out, small = reduce_units([grads[i] for i in order], small)
        summed = [None] * 6
        first = 0
        for i in order:
            n_row = pairs[i][0].shape[1] // 8 // 128
            n_col = pairs[i][1].shape[1] // 1024
            part = out[first : first + n_row * n_col].reshape(n_row, n_col, 128, 1024)
            summed[i] = part.transpose(0, 2, 1, 3).reshape(n_row * 128, n_col * 1024)
            first += n_row * n_col
        n_act = embed.shape[0]
        d_embed, vecs = small[:n_act], small[n_act:]
        dg1, ds1, dg2, ds2, dg3, ds3, d_bout = (vecs[i] for i in range(7))
        d_bin = vecs[7 : 7 + d_bin.shape[1] // width].reshape(-1)
    else:
        summed = []
        for a, b, _ in pairs:
            part = lax.dot_general(a, b, (((0,), (0,)), ((), ())), preferred_element_type=F32)
            part = lax.psum_scatter(part, "frame", scatter_dimension=0, tiled=True)
            summed.append(lax.psum(part.astype(BF16), "tile").astype(F32))
        d_embed, dg1, ds1, dg2, ds2, dg3, ds3, d_bin, d_bout = lax.psum(
            (d_embed, dg1[0], ds1[0], dg2[0], ds2[0], dg3[0], ds3[0], d_bin[0], d_bout[0]), ("frame", "tile"))

    return (result, tokens_grad, d_embed, dg1, ds1, summed[0], summed[1], dg2, ds2, summed[2], summed[3],
            dg3, ds3, summed[4], d_bin, summed[5], d_bout)


def solution(mesh):
    shard = P("frame", "tile", None)
    mat = P("frame", None)
    rep = P()
    in_specs = (shard, shard, P("frame"), rep, rep, rep, rep, rep, mat, mat, rep, rep, mat, mat,
                rep, rep, mat, rep, mat, rep)
    out_specs = (shard, shard, rep, rep, rep, mat, mat, rep, rep, mat, mat, rep, rep, mat, rep, mat, rep)
    on_boxes = mesh.shape["frame"] == 8 and mesh.shape["tile"] == 4
    return jax.shard_map(
        functools.partial(per_device, on_boxes),
        mesh=mesh, in_specs=in_specs, out_specs=out_specs, check_vma=False)
```

```python
import functools

import jax
import jax.numpy as jnp
from jax import lax
from jax.experimental import pallas as pl
from jax.experimental.pallas import tpu as pltpu
from jax.sharding import PartitionSpec as P

HD = 64
LANES = 128
EPS = 1e-5
MESH = pl.DeviceIdType.MESH
F32 = jnp.float32
BF16 = jnp.bfloat16
VMEM_SPEC = pl.BlockSpec(memory_space=pltpu.VMEM)
HBM_SPEC = pl.BlockSpec(memory_space=pltpu.HBM)


def params(**kw):
    return pltpu.CompilerParams(vmem_limit_bytes=58 * 1024 * 1024, **kw)


def at(j, size):
    return pl.ds(pl.multiple_of(j * size, size), size)


def each(n, fn):
    def step(i, carry):
        fn(i)
        return carry

    lax.fori_loop(0, n, step, 0)


def dot(a, b):
    return jnp.dot(a, b, preferred_element_type=F32)


def dot_nt(a, b):
    return lax.dot_general(a, b, (((1,), (1,)), ((), ())), preferred_element_type=F32)


def dot_tn(a, b):
    return lax.dot_general(a, b, (((0,), (0,)), ((), ())), preferred_element_type=F32)


def normed(h):
    cen = h - jnp.mean(h, -1, keepdims=True)
    inv = lax.rsqrt(jnp.mean(cen * cen, -1, keepdims=True) + EPS)
    return cen * inv, inv


ROWS = 32


def norm_rows(load, gain_ref, shift_ref, unit_ref):
    def step(i):
        rows = at(i, ROWS)
        xhat, _ = normed(load(rows))
        unit_ref[rows, :] = (xhat * gain_ref[...] + shift_ref[...]).astype(BF16)

    each(unit_ref.shape[0] // ROWS, step)


def fold(x):
    return jnp.sum(x.reshape(x.shape[0] // 8, 8, x.shape[1]), 0)


def norm_back(load, du_ref, gain_ref, dgain_ref, dshift_ref, acc_ref, store):
    acc_ref[...] = jnp.zeros_like(acc_ref)

    def step(i):
        rows = at(i, ROWS)
        xhat, inv = normed(load(rows))
        du = du_ref[rows, :]
        acc_ref[0] += fold(du * xhat)
        acc_ref[1] += fold(du)
        dx = du * gain_ref[...]
        dh = inv * (
            dx - jnp.mean(dx, -1, keepdims=True) - xhat * jnp.mean(dx * xhat, -1, keepdims=True)
        )
        store(rows, dh)

    each(du_ref.shape[0] // ROWS, step)
    dgain_ref[...] = jnp.sum(acc_ref[0], 0, keepdims=True)
    dshift_ref[...] = jnp.sum(acc_ref[1], 0, keepdims=True)


def head_masks():
    lane = lax.broadcasted_iota(jnp.int32, (1, LANES), 1)
    low = jnp.where(lane < HD, 1.0, 0.0)
    return low.astype(BF16), (1.0 - low).astype(BF16)


def head_probs(qm, k, bias_ref):
    s = dot_nt(qm, k) * (HD**-0.5)
    if bias_ref is not None:
        s = s + bias_ref[...]
    e = jnp.exp(s - jnp.max(s, -1, keepdims=True))
    return e * (1.0 / jnp.sum(e, -1, keepdims=True))


def attention(qkv_ref, bias_ref, mixed_ref):
    width = mixed_ref.shape[1]
    per = width // LANES
    masks = head_masks()

    def pair(p):
        q, k, v = (qkv_ref[:, at(p + i * per, LANES)] for i in range(3))
        out = 0.0
        for m in masks:
            out = out + dot(head_probs(q * m, k, bias_ref).astype(BF16), v * m)
        mixed_ref[:, at(p, LANES)] = out.astype(BF16)

    each(per, pair)


def attention_back(qkv_ref, bias_ref, dmix_ref, dqkv_ref):
    width = dmix_ref.shape[1]
    per = width // LANES
    masks = head_masks()
    scale = HD**-0.5

    def pair(p):
        q, k, v = (qkv_ref[:, at(p + i * per, LANES)] for i in range(3))
        dm = dmix_ref[:, at(p, LANES)]
        dq = dk = dv = 0.0
        for m in masks:
            qm = q * m
            dmm = dm * m
            probs = head_probs(qm, k, bias_ref)
            dp = dot_nt(dmm, v)
            ds = probs * (dp - jnp.sum(probs * dp, -1, keepdims=True))
            ds = ds.astype(BF16)
            dq = dq + dot(ds, k * m)
            dk = dk + dot_tn(ds, qm)
            dv = dv + dot_tn(probs.astype(BF16), dmm)
        dqkv_ref[:, at(p, LANES)] = (dq * scale).astype(BF16)
        dqkv_ref[:, at(p + per, LANES)] = (dk * scale).astype(BF16)
        dqkv_ref[:, at(p + 2 * per, LANES)] = dv.astype(BF16)

    each(per, pair)


def matmul(x_ref, w_ref, block, store):
    def step(j):
        cols = at(j, block)
        store(cols, dot(x_ref[...], w_ref[:, cols]))

    each(w_ref.shape[1] // block, step)


def matmul_nt(x_ref, w_ref, block, store):
    def step(j):
        rows = at(j, block)
        store(rows, dot_nt(x_ref[...], w_ref[rows, :]))

    each(w_ref.shape[0] // block, step)


def wgrad(core, shard, left, left_x, right, right_x, out, lt):
    tok = left.shape[0]
    col_blocks = right.shape[1] // TILE
    for rb in range(shard // 128):
        for q in range(4):
            cols = pl.ds(pl.multiple_of((2 * q + core) * shard + rb * 128, 128), 128)
            lt[q * 128 : (q + 1) * 128, :tok] = left[:, cols].T
            cols = pl.ds(q * shard + rb * 128, 128)
            lt[q * 128 : (q + 1) * 128, tok:] = left_x[:, cols].T

        def step(j, rb=rb):
            cols = at(j, 512)
            y = dot(lt[:, :tok], right[:, cols]) + dot(lt[:, tok:], right_x[:, cols])
            y = y.astype(BF16)
            unit = rb * col_blocks + j // 2
            half = pl.ds(pl.multiple_of(lax.rem(j, 2) * 512, 512), 512)
            for q in range(4):
                out[unit, q, :, half] = y[q * 128 : (q + 1) * 128]

        each(2 * col_blocks, step)


GELU_A = 0.7978845608
GELU_B = 0.044715


def xor(a, b):
    bit = lax.rem(a // b, 2)
    return a + b - 2 * b * bit


def greet(partners):
    barrier = pltpu.get_barrier_semaphore()
    for p in partners:
        pl.semaphore_signal(barrier, inc=1, device_id=p, device_id_type=MESH)
    pl.semaphore_wait(barrier, len(partners))


def remote(src, dst, ssem, rsem, dev):
    return pltpu.make_async_remote_copy(
        src_ref=src, dst_ref=dst, send_sem=ssem, recv_sem=rsem, device_id=dev, device_id_type=MESH
    )


def xor_any(a, bits):
    for b in (1, 2, 4, 8, 16):
        if bits & b:
            a = xor(a, b)
    return a


TILE = 1024
SLOTS = 6
AHEAD = 3


def gather_chunks(shapes):
    out = []
    for i, (rows, cols) in enumerate(shapes):
        step = rows
        while step * cols > 128 * 1024 and step % 32 == 0:
            step //= 2
        out += [(i, r, step) for r in range(0, rows, step)]
    return out


def weight_tiles(shapes):
    return [
        (i, r, c)
        for i, (rows, cols) in enumerate(shapes)
        for r in range(0, rows, TILE)
        for c in range(0, cols, TILE)
    ]


def forward_kernel(chunks, tiles, *refs):
    shards = refs[:6]
    (tokens, grad4, added, g1, s1, g2, s2, g3, s3, b_in, b_out, bias) = refs[6:18]
    full = refs[18:24]
    kept = refs[24:38]
    held = refs[38:52]
    (base1, unit1, qkv1, mixed1, base2, unit2, qkv2, mixed2, after2, unit3, slope, g2d, gout, res_out) = held
    (act, wt, base_in, out1, in2, g_in, y_ref, act_x, g_x, lt, ssem, rsem, bsem, tsem, z3s, z3r, z3l,
     f7s, f7r, f7l, turn_s, turn_r, turn_l, x_s, x_r, ksem) = refs[52:]
    f = lax.axis_index("frame")
    t = lax.axis_index("tile")
    core = lax.rem(f, 2)
    odd = lax.rem(t, 2)
    fx, fy = xor(f, 2), xor(f, 4)
    first = fx + (fy - fx) * odd
    second = fy + (fx - fy) * odd
    diag = xor_any(f, 6)
    sib = xor(f, 1)
    to_sib, to_first, to_second, to_z = (sib, t), (first, t), (second, t), (f, xor(t, 1))
    greet([(xor_any(f, a), xor_any(t, b)) for a in range(8) for b in range(4) if a or b])

    saves = [pltpu.make_async_copy(v, h, ksem.at[i]) for i, (v, h) in enumerate(zip(held, kept))]

    def piece(k, owner):
        a, r, n = chunks[k]
        return full[a].at[pl.ds(pl.multiple_of(owner * shards[a].shape[0] + r, 16), n)]

    def own(k):
        a, r, n = chunks[k]
        return shards[a].at[pl.ds(r, n)]

    def copy(k, kind):
        dev = (to_first, to_second, to_z, to_sib, to_sib, to_sib, to_sib)[kind]
        owner = (f, first, first, f, first, diag, second)[kind]
        src = own(k) if kind in (0, 3) else piece(k, owner)
        return remote(src, piece(k, owner), ssem.at[k, kind], rsem.at[k, kind], dev)

    def arrived(k, kind):
        owner = (first, diag, second, sib, xor(first, 1), xor(diag, 1), xor(second, 1))[kind]
        dst = piece(k, owner)
        remote(dst, dst, ssem.at[k, kind], rsem.at[k, kind], to_sib).wait_recv()

    n = len(chunks)

    def hop(k):
        copy(k, 3).start()
        arrived(k, 0)
        if k + AHEAD < n:
            copy(k + AHEAD, 0).start()
        for kind in (1, 2, 4):
            copy(k, kind).start()

    def relay(k):
        for kind in (1, 2):
            arrived(k, kind)
            copy(k, kind + 4).start()

    progress = [0, 0]

    def advance(hops):
        while progress[0] < min(hops, n):
            hop(progress[0])
            progress[0] += 1
            if progress[0] >= 2:
                relay(progress[1])
                progress[1] += 1
        if hops > n and progress[1] < n:
            relay(progress[1])
            progress[1] += 1

    bounce = []
    for a, shard in enumerate(shards):
        for r in range(0, shard.shape[0], 128):
            for c in range(0, shard.shape[1], TILE):
                i = len(bounce)
                bounce.append((a, r, c, wt.at[4 + i // 8, pl.ds(i % 8 * 128, 128)]))

    def bounce_in(i):
        a, r, c, via = bounce[i]
        return pltpu.make_async_copy(shards[a].at[pl.ds(r, 128), pl.ds(c, TILE)], via, bsem.at[i])

    def bounce_out(i):
        a, r, c, via = bounce[i]
        row = pl.multiple_of(f * shards[a].shape[0] + r, 128)
        return pltpu.make_async_copy(via, full[a].at[pl.ds(row, 128), pl.ds(c, TILE)], bsem.at[i])

    def tile_load(i):
        a, r, c = tiles[i]
        src = full[a].at[pl.ds(r, TILE), pl.ds(c, TILE)]
        return pltpu.make_async_copy(src, wt.at[i % SLOTS], tsem.at[i])

    def tile(i):
        return wt.at[i % SLOTS]

    def tiles_of(a):
        return [i for i, x in enumerate(tiles) if x[0] == a]

    def complete(a):
        ks = [k for k in range(n) if chunks[k][0] == a]
        advance(ks[-1] + 2)
        for k in ks:
            for kind in (3, 4, 5, 6):
                arrived(k, kind)

    def load(ids):
        for i in ids:
            tile_load(i).start()

    def ready(ids):
        for i in ids:
            tile_load(i).wait()

    def token_copy(i):
        d = xor_any(t, i)
        return remote(tokens.at[d], base_in.at[pl.ds(pl.multiple_of(t * 64, 64), 64)], z3s.at[i - 1], z3r.at[i - 1], (f, d))

    def token_arrived(i):
        d = xor_any(t, i)
        dst = base_in.at[pl.ds(pl.multiple_of(d * 64, 64), 64)]
        remote(tokens.at[d], dst, z3s.at[i - 1], z3r.at[i - 1], (f, d)).wait()

    own_tokens = pltpu.make_async_copy(tokens.at[t], base_in.at[pl.ds(pl.multiple_of(t * 64, 64), 64)], z3l)
    own_tokens.start()
    for i in (1, 2, 3):
        token_copy(i).start()
    for k in range(AHEAD):
        copy(k, 0).start()
    for i in range(len(bounce)):
        bounce_in(i).start()

    def grad_copy(i, dst_slot):
        d = xor_any(f, i)
        return remote(grad4.at[:, d], g_in.at[pl.ds(4 * dst_slot, 4)], f7s.at[i - 1], f7r.at[i - 1], (d, t))

    own_grad = pltpu.make_async_copy(grad4.at[:, f], g_in.at[pl.ds(4 * f, 4)], f7l)

    advance(1)
    for i in range(len(bounce)):
        bounce_in(i).wait()
        bounce_out(i).start()
    own_tokens.wait()
    for i in (1, 2, 3):
        token_arrived(i)

    def plain(i):
        rows = at(i, ROWS)
        base1[rows, :] = base_in[rows, :]

    each(base1.shape[0] // ROWS, plain)
    norm_rows(lambda rows: base1[rows, :].astype(F32) + added[...], g1, s1, unit1)
    own_grad.start()
    for i in range(1, 8):
        grad_copy(i, f).start()
    for i in range(len(bounce)):
        bounce_out(i).wait()

    def project(unit, ids, out_ref):
        for j, i in enumerate(ids):
            def put(cols, y, j=j):
                start = pl.multiple_of(cols.start + j * TILE, 512)
                out_ref[:, pl.ds(start, 512)] = y.astype(BF16)

            matmul(unit, tile(i), 512, put)

    saves[0].start()
    saves[1].start()
    complete(0)
    load(tiles_of(0))
    ready(tiles_of(0))
    project(unit1, tiles_of(0), qkv1)
    complete(1)
    load(tiles_of(1))
    saves[2].start()
    attention(qkv1, None, mixed1)
    saves[3].start()
    ready(tiles_of(1))

    def put_after1(cols, y):
        y = y + base1[:, cols].astype(F32) + added[:, cols]
        y_ref[:, cols] = y

    matmul(mixed1, tile(tiles_of(1)[0]), 512, put_after1)

    def split(i):
        rows = at(i, ROWS)
        out1[pl.ds(4 * i, 4)] = y_ref[rows, :].reshape(4, 8, TILE).astype(BF16)

    each(y_ref.shape[0] // ROWS, split)

    slot = 4 * f + t
    others = [(a, b) for a in range(8) for b in range(4) if a or b]

    def turn_copy(i, d, dst_slot):
        return remote(out1.at[8 * d[1] + d[0]], in2.at[dst_slot], turn_s.at[i], turn_r.at[i], d)

    own_turn = pltpu.make_async_copy(out1.at[8 * t + f], in2.at[slot], turn_l)
    own_turn.start()
    for i, (a, b) in enumerate(others):
        turn_copy(i, (xor_any(f, a), xor_any(t, b)), slot).start()
    complete(2)
    load(tiles_of(2))
    complete(3)
    load(tiles_of(3))
    own_turn.wait()
    for i, (a, b) in enumerate(others):
        d = (xor_any(f, a), xor_any(t, b))
        turn_copy(i, d, 4 * d[0] + d[1]).wait()

    def join(i):
        base2[at(i, ROWS), :] = in2[pl.ds(4 * i, 4)].astype(F32).reshape(ROWS, TILE).astype(BF16)

    each(base2.shape[0] // ROWS, join)
    norm_rows(lambda rows: base2[rows, :].astype(F32), g2, s2, unit2)
    ready(tiles_of(2))
    project(unit2, tiles_of(2), qkv2)
    advance(12)
    attention(qkv2, bias, mixed2)
    for i in (4, 5, 6, 7):
        saves[i].start()
    advance(14)
    ready(tiles_of(3))

    def put_after2(cols, y):
        after2[:, cols] = y + base2[:, cols].astype(F32)

    matmul(mixed2, tile(tiles_of(3)[0]), 512, put_after2)
    norm_rows(lambda rows: after2[rows, :], g3, s3, unit3)
    complete(4)
    load(tiles_of(4))
    saves[8].start()
    saves[9].start()

    own_grad.wait()
    for i in range(1, 8):
        grad_copy(i, xor_any(f, i)).wait()

    def join_grad(i):
        g2d[at(i, ROWS), :] = g_in[pl.ds(4 * i, 4)].astype(F32).reshape(ROWS, TILE).astype(BF16)

    each(g2d.shape[0] // ROWS, join_grad)

    for j, i in enumerate(tiles_of(4)):
        tile_load(i).wait()

        def put_pre(cols, y, j=j):
            cols = pl.ds(pl.multiple_of(cols.start + j * TILE, 256), 256)
            v = y + b_in[:, cols]
            th = jnp.tanh(GELU_A * (v + GELU_B * v * v * v))
            act[:, cols] = (0.5 * v * (1.0 + th)).astype(BF16)
            rise = 0.5 * (1.0 + th) + 0.5 * v * (1.0 - th * th) * GELU_A * (1.0 + 3.0 * GELU_B * v * v)
            slope[:, cols] = rise.astype(BF16)

        matmul(unit3, tile(i), 256, put_pre)

    saves[10].start()
    saves[11].start()

    shard = shards[5].shape[0]
    swaps = [
        remote(act.at[:, pl.ds(pl.multiple_of((2 * q + 1 - core) * shard, shard), shard)],
               act_x.at[:, pl.ds(q * shard, shard)], x_s.at[q], x_r.at[q], to_sib)
        for q in range(4)
    ]
    swaps.append(remote(g2d, g_x, x_s.at[4], x_r.at[4], to_sib))
    for c in swaps:
        c.start()
    advance(16)
    for c in swaps:
        c.wait()
    wgrad(core, shard, act, act_x, g2d, g_x, gout, lt)
    saves[12].start()
    complete(5)
    ids = tiles_of(5)
    load(ids)
    for j, i in enumerate(ids):
        tile_load(i).wait()

        def part(h, i=i, j=j):
            cols = at(h, 512)
            y = dot(act[:, j * TILE : (j + 1) * TILE], wt[i % SLOTS, :, cols])
            y_ref[:, cols] = y + (after2[:, cols] + b_out[:, cols] if j == 0 else y_ref[:, cols])

        each(2, part)

    def split_res(i):
        res_out[pl.ds(4 * i, 4)] = y_ref[at(i, ROWS), :].reshape(4, 8, TILE).astype(BF16)

    each(y_ref.shape[0] // ROWS, split_res)

    saves[13].start()
    for k in range(n):
        for kind in range(7):
            copy(k, kind).wait_send()
    for c in saves:
        c.wait()


def forward(mats, tokens, grad4, added, vecs, bias):
    width = tokens.shape[2]
    rows = tokens.shape[0] * tokens.shape[1]
    ff = mats[4].shape[1]
    fulls = [(8 * m.shape[0], m.shape[1]) for m in mats]
    chunks = gather_chunks([m.shape for m in mats])
    tiles = weight_tiles(fulls)
    n = len(chunks)
    dma = pltpu.SemaphoreType.DMA
    units = mats[5].shape[0] // 128
    blocks = (32, 8, width)
    held = [
        ((rows, w), d)
        for w, d in (
            (width, BF16), (width, BF16), (3 * width, BF16), (width, BF16),
            (width, BF16), (width, BF16), (3 * width, BF16), (width, BF16),
            (width, F32), (width, BF16), (ff, BF16), (width, BF16),
        )
    ]
    held += [((units, 4, 128, TILE), BF16), (blocks, BF16)]
    outs = [jax.ShapeDtypeStruct(s, BF16) for s in fulls]
    outs += [jax.ShapeDtypeStruct(s, d) for s, d in held]
    return pl.pallas_call(
        functools.partial(forward_kernel, chunks, tiles),
        out_shape=outs,
        in_specs=[HBM_SPEC] * 8 + [VMEM_SPEC] * 10,
        out_specs=[HBM_SPEC] * len(outs),
        scratch_shapes=[pltpu.VMEM(s, d) for s, d in held] + [
            pltpu.VMEM((rows, ff), BF16),
            pltpu.VMEM((SLOTS, TILE, TILE), BF16),
            pltpu.VMEM((rows, width), BF16),
            pltpu.VMEM(blocks, BF16), pltpu.VMEM(blocks, BF16), pltpu.VMEM(blocks, BF16),
            pltpu.VMEM((rows, width), F32),
            pltpu.VMEM((rows, ff // 2), BF16), pltpu.VMEM((rows, width), BF16),
            pltpu.VMEM((512, 2 * rows), BF16),
            dma((n, 7)), dma((n, 7)), dma((16,)), dma((len(tiles),)),
            dma((3,)), dma((3,)), dma, dma((7,)), dma((7,)), dma,
            dma((31,)), dma((31,)), dma, dma((5,)), dma((5,)), dma((14,)),
        ],
        compiler_params=params(collective_id=0, has_side_effects=True),
        name="forward",
    )(*mats, tokens, grad4, added, *vecs, bias)


DEEP = 3
RING = 8
SLOTS_B = 4


def add_into(dst, a, b):
    def step(i):
        r = at(i, 16)
        dst[r, :] = (a[r, :].astype(F32) + b[r, :].astype(F32)).astype(dst.dtype)

    each(dst.shape[0] // 16, step)


def backward_kernel(tiles, units, *refs):
    full = refs[:6]
    (gout_h, res_h, base1_h, unit1_h, qkv1_h, mixed1_h, base2_h, unit2_h, qkv2_h, mixed2_h,
     after2_h, unit3_h, slope_h, g_h) = refs[6:20]
    added, gain1, gain2, gain3, bias, hot = refs[20:26]
    outs = refs[26:32]
    small_out, tokens_grad, result = refs[32:35]
    (base1, unit1, qkv1, mixed1, base2, unit2, qkv2, mixed2, after2, unit3, slope, g2d,
     wt, gbuf, r1, r2, zin, zpeer, dpre_x, unit3_x, mix2_x, low2_x, unit2_x, dqkv2_x,
     mix1_x, low1_x, unit1_x, dqkv1_x, du, dafter, low2, low1, dmix, dqkv, turn_out, turn_in, tg,
     sm, smr, lt, acc, emb,
     lsem, tsem, s1s, s1r, s2s, s2r, zs, zr, zps, zpr, osem, sms, smrs, xs, xr,
     turn_s, turn_r, turn_l, o7s, o7r, o7l, z3s, z3r, z3l) = refs[35:]
    f = lax.axis_index("frame")
    t = lax.axis_index("tile")
    core = lax.rem(f, 2)
    chip = f // 2
    leaf = (t == 0) | (t == 3)
    inner = jnp.logical_not(leaf)
    sib = xor(f, 1)
    cx, cy, cd = xor(chip, 1), xor(chip, 2), xor_any(chip, 3)
    to_sib, to_x, to_y = (sib, t), (xor(f, 2), t), (xor(f, 4), t)
    to_z, to_peer = (f, xor(t, 1)), (f, 3 - t)

    kept = [(g_h, g2d), (slope_h, slope), (gout_h, gbuf.at[0]), (after2_h, after2), (unit3_h, unit3),
            (mixed2_h, mixed2), (qkv2_h, qkv2), (base2_h, base2), (unit2_h, unit2),
            (mixed1_h, mixed1), (qkv1_h, qkv1), (base1_h, base1), (unit1_h, unit1)]
    loads = [pltpu.make_async_copy(h, v, lsem.at[i]) for i, (h, v) in enumerate(kept)]

    def tile_load(i):
        a, r, c = tiles[i]
        src = full[a].at[pl.ds(r, TILE), pl.ds(c, TILE)]
        return pltpu.make_async_copy(src, wt.at[i % SLOTS_B], tsem.at[i])

    for c in loads[:3]:
        c.start()
    for i in range(SLOTS_B):
        tile_load(i).start()
    for c in loads[3:]:
        c.start()
    greet([(xor_any(f, a), xor_any(t, b)) for a in range(8) for b in range(4) if a or b])

    n = len(units)

    def hop(u):
        return (to_x, cx, to_y, cy) if u % 2 == 0 else (to_y, cy, to_x, cx)

    def part(u, p):
        return gbuf.at[u // 4 % 3, u % 4, p]

    def step1(u):
        dev1, p1, dev2, p2 = hop(u)
        k = u % RING
        return (
            remote(part(u, cd), r1.at[k, 1], s1s.at[u, 1], s1r.at[u, 1], dev1),
            remote(part(u, p1), r1.at[k, 0], s1s.at[u, 0], s1r.at[u, 0], dev1),
        )

    def step2(u):
        _, _, dev2, p2 = hop(u)
        return remote(part(u, p2), r2.at[u % RING], s2s.at[u], s2r.at[u], dev2)

    def to_inner(u):
        return remote(part(u, chip), zin.at[u % RING], zs.at[u], zr.at[u], to_z)

    def across(u):
        return remote(part(u, chip), zpeer.at[u % RING], zps.at[u], zpr.at[u], to_peer)

    def emit(u, src):
        a, r, c = units[u]
        return pltpu.make_async_copy(src, outs[a].at[pl.ds(r, 128), pl.ds(c, TILE)], osem.at[u])

    state = {"ready": 0, "issued": 0, "done": 0, "step": 0}

    def issue():
        while state["issued"] < min(state["ready"], state["done"] + DEEP):
            for c in step1(state["issued"]):
                c.start()
            state["issued"] += 1

    def offer(count):
        state["ready"] += count
        issue()

    def reduce_step():
        s = state["step"]
        state["step"] += 1
        u = s
        if u < n:
            assert u < state["issued"]
            p2 = hop(u)[3]
            far, near = step1(u)
            far.wait_recv()
            add_into(part(u, p2), part(u, p2), r1.at[u % RING, 1])
            step2(u).start()
            near.wait_recv()
            add_into(part(u, chip), part(u, chip), r1.at[u % RING, 0])
            state["done"] += 1
            issue()
        u = s - 1
        if 0 <= u < n:
            step2(u).wait_recv()
            add_into(part(u, chip), part(u, chip), r2.at[u % RING])

            @pl.when(leaf)
            def _(u=u):
                to_inner(u).start()

        u = s - 2
        if 0 <= u < n:
            @pl.when(inner)
            def _(u=u):
                to_inner(u).wait_recv()
                add_into(part(u, chip), part(u, chip), zin.at[u % RING])
                across(u).start()

        u = s - 3
        if 0 <= u < n:
            @pl.when(inner)
            def _(u=u):
                across(u).wait()
                add_into(part(u, chip), part(u, chip), zpeer.at[u % RING])
                to_inner(u).start()
                emit(u, part(u, chip)).start()

        u = s - 4
        if 0 <= u < n:
            @pl.when(leaf)
            def _(u=u):
                to_inner(u).wait()
                emit(u, zin.at[u % RING]).start()

        u = s - 5
        if 0 <= u < n:
            for c in step1(u):
                c.wait_send()
            step2(u).wait_send()

            @pl.when(inner)
            def _(u=u):
                to_inner(u).wait_send()

            emit(u, part(u, chip)).wait()

    def reduce_to(s):
        while state["step"] < s:
            reduce_step()

    def share(i, left, left_x, right, right_x):
        shard = left.shape[1] // 8
        copies = [
            remote(left.at[:, pl.ds(pl.multiple_of((2 * p + 1 - core) * shard, shard), shard)],
                   left_x.at[:, pl.ds(p * shard, shard)], xs.at[i, p], xr.at[i, p], to_sib)
            for p in range(4)
        ]
        copies.append(remote(right, right_x, xs.at[i, 4], xr.at[i, 4], to_sib))
        for c in copies:
            c.start()
        return copies

    def shared(copies):
        for c in copies:
            c.wait()

    def res_copy(i, dst):
        d = xor_any(f, i)
        return remote(res_h.at[pl.ds(4 * d, 4)], result.at[:, dst], o7s.at[i - 1], o7r.at[i - 1], (d, t))

    own_res = pltpu.make_async_copy(res_h.at[pl.ds(4 * f, 4)], result.at[:, f], o7l)

    loads[2].wait()
    offer(4)
    loads[0].wait()
    loads[1].wait()

    sm[0] = jnp.zeros_like(sm[0])
    for j in range(4):
        tile_load(j).wait()

        def put_dpre(rows, y, j=j):
            cols = pl.ds(pl.multiple_of(rows.start + j * TILE, 256), 256)
            d = (y * slope[:, cols].astype(F32)).astype(BF16)
            slope[:, cols] = d
            sm[0, 15 + j : 16 + j, rows] = jnp.sum(d.astype(F32), 0, keepdims=True)

        matmul_nt(g2d, wt.at[j], 256, put_dpre)
        tile_load(j + 4).start()
    dpre = slope
    loads[4].wait()
    swap3 = share(0, unit3, unit3_x, dpre, dpre_x)
    reduce_to(1)

    def back_through(first, count, x_ref, after):
        for j in range(count):
            i = first + j
            tile_load(i).wait()

            def put(rows, y, j=j):
                du[:, rows] = y if j == 0 else du[:, rows] + y

            def run(h, i=i, j=j, put=put):
                rows = at(h, 256)
                put(rows, dot_nt(x_ref[:, j * TILE : (j + 1) * TILE], wt[i % SLOTS_B, rows, :]))

            each(TILE // 256, run)
            if i + SLOTS_B < len(tiles):
                tile_load(i + SLOTS_B).start()

    back_through(4, 4, dpre, None)
    loads[3].wait()
    sm[0, 14:15, :] = jnp.zeros((1, TILE), F32)

    def store3(rows, dh):
        g = g2d[rows, :].astype(F32)
        d = g + dh
        dafter[rows, :] = d
        low2[rows, :] = d.astype(BF16)
        sm[0, 14:15, :] += jnp.sum(g, 0, keepdims=True)

    norm_back(lambda rows: after2[rows, :], du, gain3, sm.at[0, pl.ds(12, 1)], sm.at[0, pl.ds(13, 1)], acc, store3)
    loads[5].wait()
    swap2o = share(1, mixed2, mix2_x, low2, low2_x)
    reduce_to(2)
    shared(swap3)
    wgrad(core, unit3.shape[1] // 8, unit3, unit3_x, dpre, dpre_x, gbuf.at[1], lt)
    offer(4)

    def put_mix(rows, y):
        dmix[:, rows] = y.astype(BF16)

    tile_load(8).wait()
    matmul_nt(low2, wt.at[8 % SLOTS_B], 512, put_mix)
    tile_load(12).start()
    loads[6].wait()
    reduce_to(3)
    attention_back(qkv2, bias, dmix, dqkv)
    loads[8].wait()
    swap2 = share(2, unit2, unit2_x, dqkv, dqkv2_x)
    reduce_to(4)
    back_through(9, 3, dqkv, None)
    loads[7].wait()

    def store2(rows, dh):
        d = dafter[rows, :] + dh
        dafter[rows, :] = d

    norm_back(lambda rows: base2[rows, :].astype(F32), du, gain2, sm.at[0, pl.ds(10, 1)], sm.at[0, pl.ds(11, 1)], acc, store2)

    def split(i):
        turn_out[pl.ds(4 * i, 4)] = dafter[at(i, ROWS), :].reshape(4, 8, TILE).astype(BF16)

    each(dafter.shape[0] // ROWS, split)

    slot = 8 * t + f
    others = [(a, b) for a in range(8) for b in range(4) if a or b]

    def turn_copy(i, d, dst_slot):
        return remote(turn_out.at[4 * d[0] + d[1]], turn_in.at[dst_slot], turn_s.at[i], turn_r.at[i], d)

    own_turn = pltpu.make_async_copy(turn_out.at[4 * f + t], turn_in.at[slot], turn_l)
    own_turn.start()
    for i, (a, b) in enumerate(others):
        turn_copy(i, (xor_any(f, a), xor_any(t, b)), slot).start()
    shared(swap2o)
    wgrad(core, TILE // 8, mixed2, mix2_x, low2, low2_x, gbuf.at[2, pl.ds(0, 1)], lt)
    shared(swap2)
    wgrad(core, TILE // 8, unit2, unit2_x, dqkv, dqkv2_x, gbuf.at[2, pl.ds(1, 3)], lt)
    offer(4)
    reduce_to(5)
    own_turn.wait()
    for i, (a, b) in enumerate(others):
        d = (xor_any(f, a), xor_any(t, b))
        turn_copy(i, d, 8 * d[1] + d[0]).wait()

    def join(i):
        low1[at(i, ROWS), :] = turn_in[pl.ds(4 * i, 4)].astype(F32).reshape(ROWS, TILE).astype(BF16)

    each(low1.shape[0] // ROWS, join)
    for c in loads[9:]:
        c.wait()
    swap1o = share(3, mixed1, mix1_x, low1, low1_x)
    tile_load(12).wait()
    matmul_nt(low1, wt.at[12 % SLOTS_B], 512, put_mix)
    reduce_to(6)
    attention_back(qkv1, None, dmix, dqkv)
    swap1 = share(4, unit1, unit1_x, dqkv, dqkv1_x)
    shared(swap1o)
    wgrad(core, TILE // 8, mixed1, mix1_x, low1, low1_x, gbuf.at[0, pl.ds(0, 1)], lt)
    offer(1)
    reduce_to(7)
    back_through(13, 3, dqkv, None)
    reduce_to(9)
    shared(swap1)
    wgrad(core, TILE // 8, unit1, unit1_x, dqkv, dqkv1_x, gbuf.at[0, pl.ds(1, 3)], lt)
    offer(3)
    emb[...] = jnp.zeros_like(emb)

    def store1(rows, dh):
        d = low1[rows, :].astype(F32) + dh
        tg[rows, :] = d.astype(BF16)
        emb[...] += fold(d)

    norm_back(lambda rows: base1[rows, :].astype(F32) + added[...], du, gain1, sm.at[0, pl.ds(8, 1)], sm.at[0, pl.ds(9, 1)], acc, store1)
    sm[0, 0:8, :] = hot[...] * jnp.sum(emb[...], 0, keepdims=True)

    def token_copy(i, d, dst):
        return remote(tg.at[pl.ds(pl.multiple_of(d * 64, 64), 64)], tokens_grad.at[dst], z3s.at[i - 1], z3r.at[i - 1], (f, d))

    own_tokens = pltpu.make_async_copy(tg.at[pl.ds(pl.multiple_of(t * 64, 64), 64)], tokens_grad.at[t], z3l)
    own_tokens.start()
    for i in (1, 2, 3):
        token_copy(i, xor_any(t, i), t).start()

    def small_copy(i, dev):
        return remote(sm.at[i], smr.at[i], sms.at[i], smrs.at[i], dev)

    def small_down():
        return remote(sm.at[5], smr.at[3], sms.at[5], smrs.at[3], to_z)

    hops = (to_sib, to_x, to_y)
    small_copy(0, to_sib).start()
    for i in range(3):
        reduce_to(state["step"] + 1)
        small_copy(i, hops[i]).wait()
        sm[i + 1] = sm[i] + smr[i]
        if i < 2:
            small_copy(i + 1, hops[i + 1]).start()

    @pl.when(leaf)
    def _():
        small_copy(3, to_z).start()

    reduce_to(state["step"] + 1)

    @pl.when(inner)
    def _():
        small_copy(3, to_z).wait_recv()
        sm[4] = sm[3] + smr[3]
        small_copy(4, to_peer).start()

    reduce_to(state["step"] + 1)

    @pl.when(inner)
    def _():
        small_copy(4, to_peer).wait()
        sm[5] = sm[4] + smr[4]
        small_down().start()
        small_out[...] = sm[5]

    own_res.start()
    for i in range(1, 8):
        res_copy(i, f).start()
    reduce_to(n + 5)

    @pl.when(leaf)
    def _():
        small_copy(3, to_z).wait()
        small_out[...] = smr[3]

    @pl.when(inner)
    def _():
        small_down().wait_send()

    own_tokens.wait()
    for i in (1, 2, 3):
        d = xor_any(t, i)
        token_copy(i, d, d).wait()
    own_res.wait()
    for i in range(1, 8):
        res_copy(i, xor_any(f, i)).wait()


def backward(fulls, kept, added, gains, bias, hot, tokens_shape, result_shape):
    width = tokens_shape[2]
    rows = tokens_shape[0] * tokens_shape[1]
    order = (5, 4, 3, 2, 1, 0)
    shapes = [w.shape for w in fulls]
    all_tiles = weight_tiles(shapes)
    tiles = [x for a in order for x in all_tiles if x[0] == a]
    shards = [(s[0] // 8, s[1]) for s in shapes]
    units = [
        (a, r, c) for a in order for r in range(0, shards[a][0], 128) for c in range(0, shards[a][1], TILE)
    ]
    n = len(units)
    ff = shapes[4][1]
    dma = pltpu.SemaphoreType.DMA
    blocks = (32, 8, width)
    unit = (128, TILE)
    bf = lambda *s: pltpu.VMEM(s, BF16)
    fl = lambda *s: pltpu.VMEM(s, F32)
    half, quarter = width // 2, width // 4
    return pl.pallas_call(
        functools.partial(backward_kernel, tiles, units),
        out_shape=[jax.ShapeDtypeStruct(s, BF16) for s in shards] + [
            jax.ShapeDtypeStruct((24, width), F32),
            jax.ShapeDtypeStruct(tokens_shape, BF16),
            jax.ShapeDtypeStruct(result_shape, BF16),
        ],
        in_specs=[HBM_SPEC] * (6 + len(kept)) + [VMEM_SPEC] * 6,
        out_specs=[HBM_SPEC] * 6 + [VMEM_SPEC] + [HBM_SPEC] * 2,
        scratch_shapes=[
            bf(rows, width), bf(rows, width), bf(rows, 3 * width), bf(rows, width),
            bf(rows, width), bf(rows, width), bf(rows, 3 * width), bf(rows, width),
            fl(rows, width), bf(rows, width), bf(rows, ff), bf(rows, width),
            bf(SLOTS_B, TILE, TILE), bf(3, 4, 4, *unit), bf(RING, 2, *unit), bf(RING, *unit),
            bf(RING, *unit), bf(RING, *unit),
            bf(rows, ff), bf(rows, half),
            bf(rows, half), bf(rows, width), bf(rows, half), bf(rows, 3 * width),
            bf(rows, half), bf(rows, width), bf(rows, half), bf(rows, 3 * width),
            fl(rows, width), fl(rows, width), bf(rows, width), bf(rows, width), bf(rows, width),
            bf(rows, 3 * width), bf(*blocks), bf(*blocks), bf(rows, width),
            fl(6, 24, width), fl(5, 24, width), bf(512, 2 * rows), fl(2, 8, width), fl(8, width),
            dma((13,)), dma((len(tiles),)), dma((n, 2)), dma((n, 2)), dma((n,)), dma((n,)),
            dma((n,)), dma((n,)), dma((n,)), dma((n,)), dma((n,)), dma((6,)), dma((6,)), dma((5, 5)), dma((5, 5)),
            dma((31,)), dma((31,)), dma, dma((7,)), dma((7,)), dma, dma((3,)), dma((3,)), dma,
        ],
        compiler_params=params(collective_id=1, has_side_effects=True),
        name="backward",
    )(*fulls, *kept, added, *gains, bias, hot)


def plain_norm(h, gain, shift):
    cen = h - jnp.mean(h, -1, keepdims=True)
    inv = lax.rsqrt(jnp.mean(cen * cen, -1, keepdims=True) + EPS)
    return cen * inv * gain + shift


def attn_fwd_kernel(masked, base_ref, added_ref, gain_ref, shift_ref, wqkv_ref, wo_ref, *rest):
    if masked:
        bias_ref, unit_ref, qkv_ref, mixed_ref, after_ref = rest
    else:
        bias_ref = None
        unit_ref, qkv_ref, mixed_ref, after_ref = rest

    def load(rows):
        return base_ref[rows, :].astype(F32) + added_ref[...]

    norm_rows(load, gain_ref, shift_ref, unit_ref)

    def put_qkv(cols, y):
        qkv_ref[:, cols] = y.astype(BF16)

    matmul(unit_ref, wqkv_ref, 512, put_qkv)
    attention(qkv_ref, bias_ref, mixed_ref)

    def put_after(cols, y):
        y = y + base_ref[:, cols].astype(F32) + added_ref[:, cols]
        after_ref[:, cols] = y.astype(after_ref.dtype)

    matmul(mixed_ref, wo_ref, 512, put_after)


def attn_fwd(base, added, gain, shift, wqkv, wo, bias, out_type, name):
    rows, width = base.shape
    ins = [base, added, gain, shift, wqkv, wo] + ([bias] if bias is not None else [])
    shapes = [(width, BF16), (3 * width, BF16), (width, BF16), (width, out_type)]
    return pl.pallas_call(
        functools.partial(attn_fwd_kernel, bias is not None),
        out_shape=[jax.ShapeDtypeStruct((rows, w), d) for w, d in shapes],
        in_specs=[VMEM_SPEC] * len(ins),
        out_specs=[VMEM_SPEC] * 4,
        compiler_params=params(),
        name=name,
    )(*ins)


def attn_bwd_kernel(masked, base_ref, added_ref, gain_ref, wqkv_ref, wo_ref, dout_ref, qkv_ref, *rest):
    if masked:
        bias_ref, *rest = rest
    else:
        bias_ref = None
    dlow_ref, dqkv_ref, dbase_ref, dgain_ref, dshift_ref, dmix_ref, du_ref, acc_ref = rest

    def cast(i):
        rows = at(i, ROWS)
        dlow_ref[rows, :] = dout_ref[rows, :].astype(BF16)

    each(dlow_ref.shape[0] // ROWS, cast)

    def put_mix(rows, y):
        dmix_ref[:, rows] = y.astype(BF16)

    matmul_nt(dlow_ref, wo_ref, 512, put_mix)
    attention_back(qkv_ref, bias_ref, dmix_ref, dqkv_ref)

    def put_du(rows, y):
        du_ref[:, rows] = y

    matmul_nt(dqkv_ref, wqkv_ref, 256, put_du)

    def load(rows):
        return base_ref[rows, :].astype(F32) + added_ref[...]

    def store(rows, dh):
        dbase_ref[rows, :] = (dout_ref[rows, :].astype(F32) + dh).astype(dbase_ref.dtype)

    norm_back(load, du_ref, gain_ref, dgain_ref, dshift_ref, acc_ref, store)


def attn_bwd(base, added, gain, wqkv, wo, dout, qkv, bias, out_type, name):
    rows, width = base.shape
    ins = [base, added, gain, wqkv, wo, dout, qkv] + ([bias] if bias is not None else [])
    outs = [
        jax.ShapeDtypeStruct((rows, width), BF16),
        jax.ShapeDtypeStruct((rows, 3 * width), BF16),
        jax.ShapeDtypeStruct((rows, width), out_type),
        jax.ShapeDtypeStruct((1, width), F32),
        jax.ShapeDtypeStruct((1, width), F32),
    ]
    return pl.pallas_call(
        functools.partial(attn_bwd_kernel, bias is not None),
        out_shape=outs,
        in_specs=[VMEM_SPEC] * len(ins),
        out_specs=[VMEM_SPEC] * len(outs),
        scratch_shapes=[
            pltpu.VMEM((rows, width), BF16),
            pltpu.VMEM((rows, width), F32),
            pltpu.VMEM((2, 8, width), F32),
        ],
        compiler_params=params(),
        name=name,
    )(*ins)


def ffn_bwd_kernel(g_ref, slope_ref, after_ref, gain_ref, win_ref, wout_ref,
                   dslope_ref, dafter_ref, dgain_ref, dshift_ref, dbin_ref, dbout_ref, du_ref, acc_ref):
    def put_dpre(rows, y):
        d = (y * slope_ref[:, rows].astype(F32)).astype(BF16)
        dslope_ref[:, rows] = d
        dbin_ref[:, rows] = jnp.sum(d.astype(F32), 0, keepdims=True)

    matmul_nt(g_ref, wout_ref, 512, put_dpre)

    def put_du(rows, y):
        du_ref[:, rows] = y

    matmul_nt(dslope_ref, win_ref, 256, put_du)
    dbout_ref[...] = jnp.zeros_like(dbout_ref)

    def store(rows, dh):
        g = g_ref[rows, :].astype(F32)
        dafter_ref[rows, :] = g + dh
        dbout_ref[...] += jnp.sum(g, 0, keepdims=True)

    norm_back(lambda rows: after_ref[rows, :], du_ref, gain_ref, dgain_ref, dshift_ref, acc_ref, store)


def ffn_bwd(g, slope, after, gain, win, wout):
    rows, width = after.shape
    ff = win.shape[1]
    row = lambda n: jax.ShapeDtypeStruct((1, n), F32)
    return pl.pallas_call(
        ffn_bwd_kernel,
        out_shape=[
            jax.ShapeDtypeStruct((rows, ff), BF16),
            jax.ShapeDtypeStruct((rows, width), F32),
            row(width), row(width), row(ff), row(width),
        ],
        in_specs=[VMEM_SPEC] * 6,
        out_specs=[VMEM_SPEC] * 6,
        scratch_shapes=[pltpu.VMEM((rows, width), F32), pltpu.VMEM((2, 8, width), F32)],
        compiler_params=params(),
        name="ffn_backward",
    )(g, slope, after, gain, win, wout)


def per_device(on_boxes, tokens, out_grad, actions, segments, frame_mask, embed,
               ln1_gain, ln1_shift, spatial_qkv, spatial_out,
               ln2_gain, ln2_shift, temporal_qkv, temporal_out,
               ln3_gain, ln3_shift, ffn_in, ffn_in_bias, ffn_out, ffn_out_bias):
    frames_dev, tile_tokens, width = tokens.shape
    n_frame = lax.axis_size("frame")
    n_tile = lax.axis_size("tile")
    f = lax.axis_index("frame")
    t = lax.axis_index("tile")
    frames = frames_dev * n_frame
    place = tile_tokens // n_frame
    rows = frames_dev * tile_tokens
    row = lambda v: v[None, :]

    mats = (spatial_qkv, spatial_out, temporal_qkv, temporal_out, ffn_in, ffn_out)

    grad4 = out_grad.reshape(frames_dev, n_frame, place, width)
    action = lax.dynamic_index_in_dim(actions, t, keepdims=False)
    added = lax.dynamic_slice_in_dim(embed, action, 1, 0)

    blocks = n_frame * n_tile

    def turn(x, forward):
        x = x.reshape(blocks, rows // blocks, width)
        if forward:
            y = x.reshape(n_tile, n_frame, -1, width).transpose(1, 0, 2, 3)
            y = lax.all_to_all(y.reshape(x.shape), ("frame", "tile"), 0, 0, tiled=True)
        else:
            y = lax.all_to_all(x, ("frame", "tile"), 0, 0, tiled=True)
            y = y.reshape(n_frame, n_tile, -1, width).transpose(1, 0, 2, 3)
        return y.reshape(rows, width)

    number = jnp.arange(rows, dtype=jnp.int32)
    of_frame, of_place = number // place, number % place
    seg_row = jnp.repeat(segments, place)
    open_row = jnp.repeat(frame_mask, place)
    allowed = (
        (seg_row[:, None] == seg_row[None, :])
        & (of_place[:, None] == of_place[None, :])
        & (of_frame[None, :] <= of_frame[:, None])
        & ((open_row[None, :] == 1) | (of_frame[None, :] == of_frame[:, None]))
    )
    bias = jnp.where(allowed, 0.0, -1e30).astype(F32)
    nothing = jnp.zeros((1, width), F32)
    vecs = [row(v) for v in (ln1_gain, ln1_shift, ln2_gain, ln2_shift, ln3_gain, ln3_shift, ffn_in_bias, ffn_out_bias)]
    one_hot = (action == jnp.arange(embed.shape[0], dtype=jnp.int32)).astype(F32)[:, None]
    if on_boxes:
        fwd = forward(mats, tokens, grad4, added, vecs, bias)
        fulls, kept = fwd[:6], fwd[6:]
        kept = (kept[12], kept[13], *kept[:12])
        hot = jnp.broadcast_to(one_hot, embed.shape)
        *summed, small, tokens_grad, result = backward(
            fulls, kept, added, (vecs[0], vecs[2], vecs[4]), bias, hot, tokens.shape, grad4.shape)
        summed = [x.astype(F32) for x in summed]
        n_act = embed.shape[0]
        d_embed, lines = small[:n_act], small[n_act:]
        dg1, ds1, dg2, ds2, dg3, ds3, d_bout = (lines[i] for i in range(7))
        d_bin = lines[7 : 7 + ffn_in_bias.shape[0] // width].reshape(-1)
    else:
        w_qs, w_os, w_qt, w_ot, w_in, w_out = (lax.all_gather(m, "frame", axis=0, tiled=True) for m in mats)
        base1 = lax.all_to_all(tokens, "tile", 0, 0, tiled=True).reshape(rows, width)
        g = lax.all_to_all(grad4.transpose(1, 0, 2, 3), "frame", 0, 0, tiled=True).reshape(rows, width)
        unit1, qkv1, mixed1, after1 = attn_fwd(
            base1, added, vecs[0], vecs[1], w_qs, w_os, None, BF16, "spatial_forward")
        base2 = turn(after1, True)
        unit2, qkv2, mixed2, after2 = attn_fwd(
            base2, nothing, vecs[2], vecs[3], w_qt, w_ot, bias, F32, "temporal_forward")
        unit3 = plain_norm(after2, ln3_gain, ln3_shift).astype(BF16)
        pre = jnp.dot(unit3, w_in, preferred_element_type=F32) + ffn_in_bias
        th = jnp.tanh(GELU_A * (pre + GELU_B * pre * pre * pre))
        act = (0.5 * pre * (1.0 + th)).astype(BF16)
        slope = 0.5 * (1.0 + th) + 0.5 * pre * (1.0 - th * th) * GELU_A * (1.0 + 3.0 * GELU_B * pre * pre)
        slope = slope.astype(BF16)
        result = after2 + jnp.dot(act, w_out, preferred_element_type=F32) + ffn_out_bias
        result = result.astype(BF16).reshape(n_frame, frames_dev, place, width)
        result = lax.all_to_all(result, "frame", 0, 0, tiled=True).transpose(1, 0, 2, 3)
        d_pre, d_after2, dg3, ds3, d_bin, d_bout = ffn_bwd(g, slope, after2, vecs[4], w_in, w_out)
        low2, d_qkv2, d_after1, dg2, ds2 = attn_bwd(
            base2, nothing, vecs[2], w_qt, w_ot, d_after2, qkv2, bias, BF16, "temporal_backward")
        d_out1 = turn(d_after1, False)
        low1, d_qkv1, d_start, dg1, ds1 = attn_bwd(
            base1, added, vecs[0], w_qs, w_os, d_out1, qkv1, None, F32, "spatial_backward")
        tokens_grad = d_start.astype(BF16).reshape(n_tile, tile_tokens, width)
        tokens_grad = lax.all_to_all(tokens_grad, "tile", 0, 0, tiled=True)
        d_embed = one_hot * jnp.sum(d_start, 0, keepdims=True)
        pairs = ((unit1, d_qkv1), (mixed1, low1), (unit2, d_qkv2), (mixed2, low2), (unit3, d_pre), (act, g))
        summed = []
        for a, b in pairs:
            part = lax.dot_general(a, b, (((0,), (0,)), ((), ())), preferred_element_type=F32)
            part = lax.psum_scatter(part, "frame", scatter_dimension=0, tiled=True)
            summed.append(lax.psum(part.astype(BF16), "tile").astype(F32))
        d_embed, dg1, ds1, dg2, ds2, dg3, ds3, d_bin, d_bout = lax.psum(
            (d_embed, dg1[0], ds1[0], dg2[0], ds2[0], dg3[0], ds3[0], d_bin[0], d_bout[0]), ("frame", "tile"))

    result = result.reshape(tokens.shape)
    return (result, tokens_grad, d_embed, dg1, ds1, summed[0], summed[1], dg2, ds2, summed[2], summed[3],
            dg3, ds3, summed[4], d_bin, summed[5], d_bout)


def solution(mesh):
    shard = P("frame", "tile", None)
    mat = P("frame", None)
    rep = P()
    in_specs = (shard, shard, P("frame"), rep, rep, rep, rep, rep, mat, mat, rep, rep, mat, mat,
                rep, rep, mat, rep, mat, rep)
    out_specs = (shard, shard, rep, rep, rep, mat, mat, rep, rep, mat, mat, rep, rep, mat, rep, mat, rep)
    on_boxes = mesh.shape["frame"] == 8 and mesh.shape["tile"] == 4
    return jax.shard_map(
        functools.partial(per_device, on_boxes),
        mesh=mesh, in_specs=in_specs, out_specs=out_specs, check_vma=False)
```

```python
import functools

import jax
import jax.numpy as jnp
from jax import lax
from jax.experimental import pallas as pl
from jax.experimental.pallas import tpu as pltpu
from jax.sharding import PartitionSpec as P

HD = 64
LANES = 128
EPS = 1e-5
MESH = pl.DeviceIdType.MESH
F32 = jnp.float32
BF16 = jnp.bfloat16
VMEM_SPEC = pl.BlockSpec(memory_space=pltpu.VMEM)
HBM_SPEC = pl.BlockSpec(memory_space=pltpu.HBM)


def params(**kw):
    return pltpu.CompilerParams(vmem_limit_bytes=60 * 1024 * 1024, **kw)


def at(j, size):
    return pl.ds(pl.multiple_of(j * size, size), size)


def each(n, fn):
    def step(i, carry):
        fn(i)
        return carry

    lax.fori_loop(0, n, step, 0)


def dot(a, b):
    return jnp.dot(a, b, preferred_element_type=F32)


def dot_nt(a, b):
    return lax.dot_general(a, b, (((1,), (1,)), ((), ())), preferred_element_type=F32)


def dot_tn(a, b):
    return lax.dot_general(a, b, (((0,), (0,)), ((), ())), preferred_element_type=F32)


def normed(h):
    cen = h - jnp.mean(h, -1, keepdims=True)
    inv = lax.rsqrt(jnp.mean(cen * cen, -1, keepdims=True) + EPS)
    return cen * inv, inv


ROWS = 32


def norm_rows(load, gain_ref, shift_ref, unit_ref):
    def step(i):
        rows = at(i, ROWS)
        xhat, _ = normed(load(rows))
        unit_ref[rows, :] = (xhat * gain_ref[...] + shift_ref[...]).astype(BF16)

    each(unit_ref.shape[0] // ROWS, step)


def fold(x):
    return jnp.sum(x.reshape(x.shape[0] // 8, 8, x.shape[1]), 0)


def norm_back(load, du_ref, gain_ref, dgain_ref, dshift_ref, acc_ref, store):
    acc_ref[...] = jnp.zeros_like(acc_ref)

    def step(i):
        rows = at(i, ROWS)
        xhat, inv = normed(load(rows))
        du = du_ref[rows, :]
        acc_ref[0] += fold(du * xhat)
        acc_ref[1] += fold(du)
        dx = du * gain_ref[...]
        dh = inv * (
            dx - jnp.mean(dx, -1, keepdims=True) - xhat * jnp.mean(dx * xhat, -1, keepdims=True)
        )
        store(rows, dh)

    each(du_ref.shape[0] // ROWS, step)
    dgain_ref[...] = jnp.sum(acc_ref[0], 0, keepdims=True)
    dshift_ref[...] = jnp.sum(acc_ref[1], 0, keepdims=True)


def head_masks():
    lane = lax.broadcasted_iota(jnp.int32, (1, LANES), 1)
    low = jnp.where(lane < HD, 1.0, 0.0)
    return low.astype(BF16), (1.0 - low).astype(BF16)


def head_probs(qm, k, bias_ref):
    s = dot_nt(qm, k) * (HD**-0.5)
    if bias_ref is not None:
        s = s + bias_ref[...]
    e = jnp.exp(s - jnp.max(s, -1, keepdims=True))
    return e * (1.0 / jnp.sum(e, -1, keepdims=True))


def attention(qkv_ref, bias_ref, mixed_ref):
    width = mixed_ref.shape[1]
    per = width // LANES
    masks = head_masks()

    def pair(p):
        q, k, v = (qkv_ref[:, at(p + i * per, LANES)] for i in range(3))
        out = 0.0
        for m in masks:
            out = out + dot(head_probs(q * m, k, bias_ref).astype(BF16), v * m)
        mixed_ref[:, at(p, LANES)] = out.astype(BF16)

    each(per, pair)


def attention_back(qkv_ref, bias_ref, dmix_ref, dqkv_ref):
    width = dmix_ref.shape[1]
    per = width // LANES
    masks = head_masks()
    scale = HD**-0.5

    def pair(p):
        q, k, v = (qkv_ref[:, at(p + i * per, LANES)] for i in range(3))
        dm = dmix_ref[:, at(p, LANES)]
        dq = dk = dv = 0.0
        for m in masks:
            qm = q * m
            dmm = dm * m
            probs = head_probs(qm, k, bias_ref)
            dp = dot_nt(dmm, v)
            ds = probs * (dp - jnp.sum(probs * dp, -1, keepdims=True))
            ds = ds.astype(BF16)
            dq = dq + dot(ds, k * m)
            dk = dk + dot_tn(ds, qm)
            dv = dv + dot_tn(probs.astype(BF16), dmm)
        dqkv_ref[:, at(p, LANES)] = (dq * scale).astype(BF16)
        dqkv_ref[:, at(p + per, LANES)] = (dk * scale).astype(BF16)
        dqkv_ref[:, at(p + 2 * per, LANES)] = dv.astype(BF16)

    each(per, pair)


def matmul(x_ref, w_ref, block, store):
    def step(j):
        cols = at(j, block)
        store(cols, dot(x_ref[...], w_ref[:, cols]))

    each(w_ref.shape[1] // block, step)


def matmul_nt(x_ref, w_ref, block, store):
    def step(j):
        rows = at(j, block)
        store(rows, dot_nt(x_ref[...], w_ref[rows, :]))

    each(w_ref.shape[0] // block, step)


def wgrad(core, shard, left, left_x, right, right_x, out, lt):
    tok = left.shape[0]
    col_blocks = right.shape[1] // TILE
    for rb in range(shard // 128):
        for q in range(4):
            cols = pl.ds(pl.multiple_of((2 * q + core) * shard + rb * 128, 128), 128)
            lt[q * 128 : (q + 1) * 128, :tok] = left[:, cols].T
            cols = pl.ds(q * shard + rb * 128, 128)
            lt[q * 128 : (q + 1) * 128, tok:] = left_x[:, cols].T

        def step(j, rb=rb):
            cols = at(j, 512)
            y = dot(lt[:, :tok], right[:, cols]) + dot(lt[:, tok:], right_x[:, cols])
            y = y.astype(BF16)
            unit = rb * col_blocks + j // 2
            half = pl.ds(pl.multiple_of(lax.rem(j, 2) * 512, 512), 512)
            for q in range(4):
                out[unit, q, :, half] = y[q * 128 : (q + 1) * 128]

        each(2 * col_blocks, step)


GELU_A = 0.7978845608
GELU_B = 0.044715


def xor(a, b):
    bit = lax.rem(a // b, 2)
    return a + b - 2 * b * bit


def greet(partners):
    barrier = pltpu.get_barrier_semaphore()
    for p in partners:
        pl.semaphore_signal(barrier, inc=1, device_id=p, device_id_type=MESH)
    pl.semaphore_wait(barrier, len(partners))


def remote(src, dst, ssem, rsem, dev):
    return pltpu.make_async_remote_copy(
        src_ref=src, dst_ref=dst, send_sem=ssem, recv_sem=rsem, device_id=dev, device_id_type=MESH
    )


def xor_any(a, bits):
    for b in (1, 2, 4, 8, 16):
        if bits & b:
            a = xor(a, b)
    return a


TILE = 1024
SLOTS = 4
AHEAD = 3
DEEP = 3
RING = 6


def gather_chunks(shapes):
    out = []
    for i, (rows, cols) in enumerate(shapes):
        step = rows
        while step * cols > 128 * 1024 and step % 32 == 0:
            step //= 2
        out += [(i, r, step) for r in range(0, rows, step)]
    return out


def weight_tiles(shapes):
    return [
        (i, r, c)
        for i, (rows, cols) in enumerate(shapes)
        for r in range(0, rows, TILE)
        for c in range(0, cols, TILE)
    ]


def add_into(dst, a, b):
    def step(i):
        r = at(i, 16)
        dst[r, :] = (a[r, :].astype(F32) + b[r, :].astype(F32)).astype(dst.dtype)

    each(dst.shape[0] // 16, step)


def layer_kernel(chunks, tiles, units, *refs):
    shards = refs[:6]
    (tokens, grad4, actions, segments, frame_mask, embed,
     gain1, shift1, gain2, shift2, gain3, shift3, b_in, b_out) = refs[6:20]
    full = refs[20:26]
    outs = refs[26:32]
    small_out, tokens_grad, result = refs[32:35]
    (base1, unit1, qkv1, mixed1, base2, unit2, qkv2, mixed2, after2, unit3, slope, g2d, act,
     wt, gbuf, r1, r2, zin, zpeer, act_x, g_x, dpre_x, unit3_x, mix2_x, low2_x, unit2_x, dqkv2_x,
     mix1_x, low1_x, unit1_x, dqkv1_x, du, low2, low1, dmix, dqkv,
     out1, in2, g_in, res_out, turn_out, turn_in, bias, added, sm, smr, lt, acc, emb,
     ssem, rsem, bsem, tsem, z3s, z3r, z3l, f7s, f7r, f7l, turn_s, turn_r, turn_l, back_s, back_r, back_l,
     s1s, s1r, s2s, s2r, zs, zr, zps, zpr, osem, sms, smrs, xs, xr, o7s, o7r, o7l, t3s, t3r, t3l) = refs[35:]
    f = lax.axis_index("frame")
    t = lax.axis_index("tile")
    core = lax.rem(f, 2)
    chip = f // 2
    odd = lax.rem(t, 2)
    leaf = (t == 0) | (t == 3)
    inner = jnp.logical_not(leaf)
    fx, fy, sib = xor(f, 2), xor(f, 4), xor(f, 1)
    first = fx + (fy - fx) * odd
    second = fy + (fx - fy) * odd
    diag = xor_any(f, 6)
    cx, cy, cd = xor(chip, 1), xor(chip, 2), xor_any(chip, 3)
    to_sib, to_first, to_second = (sib, t), (first, t), (second, t)
    to_x, to_y, to_z, to_peer = (fx, t), (fy, t), (f, xor(t, 1)), (f, 3 - t)
    others = [(a, b) for a in range(8) for b in range(4) if a or b]
    greet([(xor_any(f, a), xor_any(t, b)) for a, b in others])

    def piece(k, owner):
        a, r, rows = chunks[k]
        return full[a].at[pl.ds(pl.multiple_of(owner * shards[a].shape[0] + r, 16), rows)]

    def own(k):
        a, r, rows = chunks[k]
        return shards[a].at[pl.ds(r, rows)]

    def copy(k, kind):
        dev = (to_first, to_second, to_z, to_sib, to_sib, to_sib, to_sib)[kind]
        owner = (f, first, first, f, first, diag, second)[kind]
        src = own(k) if kind in (0, 3) else piece(k, owner)
        return remote(src, piece(k, owner), ssem.at[k, kind], rsem.at[k, kind], dev)

    def arrived(k, kind):
        owner = (first, diag, second, sib, xor(first, 1), xor(diag, 1), xor(second, 1))[kind]
        dst = piece(k, owner)
        remote(dst, dst, ssem.at[k, kind], rsem.at[k, kind], to_sib).wait_recv()

    n_chunks = len(chunks)
    progress = [0, 0]

    def relay():
        k = progress[1]
        progress[1] += 1
        for kind in (1, 2):
            arrived(k, kind)
            copy(k, kind + 4).start()

    def advance(hops):
        while progress[0] < min(hops, n_chunks):
            k = progress[0]
            progress[0] += 1
            copy(k, 3).start()
            arrived(k, 0)
            if k + AHEAD < n_chunks:
                copy(k + AHEAD, 0).start()
            for kind in (1, 2, 4):
                copy(k, kind).start()
            if k >= 1:
                relay()
        if hops > n_chunks and progress[1] < n_chunks:
            relay()

    def complete(a):
        ks = [k for k in range(n_chunks) if chunks[k][0] == a]
        advance(ks[-1] + 2)
        for k in ks:
            for kind in (3, 4, 5, 6):
                arrived(k, kind)

    bounce = []
    for a, shard in enumerate(shards):
        for r in range(0, shard.shape[0], 128):
            for c in range(0, shard.shape[1], TILE):
                i = len(bounce)
                bounce.append((a, r, c, wt.at[2 + i // 8, pl.ds(i % 8 * 128, 128)]))

    def bounce_in(i):
        a, r, c, via = bounce[i]
        return pltpu.make_async_copy(shards[a].at[pl.ds(r, 128), pl.ds(c, TILE)], via, bsem.at[i])

    def bounce_out(i):
        a, r, c, via = bounce[i]
        row = pl.multiple_of(f * shards[a].shape[0] + r, 128)
        return pltpu.make_async_copy(via, full[a].at[pl.ds(row, 128), pl.ds(c, TILE)], bsem.at[i])

    def tile_load(i):
        a, r, c = tiles[i]
        src = full[a].at[pl.ds(r, TILE), pl.ds(c, TILE)]
        return pltpu.make_async_copy(src, wt.at[i % SLOTS], tsem.at[i])

    def load(ids):
        for i in ids:
            if i < len(tiles):
                tile_load(i).start()

    n = len(units)

    def hop(u):
        return (to_x, cx, to_y, cy) if u % 2 == 0 else (to_y, cy, to_x, cx)

    def part(u, p):
        return gbuf.at[u // 4 % 3, u % 4, p]

    def step1(u):
        dev1, p1, _, _ = hop(u)
        k = u % RING
        return (
            remote(part(u, cd), r1.at[k, 1], s1s.at[u, 1], s1r.at[u, 1], dev1),
            remote(part(u, p1), r1.at[k, 0], s1s.at[u, 0], s1r.at[u, 0], dev1),
        )

    def step2(u):
        _, _, dev2, p2 = hop(u)
        return remote(part(u, p2), r2.at[u % RING], s2s.at[u], s2r.at[u], dev2)

    def along(u):
        return remote(part(u, chip), zin.at[u % RING], zs.at[u], zr.at[u], to_z)

    def across(u):
        return remote(part(u, chip), zpeer.at[u % RING], zps.at[u], zpr.at[u], to_peer)

    def emit(u, src):
        a, r, c = units[u]
        return pltpu.make_async_copy(src, outs[a].at[pl.ds(r, 128), pl.ds(c, TILE)], osem.at[u])

    state = {"ready": 0, "issued": 0, "done": 0, "step": 0}

    def issue():
        while state["issued"] < min(state["ready"], state["done"] + DEEP):
            for c in step1(state["issued"]):
                c.start()
            state["issued"] += 1

    def offer(count):
        state["ready"] += count
        issue()

    def reduce_step():
        s = state["step"]
        state["step"] += 1
        u = s
        if u < n:
            assert u < state["issued"]
            p2 = hop(u)[3]
            far, near = step1(u)
            far.wait_recv()
            add_into(part(u, p2), part(u, p2), r1.at[u % RING, 1])
            step2(u).start()
            near.wait_recv()
            add_into(part(u, chip), part(u, chip), r1.at[u % RING, 0])
            state["done"] += 1
            issue()
        u = s - 1
        if 0 <= u < n:
            step2(u).wait_recv()
            add_into(part(u, chip), part(u, chip), r2.at[u % RING])

            @pl.when(leaf)
            def _(u=u):
                along(u).start()

        u = s - 2
        if 0 <= u < n:
            @pl.when(inner)
            def _(u=u):
                along(u).wait_recv()
                add_into(part(u, chip), part(u, chip), zin.at[u % RING])
                across(u).start()

        u = s - 3
        if 0 <= u < n:
            @pl.when(inner)
            def _(u=u):
                across(u).wait()
                add_into(part(u, chip), part(u, chip), zpeer.at[u % RING])
                along(u).start()
                emit(u, part(u, chip)).start()

        u = s - 4
        if 0 <= u < n:
            @pl.when(leaf)
            def _(u=u):
                along(u).wait()
                emit(u, zin.at[u % RING]).start()

        u = s - 5
        if 0 <= u < n:
            for c in step1(u):
                c.wait_send()
            step2(u).wait_send()

            @pl.when(inner)
            def _(u=u):
                along(u).wait_send()

            emit(u, part(u, chip)).wait()

    def reduce_to(s):
        while state["step"] < s:
            reduce_step()

    def share(i, left, left_x, right, right_x):
        shard = left.shape[1] // 8
        copies = [
            remote(left.at[:, pl.ds(pl.multiple_of((2 * p + 1 - core) * shard, shard), shard)],
                   left_x.at[:, pl.ds(p * shard, shard)], xs.at[i, p], xr.at[i, p], to_sib)
            for p in range(4)
        ]
        copies.append(remote(right, right_x, xs.at[i, 4], xr.at[i, 4], to_sib))
        for c in copies:
            c.start()
        return copies

    def wait_all(copies):
        for c in copies:
            c.wait()

    def rows_of(ref, i):
        return ref.at[pl.ds(pl.multiple_of(i * 64, 64), 64)]

    def over_tile(src, dst, ssems, rsems, lsem):
        ds = [xor_any(t, i) for i in (1, 2, 3)]
        own = pltpu.make_async_copy(src(t), dst(t), lsem)
        go = [remote(src(d), dst(t), ssems.at[i], rsems.at[i], (f, d)) for i, d in enumerate(ds)]
        end = [remote(src(d), dst(d), ssems.at[i], rsems.at[i], (f, d)) for i, d in enumerate(ds)]
        return [own] + go, [own] + end

    def over_frame(src, dst, ssems, rsems, lsem):
        ds = [xor_any(f, i) for i in range(1, 8)]
        own = pltpu.make_async_copy(src(f), dst(f), lsem)
        go = [remote(src(d), dst(f), ssems.at[i], rsems.at[i], (d, t)) for i, d in enumerate(ds)]
        end = [remote(src(d), dst(d), ssems.at[i], rsems.at[i], (d, t)) for i, d in enumerate(ds)]
        return [own] + go, [own] + end

    def over_both(src, dst, ssems, rsems, lsem):
        ds = [(xor_any(f, a), xor_any(t, b)) for a, b in others]
        own = pltpu.make_async_copy(src(f, t), dst(f, t), lsem)
        go = [remote(src(*d), dst(f, t), ssems.at[i], rsems.at[i], d) for i, d in enumerate(ds)]
        end = [remote(src(*d), dst(*d), ssems.at[i], rsems.at[i], d) for i, d in enumerate(ds)]
        return [own] + go, [own] + end

    def start_all(copies):
        for c in copies:
            c.start()

    def split(load_rows, dst):
        def step(i):
            dst[pl.ds(4 * i, 4)] = load_rows(at(i, ROWS)).reshape(4, 8, TILE).astype(BF16)

        each(dst.shape[0] // 4, step)

    def join(src, dst):
        def step(i):
            dst[at(i, ROWS), :] = src[pl.ds(4 * i, 4)].astype(F32).reshape(ROWS, TILE).astype(BF16)

        each(src.shape[0] // 4, step)

    tok_go, tok_end = over_tile(lambda d: tokens.at[d], lambda d: rows_of(base1, d), z3s, z3r, z3l)
    start_all(tok_go)
    for k in range(AHEAD):
        copy(k, 0).start()
    for i in range(len(bounce)):
        bounce_in(i).start()
    grad_go, grad_end = over_frame(
        lambda d: grad4.at[:, d], lambda d: g_in.at[pl.ds(4 * d, 4)], f7s, f7r, f7l)

    which = jnp.sum(jnp.where(lax.broadcasted_iota(jnp.int32, (1, 4), 1) == t, actions[...], 0), -1, keepdims=True)
    hot = jnp.where(lax.broadcasted_iota(jnp.int32, (8, 1), 0) == which, 1.0, 0.0)
    added[...] = jnp.sum(hot * embed[...], 0, keepdims=True)
    n_frames = segments.shape[1]
    n_rows = bias.shape[0]
    place = n_rows // n_frames

    def column(ref):
        a = lax.broadcasted_iota(jnp.int32, (n_frames, n_frames), 0)
        b = lax.broadcasted_iota(jnp.int32, (n_frames, n_frames), 1)
        return jnp.sum(jnp.where(a == b, ref[...].astype(F32), 0.0), 1, keepdims=True)

    by_row = lax.broadcasted_iota(jnp.int32, (n_rows, n_frames), 0) // place
    by_row = by_row == lax.broadcasted_iota(jnp.int32, (n_rows, n_frames), 1)
    by_col = lax.broadcasted_iota(jnp.int32, (n_frames, n_rows), 1) // place
    by_col = by_col == lax.broadcasted_iota(jnp.int32, (n_frames, n_rows), 0)
    seg_q = jnp.sum(jnp.where(by_row, segments[...].astype(F32), 0.0), 1, keepdims=True)
    seg_k = jnp.sum(jnp.where(by_col, column(segments), 0.0), 0, keepdims=True)
    open_k = jnp.sum(jnp.where(by_col, column(frame_mask), 0.0), 0, keepdims=True)
    row_q = lax.broadcasted_iota(jnp.int32, (n_rows, n_rows), 0)
    row_k = lax.broadcasted_iota(jnp.int32, (n_rows, n_rows), 1)
    allowed = (
        (seg_q == seg_k)
        & (lax.rem(row_q, place) == lax.rem(row_k, place))
        & (row_k // place <= row_q // place)
        & ((open_k == 1.0) | (row_k == row_q))
    )
    bias[...] = jnp.where(allowed, 0.0, -1e30)

    advance(1)
    for i in range(len(bounce)):
        bounce_in(i).wait()
        bounce_out(i).start()
    wait_all(tok_end)
    norm_rows(lambda rows: base1[rows, :].astype(F32) + added[...], gain1, shift1, unit1)
    start_all(grad_go)
    for i in range(len(bounce)):
        bounce_out(i).wait()

    def project(unit, ids, out_ref):
        for j, i in enumerate(ids):
            tile_load(i).wait()

            def put(cols, y, j=j):
                start = pl.multiple_of(cols.start + j * TILE, 512)
                out_ref[:, pl.ds(start, 512)] = y.astype(BF16)

            matmul(unit, wt.at[i % SLOTS], 512, put)

    complete(0)
    load((0, 1, 2))
    project(unit1, (0, 1, 2), qkv1)
    complete(1)
    load((3,))
    attention(qkv1, None, mixed1)
    tile_load(3).wait()

    def put_after1(cols, y):
        du[:, cols] = y + base1[:, cols].astype(F32) + added[:, cols]

    matmul(mixed1, wt.at[3], 512, put_after1)
    split(lambda rows: du[rows, :], out1)

    turn_go, turn_end = over_both(
        lambda a, b: out1.at[8 * b + a], lambda a, b: in2.at[4 * a + b], turn_s, turn_r, turn_l)
    start_all(turn_go)
    complete(2)
    load((4, 5, 6))
    complete(3)
    load((7,))
    wait_all(turn_end)
    join(in2, base2)
    norm_rows(lambda rows: base2[rows, :].astype(F32), gain2, shift2, unit2)
    project(unit2, (4, 5, 6), qkv2)
    advance(12)
    attention(qkv2, bias, mixed2)
    advance(14)
    tile_load(7).wait()

    def put_after2(cols, y):
        after2[:, cols] = y + base2[:, cols].astype(F32)

    matmul(mixed2, wt.at[3], 512, put_after2)
    norm_rows(lambda rows: after2[rows, :], gain3, shift3, unit3)
    complete(4)
    load((8, 9, 10, 11))
    wait_all(grad_end)
    join(g_in, g2d)

    for j in range(4):
        tile_load(8 + j).wait()

        def put_pre(cols, y, j=j):
            cols = pl.ds(pl.multiple_of(cols.start + j * TILE, 256), 256)
            v = y + b_in[:, cols]
            th = jnp.tanh(GELU_A * (v + GELU_B * v * v * v))
            act[:, cols] = (0.5 * v * (1.0 + th)).astype(BF16)
            rise = 0.5 * (1.0 + th) + 0.5 * v * (1.0 - th * th) * GELU_A * (1.0 + 3.0 * GELU_B * v * v)
            slope[:, cols] = rise.astype(BF16)

        matmul(unit3, wt.at[j], 256, put_pre)

    swap4 = share(0, act, act_x, g2d, g_x)
    advance(16)
    wait_all(swap4)
    wgrad(core, act.shape[1] // 8, act, act_x, g2d, g_x, gbuf.at[0], lt)
    complete(5)
    load((12, 13, 14, 15))
    offer(4)

    sm[0] = jnp.zeros_like(sm[0])
    for j in range(4):
        tile_load(12 + j).wait()

        def put_dpre(rows, y, j=j):
            cols = pl.ds(pl.multiple_of(rows.start + j * TILE, 256), 256)
            d = (y * slope[:, cols].astype(F32)).astype(BF16)
            slope[:, cols] = d
            sm[0, 15 + j : 16 + j, rows] = jnp.sum(d.astype(F32), 0, keepdims=True)

        matmul_nt(g2d, wt.at[j], 256, put_dpre)

        def add_up(h, j=j):
            cols = at(h, 512)
            y = dot(act[:, j * TILE : (j + 1) * TILE], wt[j, :, cols])
            du[:, cols] = y + (after2[:, cols] + b_out[:, cols] if j == 0 else du[:, cols])

        each(2, add_up)
        load((16 + j,))
    dpre = slope
    swap3 = share(1, unit3, unit3_x, dpre, dpre_x)
    split(lambda rows: du[rows, :], res_out)
    res_go, res_end = over_frame(
        lambda d: res_out.at[pl.ds(4 * d, 4)], lambda d: result.at[:, d], o7s, o7r, o7l)
    reduce_to(1)

    def back_through(first_tile, count, x_ref):
        for j in range(count):
            i = first_tile + j
            tile_load(i).wait()

            def run(h, i=i, j=j):
                rows = at(h, 256)
                y = dot_nt(x_ref[:, j * TILE : (j + 1) * TILE], wt[i % SLOTS, rows, :])
                du[:, rows] = y if j == 0 else du[:, rows] + y

            each(TILE // 256, run)
            load((i + SLOTS,))

    back_through(16, 4, dpre)

    def store3(rows, dh):
        g = g2d[rows, :].astype(F32)
        d = g + dh
        after2[rows, :] = d
        low2[rows, :] = d.astype(BF16)
        sm[0, 14:15, :] += jnp.sum(g, 0, keepdims=True)

    norm_back(lambda rows: after2[rows, :], du, gain3, sm.at[0, pl.ds(12, 1)], sm.at[0, pl.ds(13, 1)], acc, store3)
    dafter = after2
    swap2o = share(2, mixed2, mix2_x, low2, low2_x)
    reduce_to(2)
    wait_all(swap3)
    wgrad(core, TILE // 8, unit3, unit3_x, dpre, dpre_x, gbuf.at[1], lt)
    offer(4)

    def put_mix(rows, y):
        dmix[:, rows] = y.astype(BF16)

    tile_load(20).wait()
    matmul_nt(low2, wt.at[0], 512, put_mix)
    load((24,))
    reduce_to(3)
    attention_back(qkv2, bias, dmix, dqkv)
    swap2 = share(3, unit2, unit2_x, dqkv, dqkv2_x)
    reduce_to(4)
    back_through(21, 3, dqkv)

    def store2(rows, dh):
        dafter[rows, :] = dafter[rows, :] + dh

    norm_back(lambda rows: base2[rows, :].astype(F32), du, gain2, sm.at[0, pl.ds(10, 1)], sm.at[0, pl.ds(11, 1)], acc, store2)
    split(lambda rows: dafter[rows, :], turn_out)

    back_go, back_end = over_both(
        lambda a, b: turn_out.at[4 * a + b], lambda a, b: turn_in.at[8 * b + a], back_s, back_r, back_l)
    start_all(back_go)
    wait_all(swap2o)
    wgrad(core, TILE // 8, mixed2, mix2_x, low2, low2_x, gbuf.at[2, pl.ds(0, 1)], lt)
    wait_all(swap2)
    wgrad(core, TILE // 8, unit2, unit2_x, dqkv, dqkv2_x, gbuf.at[2, pl.ds(1, 3)], lt)
    offer(4)
    reduce_to(5)
    wait_all(back_end)
    join(turn_in, low1)
    swap1o = share(4, mixed1, mix1_x, low1, low1_x)
    tile_load(24).wait()
    matmul_nt(low1, wt.at[0], 512, put_mix)
    reduce_to(6)
    attention_back(qkv1, None, dmix, dqkv)
    swap1 = share(5, unit1, unit1_x, dqkv, dqkv1_x)
    wait_all(swap1o)
    wgrad(core, TILE // 8, mixed1, mix1_x, low1, low1_x, gbuf.at[0, pl.ds(0, 1)], lt)
    offer(1)
    reduce_to(7)
    back_through(25, 3, dqkv)
    reduce_to(9)
    wait_all(swap1)
    wgrad(core, TILE // 8, unit1, unit1_x, dqkv, dqkv1_x, gbuf.at[0, pl.ds(1, 3)], lt)
    offer(3)
    emb[...] = jnp.zeros_like(emb)

    def store1(rows, dh):
        d = low1[rows, :].astype(F32) + dh
        low2[rows, :] = d.astype(BF16)
        emb[...] += fold(d)

    norm_back(lambda rows: base1[rows, :].astype(F32) + added[...], du, gain1, sm.at[0, pl.ds(8, 1)], sm.at[0, pl.ds(9, 1)], acc, store1)
    sm[0, 0:8, :] = hot * jnp.sum(emb[...], 0, keepdims=True)

    last_go, last_end = over_tile(lambda d: rows_of(low2, d), lambda d: tokens_grad.at[d], t3s, t3r, t3l)
    start_all(last_go)

    def small_copy(i, dev):
        return remote(sm.at[i], smr.at[i], sms.at[i], smrs.at[i], dev)

    def small_down():
        return remote(sm.at[5], smr.at[3], sms.at[5], smrs.at[3], to_z)

    hops = (to_sib, to_x, to_y)
    small_copy(0, to_sib).start()
    for i in range(3):
        reduce_to(state["step"] + 1)
        small_copy(i, hops[i]).wait()
        sm[i + 1] = sm[i] + smr[i]
        if i < 2:
            small_copy(i + 1, hops[i + 1]).start()

    @pl.when(leaf)
    def _():
        small_copy(3, to_z).start()

    reduce_to(state["step"] + 1)

    @pl.when(inner)
    def _():
        small_copy(3, to_z).wait_recv()
        sm[4] = sm[3] + smr[3]
        small_copy(4, to_peer).start()

    start_all(res_go)
    reduce_to(state["step"] + 1)

    @pl.when(inner)
    def _():
        small_copy(4, to_peer).wait()
        sm[5] = sm[4] + smr[4]
        small_down().start()
        small_out[...] = sm[5]

    reduce_to(n + 5)

    @pl.when(leaf)
    def _():
        small_copy(3, to_z).wait()
        small_out[...] = smr[3]

    @pl.when(inner)
    def _():
        small_down().wait_send()

    wait_all(last_end)
    wait_all(res_end)
    for k in range(n_chunks):
        for kind in range(7):
            copy(k, kind).wait_send()


def layer(mats, tokens, grad4, actions, segments, frame_mask, embed, vecs):
    width = tokens.shape[2]
    rows = tokens.shape[0] * tokens.shape[1]
    ff = mats[4].shape[1]
    fulls = [(8 * m.shape[0], m.shape[1]) for m in mats]
    chunks = gather_chunks([m.shape for m in mats])
    by_mat = weight_tiles(fulls)
    order = (5, 4, 3, 2, 1, 0)
    tiles = by_mat + [x for a in order[1:] for x in by_mat if x[0] == a]
    units = [
        (a, r, c) for a in order
        for r in range(0, mats[a].shape[0], 128) for c in range(0, mats[a].shape[1], TILE)
    ]
    n = len(units)
    n_chunks = len(chunks)
    dma = pltpu.SemaphoreType.DMA
    blocks = (32, 8, width)
    unit = (128, TILE)
    bf = lambda *s: pltpu.VMEM(s, BF16)
    fl = lambda *s: pltpu.VMEM(s, F32)
    half = width // 2
    scratch = [
        bf(rows, width), bf(rows, width), bf(rows, 3 * width), bf(rows, width),
        bf(rows, width), bf(rows, width), bf(rows, 3 * width), bf(rows, width),
        fl(rows, width), bf(rows, width), bf(rows, ff), bf(rows, width), bf(rows, ff),
        bf(SLOTS, TILE, TILE), bf(3, 4, 4, *unit), bf(RING, 2, *unit), bf(RING, *unit),
        bf(RING, *unit), bf(RING, *unit),
        bf(rows, ff // 2), bf(rows, width), bf(rows, ff), bf(rows, half),
        bf(rows, half), bf(rows, width), bf(rows, half), bf(rows, 3 * width),
        bf(rows, half), bf(rows, width), bf(rows, half), bf(rows, 3 * width),
        fl(rows, width), bf(rows, width), bf(rows, width), bf(rows, width), bf(rows, 3 * width),
        bf(*blocks), bf(*blocks), bf(*blocks), bf(*blocks), bf(*blocks), bf(*blocks),
        fl(rows, rows), fl(1, width),
        fl(6, 24, width), fl(5, 24, width), bf(512, 2 * rows), fl(2, 8, width), fl(8, width),
    ]
    sems = [
        (n_chunks, 7), (n_chunks, 7), (16,), (len(tiles),), (3,), (3,), (), (7,), (7,), (),
        (31,), (31,), (), (31,), (31,), (),
        (n, 2), (n, 2), (n,), (n,), (n,), (n,), (n,), (n,), (n,), (6,), (6,), (6, 5), (6, 5),
        (7,), (7,), (), (3,), (3,), (),
    ]
    return pl.pallas_call(
        functools.partial(layer_kernel, chunks, tiles, units),
        out_shape=[jax.ShapeDtypeStruct(s, BF16) for s in fulls]
        + [jax.ShapeDtypeStruct(m.shape, BF16) for m in mats]
        + [
            jax.ShapeDtypeStruct((24, width), F32),
            jax.ShapeDtypeStruct(tokens.shape, BF16),
            jax.ShapeDtypeStruct(grad4.shape, BF16),
        ],
        in_specs=[HBM_SPEC] * 8 + [VMEM_SPEC] * (4 + len(vecs)),
        out_specs=[HBM_SPEC] * 12 + [VMEM_SPEC] + [HBM_SPEC] * 2,
        scratch_shapes=scratch + [dma(s) if s else dma for s in sems],
        compiler_params=params(collective_id=0, has_side_effects=True),
        name="layer",
    )(*mats, tokens, grad4, actions, segments, frame_mask, embed, *vecs)


def plain_norm(h, gain, shift):
    cen = h - jnp.mean(h, -1, keepdims=True)
    inv = lax.rsqrt(jnp.mean(cen * cen, -1, keepdims=True) + EPS)
    return cen * inv * gain + shift


def attn_fwd_kernel(masked, base_ref, added_ref, gain_ref, shift_ref, wqkv_ref, wo_ref, *rest):
    if masked:
        bias_ref, unit_ref, qkv_ref, mixed_ref, after_ref = rest
    else:
        bias_ref = None
        unit_ref, qkv_ref, mixed_ref, after_ref = rest

    def load(rows):
        return base_ref[rows, :].astype(F32) + added_ref[...]

    norm_rows(load, gain_ref, shift_ref, unit_ref)

    def put_qkv(cols, y):
        qkv_ref[:, cols] = y.astype(BF16)

    matmul(unit_ref, wqkv_ref, 512, put_qkv)
    attention(qkv_ref, bias_ref, mixed_ref)

    def put_after(cols, y):
        y = y + base_ref[:, cols].astype(F32) + added_ref[:, cols]
        after_ref[:, cols] = y.astype(after_ref.dtype)

    matmul(mixed_ref, wo_ref, 512, put_after)


def attn_fwd(base, added, gain, shift, wqkv, wo, bias, out_type, name):
    rows, width = base.shape
    ins = [base, added, gain, shift, wqkv, wo] + ([bias] if bias is not None else [])
    shapes = [(width, BF16), (3 * width, BF16), (width, BF16), (width, out_type)]
    return pl.pallas_call(
        functools.partial(attn_fwd_kernel, bias is not None),
        out_shape=[jax.ShapeDtypeStruct((rows, w), d) for w, d in shapes],
        in_specs=[VMEM_SPEC] * len(ins),
        out_specs=[VMEM_SPEC] * 4,
        compiler_params=params(),
        name=name,
    )(*ins)


def attn_bwd_kernel(masked, base_ref, added_ref, gain_ref, wqkv_ref, wo_ref, dout_ref, qkv_ref, *rest):
    if masked:
        bias_ref, *rest = rest
    else:
        bias_ref = None
    dlow_ref, dqkv_ref, dbase_ref, dgain_ref, dshift_ref, dmix_ref, du_ref, acc_ref = rest

    def cast(i):
        rows = at(i, ROWS)
        dlow_ref[rows, :] = dout_ref[rows, :].astype(BF16)

    each(dlow_ref.shape[0] // ROWS, cast)

    def put_mix(rows, y):
        dmix_ref[:, rows] = y.astype(BF16)

    matmul_nt(dlow_ref, wo_ref, 512, put_mix)
    attention_back(qkv_ref, bias_ref, dmix_ref, dqkv_ref)

    def put_du(rows, y):
        du_ref[:, rows] = y

    matmul_nt(dqkv_ref, wqkv_ref, 256, put_du)

    def load(rows):
        return base_ref[rows, :].astype(F32) + added_ref[...]

    def store(rows, dh):
        dbase_ref[rows, :] = (dout_ref[rows, :].astype(F32) + dh).astype(dbase_ref.dtype)

    norm_back(load, du_ref, gain_ref, dgain_ref, dshift_ref, acc_ref, store)


def attn_bwd(base, added, gain, wqkv, wo, dout, qkv, bias, out_type, name):
    rows, width = base.shape
    ins = [base, added, gain, wqkv, wo, dout, qkv] + ([bias] if bias is not None else [])
    outs = [
        jax.ShapeDtypeStruct((rows, width), BF16),
        jax.ShapeDtypeStruct((rows, 3 * width), BF16),
        jax.ShapeDtypeStruct((rows, width), out_type),
        jax.ShapeDtypeStruct((1, width), F32),
        jax.ShapeDtypeStruct((1, width), F32),
    ]
    return pl.pallas_call(
        functools.partial(attn_bwd_kernel, bias is not None),
        out_shape=outs,
        in_specs=[VMEM_SPEC] * len(ins),
        out_specs=[VMEM_SPEC] * len(outs),
        scratch_shapes=[
            pltpu.VMEM((rows, width), BF16),
            pltpu.VMEM((rows, width), F32),
            pltpu.VMEM((2, 8, width), F32),
        ],
        compiler_params=params(),
        name=name,
    )(*ins)


def ffn_bwd_kernel(g_ref, slope_ref, after_ref, gain_ref, win_ref, wout_ref,
                   dslope_ref, dafter_ref, dgain_ref, dshift_ref, dbin_ref, dbout_ref, du_ref, acc_ref):
    def put_dpre(rows, y):
        d = (y * slope_ref[:, rows].astype(F32)).astype(BF16)
        dslope_ref[:, rows] = d
        dbin_ref[:, rows] = jnp.sum(d.astype(F32), 0, keepdims=True)

    matmul_nt(g_ref, wout_ref, 512, put_dpre)

    def put_du(rows, y):
        du_ref[:, rows] = y

    matmul_nt(dslope_ref, win_ref, 256, put_du)
    dbout_ref[...] = jnp.zeros_like(dbout_ref)

    def store(rows, dh):
        g = g_ref[rows, :].astype(F32)
        dafter_ref[rows, :] = g + dh
        dbout_ref[...] += jnp.sum(g, 0, keepdims=True)

    norm_back(lambda rows: after_ref[rows, :], du_ref, gain_ref, dgain_ref, dshift_ref, acc_ref, store)


def ffn_bwd(g, slope, after, gain, win, wout):
    rows, width = after.shape
    ff = win.shape[1]
    row = lambda n: jax.ShapeDtypeStruct((1, n), F32)
    return pl.pallas_call(
        ffn_bwd_kernel,
        out_shape=[
            jax.ShapeDtypeStruct((rows, ff), BF16),
            jax.ShapeDtypeStruct((rows, width), F32),
            row(width), row(width), row(ff), row(width),
        ],
        in_specs=[VMEM_SPEC] * 6,
        out_specs=[VMEM_SPEC] * 6,
        scratch_shapes=[pltpu.VMEM((rows, width), F32), pltpu.VMEM((2, 8, width), F32)],
        compiler_params=params(),
        name="ffn_backward",
    )(g, slope, after, gain, win, wout)


def per_device(on_boxes, tokens, out_grad, actions, segments, frame_mask, embed,
               ln1_gain, ln1_shift, spatial_qkv, spatial_out,
               ln2_gain, ln2_shift, temporal_qkv, temporal_out,
               ln3_gain, ln3_shift, ffn_in, ffn_in_bias, ffn_out, ffn_out_bias):
    frames_dev, tile_tokens, width = tokens.shape
    n_frame = lax.axis_size("frame")
    n_tile = lax.axis_size("tile")
    f = lax.axis_index("frame")
    t = lax.axis_index("tile")
    frames = frames_dev * n_frame
    place = tile_tokens // n_frame
    rows = frames_dev * tile_tokens
    row = lambda v: v[None, :]

    mats = (spatial_qkv, spatial_out, temporal_qkv, temporal_out, ffn_in, ffn_out)

    grad4 = out_grad.reshape(frames_dev, n_frame, place, width)
    blocks = n_frame * n_tile

    def turn(x, forward):
        x = x.reshape(blocks, rows // blocks, width)
        if forward:
            y = x.reshape(n_tile, n_frame, -1, width).transpose(1, 0, 2, 3)
            y = lax.all_to_all(y.reshape(x.shape), ("frame", "tile"), 0, 0, tiled=True)
        else:
            y = lax.all_to_all(x, ("frame", "tile"), 0, 0, tiled=True)
            y = y.reshape(n_frame, n_tile, -1, width).transpose(1, 0, 2, 3)
        return y.reshape(rows, width)

    vecs = [row(v) for v in (ln1_gain, ln1_shift, ln2_gain, ln2_shift, ln3_gain, ln3_shift, ffn_in_bias, ffn_out_bias)]
    if on_boxes:
        *rest, small, tokens_grad, result = layer(
            mats, tokens, grad4, row(actions), row(segments), row(frame_mask), embed, vecs)
        summed = rest[6:]
        summed = [x.astype(F32) for x in summed]
        n_act = embed.shape[0]
        d_embed, lines = small[:n_act], small[n_act:]
        dg1, ds1, dg2, ds2, dg3, ds3, d_bout = (lines[i] for i in range(7))
        d_bin = lines[7 : 7 + ffn_in_bias.shape[0] // width].reshape(-1)
    else:
        action = lax.dynamic_index_in_dim(actions, t, keepdims=False)
        added = lax.dynamic_slice_in_dim(embed, action, 1, 0)
        one_hot = (action == jnp.arange(embed.shape[0], dtype=jnp.int32)).astype(F32)[:, None]
        number = jnp.arange(rows, dtype=jnp.int32)
        of_frame, of_place = number // place, number % place
        seg_row = jnp.repeat(segments, place)
        open_row = jnp.repeat(frame_mask, place)
        allowed = (
            (seg_row[:, None] == seg_row[None, :])
            & (of_place[:, None] == of_place[None, :])
            & (of_frame[None, :] <= of_frame[:, None])
            & ((open_row[None, :] == 1) | (of_frame[None, :] == of_frame[:, None]))
        )
        bias = jnp.where(allowed, 0.0, -1e30).astype(F32)
        nothing = jnp.zeros((1, width), F32)
        w_qs, w_os, w_qt, w_ot, w_in, w_out = (lax.all_gather(m, "frame", axis=0, tiled=True) for m in mats)
        base1 = lax.all_to_all(tokens, "tile", 0, 0, tiled=True).reshape(rows, width)
        g = lax.all_to_all(grad4.transpose(1, 0, 2, 3), "frame", 0, 0, tiled=True).reshape(rows, width)
        unit1, qkv1, mixed1, after1 = attn_fwd(
            base1, added, vecs[0], vecs[1], w_qs, w_os, None, BF16, "spatial_forward")
        base2 = turn(after1, True)
        unit2, qkv2, mixed2, after2 = attn_fwd(
            base2, nothing, vecs[2], vecs[3], w_qt, w_ot, bias, F32, "temporal_forward")
        unit3 = plain_norm(after2, ln3_gain, ln3_shift).astype(BF16)
        pre = jnp.dot(unit3, w_in, preferred_element_type=F32) + ffn_in_bias
        th = jnp.tanh(GELU_A * (pre + GELU_B * pre * pre * pre))
        act = (0.5 * pre * (1.0 + th)).astype(BF16)
        slope = 0.5 * (1.0 + th) + 0.5 * pre * (1.0 - th * th) * GELU_A * (1.0 + 3.0 * GELU_B * pre * pre)
        slope = slope.astype(BF16)
        result = after2 + jnp.dot(act, w_out, preferred_element_type=F32) + ffn_out_bias
        result = result.astype(BF16).reshape(n_frame, frames_dev, place, width)
        result = lax.all_to_all(result, "frame", 0, 0, tiled=True).transpose(1, 0, 2, 3)
        d_pre, d_after2, dg3, ds3, d_bin, d_bout = ffn_bwd(g, slope, after2, vecs[4], w_in, w_out)
        low2, d_qkv2, d_after1, dg2, ds2 = attn_bwd(
            base2, nothing, vecs[2], w_qt, w_ot, d_after2, qkv2, bias, BF16, "temporal_backward")
        d_out1 = turn(d_after1, False)
        low1, d_qkv1, d_start, dg1, ds1 = attn_bwd(
            base1, added, vecs[0], w_qs, w_os, d_out1, qkv1, None, F32, "spatial_backward")
        tokens_grad = d_start.astype(BF16).reshape(n_tile, tile_tokens, width)
        tokens_grad = lax.all_to_all(tokens_grad, "tile", 0, 0, tiled=True)
        d_embed = one_hot * jnp.sum(d_start, 0, keepdims=True)
        pairs = ((unit1, d_qkv1), (mixed1, low1), (unit2, d_qkv2), (mixed2, low2), (unit3, d_pre), (act, g))
        summed = []
        for a, b in pairs:
            part = lax.dot_general(a, b, (((0,), (0,)), ((), ())), preferred_element_type=F32)
            part = lax.psum_scatter(part, "frame", scatter_dimension=0, tiled=True)
            summed.append(lax.psum(part.astype(BF16), "tile").astype(F32))
        d_embed, dg1, ds1, dg2, ds2, dg3, ds3, d_bin, d_bout = lax.psum(
            (d_embed, dg1[0], ds1[0], dg2[0], ds2[0], dg3[0], ds3[0], d_bin[0], d_bout[0]), ("frame", "tile"))

    result = result.reshape(tokens.shape)
    return (result, tokens_grad, d_embed, dg1, ds1, summed[0], summed[1], dg2, ds2, summed[2], summed[3],
            dg3, ds3, summed[4], d_bin, summed[5], d_bout)


def solution(mesh):
    shard = P("frame", "tile", None)
    mat = P("frame", None)
    rep = P()
    in_specs = (shard, shard, P("frame"), rep, rep, rep, rep, rep, mat, mat, rep, rep, mat, mat,
                rep, rep, mat, rep, mat, rep)
    out_specs = (shard, shard, rep, rep, rep, mat, mat, rep, rep, mat, mat, rep, rep, mat, rep, mat, rep)
    on_boxes = mesh.shape["frame"] == 8 and mesh.shape["tile"] == 4
    return jax.shard_map(
        functools.partial(per_device, on_boxes),
        mesh=mesh, in_specs=in_specs, out_specs=out_specs, check_vma=False)
```

```python
import functools

import jax
import jax.numpy as jnp
from jax import lax
from jax.experimental import pallas as pl
from jax.experimental.pallas import tpu as pltpu
from jax.sharding import PartitionSpec as P

HD = 64
LANES = 128
EPS = 1e-5
MESH = pl.DeviceIdType.MESH
F32 = jnp.float32
BF16 = jnp.bfloat16
VMEM_SPEC = pl.BlockSpec(memory_space=pltpu.VMEM)
HBM_SPEC = pl.BlockSpec(memory_space=pltpu.HBM)


def params(**kw):
    return pltpu.CompilerParams(vmem_limit_bytes=60 * 1024 * 1024, **kw)


def at(j, size):
    return pl.ds(pl.multiple_of(j * size, size), size)


def each(n, fn):
    def step(i, carry):
        fn(i)
        return carry

    lax.fori_loop(0, n, step, 0)


def dot(a, b):
    return jnp.dot(a, b, preferred_element_type=F32)


def dot_nt(a, b):
    return lax.dot_general(a, b, (((1,), (1,)), ((), ())), preferred_element_type=F32)


def dot_tn(a, b):
    return lax.dot_general(a, b, (((0,), (0,)), ((), ())), preferred_element_type=F32)


def normed(h):
    cen = h - jnp.mean(h, -1, keepdims=True)
    inv = lax.rsqrt(jnp.mean(cen * cen, -1, keepdims=True) + EPS)
    return cen * inv, inv


ROWS = 32


def norm_rows(load, gain_ref, shift_ref, unit_ref):
    def step(i):
        rows = at(i, ROWS)
        xhat, _ = normed(load(rows))
        unit_ref[rows, :] = (xhat * gain_ref[...] + shift_ref[...]).astype(BF16)

    each(unit_ref.shape[0] // ROWS, step)


def fold(x):
    return jnp.sum(x.reshape(x.shape[0] // 8, 8, x.shape[1]), 0)


def norm_back(load, du_ref, gain_ref, dgain_ref, dshift_ref, acc_ref, store):
    acc_ref[...] = jnp.zeros_like(acc_ref)

    def step(i):
        rows = at(i, ROWS)
        xhat, inv = normed(load(rows))
        du = du_ref[rows, :]
        acc_ref[0] += fold(du * xhat)
        acc_ref[1] += fold(du)
        dx = du * gain_ref[...]
        dh = inv * (
            dx - jnp.mean(dx, -1, keepdims=True) - xhat * jnp.mean(dx * xhat, -1, keepdims=True)
        )
        store(rows, dh)

    each(du_ref.shape[0] // ROWS, step)
    dgain_ref[...] = jnp.sum(acc_ref[0], 0, keepdims=True)
    dshift_ref[...] = jnp.sum(acc_ref[1], 0, keepdims=True)


def head_masks():
    lane = lax.broadcasted_iota(jnp.int32, (1, LANES), 1)
    low = jnp.where(lane < HD, 1.0, 0.0)
    return low.astype(BF16), (1.0 - low).astype(BF16)


def head_probs(qm, k, bias_ref):
    s = dot_nt(qm, k) * (HD**-0.5)
    if bias_ref is not None:
        s = s + bias_ref[...]
    e = jnp.exp(s - jnp.max(s, -1, keepdims=True))
    return e * (1.0 / jnp.sum(e, -1, keepdims=True))


def attention(qkv_ref, bias_ref, mixed_ref, part=0, parts=1):
    width = mixed_ref.shape[1]
    per = width // LANES
    count = per // parts
    masks = head_masks()

    def pair(p):
        p = p + part * count
        q, k, v = (qkv_ref[:, at(p + i * per, LANES)] for i in range(3))
        out = 0.0
        for m in masks:
            out = out + dot(head_probs(q * m, k, bias_ref).astype(BF16), v * m)
        mixed_ref[:, at(p, LANES)] = out.astype(BF16)

    each(count, pair)


def attention_back(qkv_ref, bias_ref, dmix_ref, dqkv_ref):
    width = dmix_ref.shape[1]
    per = width // LANES
    masks = head_masks()
    scale = HD**-0.5

    def pair(p):
        q, k, v = (qkv_ref[:, at(p + i * per, LANES)] for i in range(3))
        dm = dmix_ref[:, at(p, LANES)]
        dq = dk = dv = 0.0
        for m in masks:
            qm = q * m
            dmm = dm * m
            probs = head_probs(qm, k, bias_ref)
            dp = dot_nt(dmm, v)
            ds = probs * (dp - jnp.sum(probs * dp, -1, keepdims=True))
            ds = ds.astype(BF16)
            dq = dq + dot(ds, k * m)
            dk = dk + dot_tn(ds, qm)
            dv = dv + dot_tn(probs.astype(BF16), dmm)
        dqkv_ref[:, at(p, LANES)] = (dq * scale).astype(BF16)
        dqkv_ref[:, at(p + per, LANES)] = (dk * scale).astype(BF16)
        dqkv_ref[:, at(p + 2 * per, LANES)] = dv.astype(BF16)

    each(per, pair)


def matmul(x_ref, w_ref, block, store):
    def step(j):
        cols = at(j, block)
        store(cols, dot(x_ref[...], w_ref[:, cols]))

    each(w_ref.shape[1] // block, step)


def matmul_nt(x_ref, w_ref, block, store):
    def step(j):
        rows = at(j, block)
        store(rows, dot_nt(x_ref[...], w_ref[rows, :]))

    each(w_ref.shape[0] // block, step)


def wgrad(core, shard, left, left_x, right, right_x, out, lt):
    tok = left.shape[0]
    col_blocks = right.shape[1] // TILE
    for rb in range(shard // 128):
        for q in range(4):
            cols = pl.ds(pl.multiple_of((2 * q + core) * shard + rb * 128, 128), 128)
            lt[q * 128 : (q + 1) * 128, :tok] = left[:, cols].T
            cols = pl.ds(q * shard + rb * 128, 128)
            lt[q * 128 : (q + 1) * 128, tok:] = left_x[:, cols].T

        def step(j, rb=rb):
            cols = at(j, 512)
            y = dot(lt[:, :tok], right[:, cols]) + dot(lt[:, tok:], right_x[:, cols])
            y = y.astype(BF16)
            unit = rb * col_blocks + j // 2
            half = pl.ds(pl.multiple_of(lax.rem(j, 2) * 512, 512), 512)
            for q in range(4):
                out[unit, q, :, half] = y[q * 128 : (q + 1) * 128]

        each(2 * col_blocks, step)


GELU_A = 0.7978845608
GELU_B = 0.044715


def xor(a, b):
    bit = lax.rem(a // b, 2)
    return a + b - 2 * b * bit


def greet(partners):
    barrier = pltpu.get_barrier_semaphore()
    for p in partners:
        pl.semaphore_signal(barrier, inc=1, device_id=p, device_id_type=MESH)
    pl.semaphore_wait(barrier, len(partners))


def remote(src, dst, ssem, rsem, dev):
    return pltpu.make_async_remote_copy(
        src_ref=src, dst_ref=dst, send_sem=ssem, recv_sem=rsem, device_id=dev, device_id_type=MESH
    )


def xor_any(a, bits):
    for b in (1, 2, 4, 8, 16):
        if bits & b:
            a = xor(a, b)
    return a


TILE = 1024
SLOTS = 4
AHEAD = 3
LAG = 2
PACE = (6, 7, 8, 10, 12, 13, 14, 15, 16, 17, 18)
DEEP = 3
RING = 6


def gather_chunks(shapes):
    out = []
    for i, (rows, cols) in enumerate(shapes):
        step = rows
        while step * cols > 128 * 1024 and step % 32 == 0:
            step //= 2
        out += [(i, r, step) for r in range(0, rows, step)]
    return out


def weight_tiles(shapes):
    return [
        (i, r, c)
        for i, (rows, cols) in enumerate(shapes)
        for r in range(0, rows, TILE)
        for c in range(0, cols, TILE)
    ]


def add_into(dst, a, b):
    def step(i):
        r = at(i, 16)
        dst[r, :] = (a[r, :].astype(F32) + b[r, :].astype(F32)).astype(dst.dtype)

    each(dst.shape[0] // 16, step)


def layer_kernel(chunks, tiles, units, *refs):
    shards = refs[:6]
    (tokens, grad4, actions, segments, frame_mask, embed,
     gain1, shift1, gain2, shift2, gain3, shift3, b_in, b_out) = refs[6:20]
    full = refs[20:26]
    outs = refs[26:32]
    small_out, tokens_grad, result = refs[32:35]
    (base1, unit1, qkv1, mixed1, base2, unit2, qkv2, mixed2, after2, unit3, slope, g2d, act,
     wt, gbuf, r1, r2, zin, zpeer, act_x, g_x, dpre_x, unit3_x, mix2_x, low2_x, unit2_x, dqkv2_x,
     mix1_x, low1_x, unit1_x, dqkv1_x, du, low2, low1, dmix, dqkv,
     out1, in2, g_in, res_out, turn_out, turn_in, bias, added, sm, smr, lt, acc, emb,
     ssem, rsem, bsem, tsem, z3s, z3r, z3l, f7s, f7r, f7l, turn_s, turn_r, turn_l, back_s, back_r, back_l,
     s1s, s1r, s2s, s2r, zs, zr, zps, zpr, osem, sms, smrs, xs, xr, o7s, o7r, o7l, t3s, t3r, t3l) = refs[35:]
    f = lax.axis_index("frame")
    t = lax.axis_index("tile")
    core = lax.rem(f, 2)
    chip = f // 2
    odd = lax.rem(t, 2)
    leaf = (t == 0) | (t == 3)
    inner = jnp.logical_not(leaf)
    fx, fy, sib = xor(f, 2), xor(f, 4), xor(f, 1)
    first = fx + (fy - fx) * odd
    second = fy + (fx - fy) * odd
    diag = xor_any(f, 6)
    cx, cy, cd = xor(chip, 1), xor(chip, 2), xor_any(chip, 3)
    to_sib, to_first, to_second = (sib, t), (first, t), (second, t)
    to_x, to_y, to_z, to_peer = (fx, t), (fy, t), (f, xor(t, 1)), (f, 3 - t)
    others = [(a, b) for a in range(8) for b in range(4) if a or b]
    greet([(xor_any(f, a), xor_any(t, b)) for a, b in others])

    def piece(k, owner):
        a, r, rows = chunks[k]
        return full[a].at[pl.ds(pl.multiple_of(owner * shards[a].shape[0] + r, 16), rows)]

    def own(k):
        a, r, rows = chunks[k]
        return shards[a].at[pl.ds(r, rows)]

    def copy(k, kind):
        dev = (to_first, to_second, to_z, to_sib, to_sib, to_sib, to_sib)[kind]
        owner = (f, first, first, f, first, diag, second)[kind]
        src = own(k) if kind in (0, 3) else piece(k, owner)
        return remote(src, piece(k, owner), ssem.at[k, kind], rsem.at[k, kind], dev)

    def arrived(k, kind):
        owner = (first, diag, second, sib, xor(first, 1), xor(diag, 1), xor(second, 1))[kind]
        dst = piece(k, owner)
        remote(dst, dst, ssem.at[k, kind], rsem.at[k, kind], to_sib).wait_recv()

    n_chunks = len(chunks)
    progress = [0, 0, AHEAD]

    def relay_to(k):
        while progress[1] < min(k, progress[0]):
            k1 = progress[1]
            progress[1] += 1
            for kind in (1, 2):
                arrived(k1, kind)
                copy(k1, kind + 4).start()

    def advance(hops, ahead=AHEAD, lag=LAG):
        while progress[0] < min(hops, n_chunks):
            k = progress[0]
            progress[0] += 1
            copy(k, 3).start()
            arrived(k, 0)
            while progress[2] < min(k + 1 + ahead, n_chunks):
                copy(progress[2], 0).start()
                progress[2] += 1
            for kind in (1, 2, 4):
                copy(k, kind).start()
            relay_to(k + 1 - lag)

    def complete(a):
        ks = [k for k in range(n_chunks) if chunks[k][0] == a]
        advance(ks[-1] + 2)
        relay_to(ks[-1] + 1)
        for k in ks:
            for kind in (3, 4, 5, 6):
                arrived(k, kind)

    bounce = []
    for a, shard in enumerate(shards):
        for r in range(0, shard.shape[0], 128):
            for c in range(0, shard.shape[1], TILE):
                i = len(bounce)
                bounce.append((a, r, c, wt.at[2 + i // 8, pl.ds(i % 8 * 128, 128)]))

    def bounce_in(i):
        a, r, c, via = bounce[i]
        return pltpu.make_async_copy(shards[a].at[pl.ds(r, 128), pl.ds(c, TILE)], via, bsem.at[i])

    def bounce_out(i):
        a, r, c, via = bounce[i]
        row = pl.multiple_of(f * shards[a].shape[0] + r, 128)
        return pltpu.make_async_copy(via, full[a].at[pl.ds(row, 128), pl.ds(c, TILE)], bsem.at[i])

    def tile_load(i):
        a, r, c = tiles[i]
        src = full[a].at[pl.ds(r, TILE), pl.ds(c, TILE)]
        return pltpu.make_async_copy(src, wt.at[i % SLOTS], tsem.at[i])

    def load(ids):
        for i in ids:
            if i < len(tiles):
                tile_load(i).start()

    n = len(units)

    def hop(u):
        return (to_x, cx, to_y, cy) if u % 2 == 0 else (to_y, cy, to_x, cx)

    def part(u, p):
        _, _, _, rows, unit, top = units[u]
        return gbuf.at[unit // 4 % 3, unit % 4, p, pl.ds(top, rows)]

    def slot(ref, u, *more):
        return ref.at[(u % RING, *more, pl.ds(0, units[u][3]))]

    def step1(u):
        dev1, p1, _, _ = hop(u)
        return (
            remote(part(u, cd), slot(r1, u, 1), s1s.at[u, 1], s1r.at[u, 1], dev1),
            remote(part(u, p1), slot(r1, u, 0), s1s.at[u, 0], s1r.at[u, 0], dev1),
        )

    def step2(u):
        _, _, dev2, p2 = hop(u)
        return remote(part(u, p2), slot(r2, u), s2s.at[u], s2r.at[u], dev2)

    def along(u):
        return remote(part(u, chip), slot(zin, u), zs.at[u], zr.at[u], to_z)

    def across(u):
        return remote(part(u, chip), slot(zpeer, u), zps.at[u], zpr.at[u], to_peer)

    def emit(u, src):
        a, r, c, rows, _, _ = units[u]
        return pltpu.make_async_copy(src, outs[a].at[pl.ds(r, rows), pl.ds(c, TILE)], osem.at[u])

    state = {"ready": 0, "issued": 0, "done": 0, "step": 0}

    def issue():
        while state["issued"] < min(state["ready"], state["done"] + DEEP):
            for c in step1(state["issued"]):
                c.start()
            state["issued"] += 1

    def offer(count):
        state["ready"] += count
        issue()

    def reduce_step():
        s = state["step"]
        state["step"] += 1
        u = s
        if u < n:
            assert u < state["issued"]
            p2 = hop(u)[3]
            far, near = step1(u)
            far.wait_recv()
            add_into(part(u, p2), part(u, p2), slot(r1, u, 1))
            step2(u).start()
            near.wait_recv()
            add_into(part(u, chip), part(u, chip), slot(r1, u, 0))
            state["done"] += 1
            issue()
        u = s - 1
        if 0 <= u < n:
            step2(u).wait_recv()
            add_into(part(u, chip), part(u, chip), slot(r2, u))

            @pl.when(leaf)
            def _(u=u):
                along(u).start()

        u = s - 2
        if 0 <= u < n:
            @pl.when(inner)
            def _(u=u):
                along(u).wait_recv()
                add_into(part(u, chip), part(u, chip), slot(zin, u))
                across(u).start()

        u = s - 3
        if 0 <= u < n:
            @pl.when(inner)
            def _(u=u):
                across(u).wait()
                add_into(part(u, chip), part(u, chip), slot(zpeer, u))
                along(u).start()
                emit(u, part(u, chip)).start()

        u = s - 4
        if 0 <= u < n:
            @pl.when(leaf)
            def _(u=u):
                along(u).wait()
                emit(u, slot(zin, u)).start()

        u = s - 5
        if 0 <= u < n:
            for c in step1(u):
                c.wait_send()
            step2(u).wait_send()

            @pl.when(inner)
            def _(u=u):
                along(u).wait_send()

            emit(u, part(u, chip)).wait()

    def reduce_to(s):
        while state["step"] < s:
            reduce_step()

    def share(i, left, left_x, right, right_x):
        shard = left.shape[1] // 8
        copies = [
            remote(left.at[:, pl.ds(pl.multiple_of((2 * p + 1 - core) * shard, shard), shard)],
                   left_x.at[:, pl.ds(p * shard, shard)], xs.at[i, p], xr.at[i, p], to_sib)
            for p in range(4)
        ]
        copies.append(remote(right, right_x, xs.at[i, 4], xr.at[i, 4], to_sib))
        for c in copies:
            c.start()
        return copies

    def wait_all(copies):
        for c in copies:
            c.wait()

    def rows_of(ref, i):
        return ref.at[pl.ds(pl.multiple_of(i * 64, 64), 64)]

    def over_tile(src, dst, ssems, rsems, lsem):
        ds = [xor_any(t, i) for i in (1, 2, 3)]
        own = pltpu.make_async_copy(src(t), dst(t), lsem)
        go = [remote(src(d), dst(t), ssems.at[i], rsems.at[i], (f, d)) for i, d in enumerate(ds)]
        end = [remote(src(d), dst(d), ssems.at[i], rsems.at[i], (f, d)) for i, d in enumerate(ds)]
        return [own] + go, [own] + end

    def over_frame(src, dst, ssems, rsems, lsem):
        ds = [xor_any(f, i) for i in range(1, 8)]
        own = pltpu.make_async_copy(src(f), dst(f), lsem)
        go = [remote(src(d), dst(f), ssems.at[i], rsems.at[i], (d, t)) for i, d in enumerate(ds)]
        end = [remote(src(d), dst(d), ssems.at[i], rsems.at[i], (d, t)) for i, d in enumerate(ds)]
        return [own] + go, [own] + end

    def over_both(src, dst, ssems, rsems, lsem):
        ds = [(xor_any(f, a), xor_any(t, b)) for a, b in others]
        own = pltpu.make_async_copy(src(f, t), dst(f, t), lsem)
        go = [remote(src(*d), dst(f, t), ssems.at[i], rsems.at[i], d) for i, d in enumerate(ds)]
        end = [remote(src(*d), dst(*d), ssems.at[i], rsems.at[i], d) for i, d in enumerate(ds)]
        return [own] + go, [own] + end

    def start_all(copies):
        for c in copies:
            c.start()

    def split(load_rows, dst):
        def step(i):
            dst[pl.ds(4 * i, 4)] = load_rows(at(i, ROWS)).reshape(4, 8, TILE).astype(BF16)

        each(dst.shape[0] // 4, step)

    def join(src, dst):
        def step(i):
            dst[at(i, ROWS), :] = src[pl.ds(4 * i, 4)].astype(F32).reshape(ROWS, TILE).astype(BF16)

        each(src.shape[0] // 4, step)

    tok_go, tok_end = over_tile(lambda d: tokens.at[d], lambda d: rows_of(base1, d), z3s, z3r, z3l)
    start_all(tok_go)
    for k in range(AHEAD):
        copy(k, 0).start()
    for i in range(len(bounce)):
        bounce_in(i).start()
    grad_go, grad_end = over_frame(
        lambda d: grad4.at[:, d], lambda d: g_in.at[pl.ds(4 * d, 4)], f7s, f7r, f7l)

    which = jnp.sum(jnp.where(lax.broadcasted_iota(jnp.int32, (1, 4), 1) == t, actions[...], 0), -1, keepdims=True)
    hot = jnp.where(lax.broadcasted_iota(jnp.int32, (8, 1), 0) == which, 1.0, 0.0)
    added[...] = jnp.sum(hot * embed[...], 0, keepdims=True)
    n_frames = segments.shape[1]
    n_rows = bias.shape[0]
    place = n_rows // n_frames

    def column(ref):
        a = lax.broadcasted_iota(jnp.int32, (n_frames, n_frames), 0)
        b = lax.broadcasted_iota(jnp.int32, (n_frames, n_frames), 1)
        return jnp.sum(jnp.where(a == b, ref[...].astype(F32), 0.0), 1, keepdims=True)

    by_row = lax.broadcasted_iota(jnp.int32, (n_rows, n_frames), 0) // place
    by_row = by_row == lax.broadcasted_iota(jnp.int32, (n_rows, n_frames), 1)
    by_col = lax.broadcasted_iota(jnp.int32, (n_frames, n_rows), 1) // place
    by_col = by_col == lax.broadcasted_iota(jnp.int32, (n_frames, n_rows), 0)
    seg_q = jnp.sum(jnp.where(by_row, segments[...].astype(F32), 0.0), 1, keepdims=True)
    seg_k = jnp.sum(jnp.where(by_col, column(segments), 0.0), 0, keepdims=True)
    open_k = jnp.sum(jnp.where(by_col, column(frame_mask), 0.0), 0, keepdims=True)
    row_q = lax.broadcasted_iota(jnp.int32, (n_rows, n_rows), 0)
    row_k = lax.broadcasted_iota(jnp.int32, (n_rows, n_rows), 1)
    allowed = (
        (seg_q == seg_k)
        & (lax.rem(row_q, place) == lax.rem(row_k, place))
        & (row_k // place <= row_q // place)
        & ((open_k == 1.0) | (row_k == row_q))
    )
    bias[...] = jnp.where(allowed, 0.0, -1e30)

    advance(1)
    for i in range(len(bounce)):
        bounce_in(i).wait()
        bounce_out(i).start()
    wait_all(tok_end)
    norm_rows(lambda rows: base1[rows, :].astype(F32) + added[...], gain1, shift1, unit1)
    start_all(grad_go)
    for i in range(len(bounce)):
        bounce_out(i).wait()

    def project(unit, ids, out_ref):
        for j, i in enumerate(ids):
            tile_load(i).wait()

            def put(cols, y, j=j):
                start = pl.multiple_of(cols.start + j * TILE, 512)
                out_ref[:, pl.ds(start, 512)] = y.astype(BF16)

            matmul(unit, wt.at[i % SLOTS], 512, put)

    complete(0)
    load((0, 1, 2))
    project(unit1, (0, 1, 2), qkv1)
    advance(PACE[0])
    complete(1)
    load((3,))
    attention(qkv1, None, mixed1, 0, 2)
    advance(PACE[1])
    attention(qkv1, None, mixed1, 1, 2)
    advance(PACE[2])
    tile_load(3).wait()

    def put_after1(cols, y):
        du[:, cols] = y + base1[:, cols].astype(F32) + added[:, cols]

    matmul(mixed1, wt.at[3], 512, put_after1)
    split(lambda rows: du[rows, :], out1)

    turn_go, turn_end = over_both(
        lambda a, b: out1.at[8 * b + a], lambda a, b: in2.at[4 * a + b], turn_s, turn_r, turn_l)
    start_all(turn_go)
    advance(PACE[3])
    complete(2)
    load((4, 5, 6))
    complete(3)
    load((7,))
    advance(PACE[4])
    wait_all(turn_end)
    join(in2, base2)
    norm_rows(lambda rows: base2[rows, :].astype(F32), gain2, shift2, unit2)
    advance(PACE[5])
    project(unit2, (4, 5, 6), qkv2)
    advance(PACE[6])
    attention(qkv2, bias, mixed2, 0, 2)
    advance(PACE[7])
    attention(qkv2, bias, mixed2, 1, 2)
    advance(PACE[8])
    tile_load(7).wait()

    def put_after2(cols, y):
        after2[:, cols] = y + base2[:, cols].astype(F32)

    matmul(mixed2, wt.at[3], 512, put_after2)
    norm_rows(lambda rows: after2[rows, :], gain3, shift3, unit3)
    complete(4)
    load((8, 9, 10, 11))
    wait_all(grad_end)
    join(g_in, g2d)

    for j in range(4):
        tile_load(8 + j).wait()

        def put_pre(cols, y, j=j):
            cols = pl.ds(pl.multiple_of(cols.start + j * TILE, 256), 256)
            v = y + b_in[:, cols]
            th = jnp.tanh(GELU_A * (v + GELU_B * v * v * v))
            act[:, cols] = (0.5 * v * (1.0 + th)).astype(BF16)
            rise = 0.5 * (1.0 + th) + 0.5 * v * (1.0 - th * th) * GELU_A * (1.0 + 3.0 * GELU_B * v * v)
            slope[:, cols] = rise.astype(BF16)

        matmul(unit3, wt.at[j], 256, put_pre)
        if j == 1:
            advance(PACE[9])

    swap4 = share(0, act, act_x, g2d, g_x)
    advance(PACE[10])
    wait_all(swap4)
    wgrad(core, act.shape[1] // 8, act, act_x, g2d, g_x, gbuf.at[0], lt)
    complete(5)
    load((12, 13, 14, 15))
    offer(4)

    sm[0] = jnp.zeros_like(sm[0])
    for j in range(4):
        tile_load(12 + j).wait()

        def put_dpre(rows, y, j=j):
            cols = pl.ds(pl.multiple_of(rows.start + j * TILE, 256), 256)
            d = (y * slope[:, cols].astype(F32)).astype(BF16)
            slope[:, cols] = d
            sm[0, 15 + j : 16 + j, rows] = jnp.sum(d.astype(F32), 0, keepdims=True)

        matmul_nt(g2d, wt.at[j], 256, put_dpre)

        def add_up(h, j=j):
            cols = at(h, 512)
            y = dot(act[:, j * TILE : (j + 1) * TILE], wt[j, :, cols])
            du[:, cols] = y + (after2[:, cols] + b_out[:, cols] if j == 0 else du[:, cols])

        each(2, add_up)
        load((16 + j,))
    dpre = slope
    swap3 = share(1, unit3, unit3_x, dpre, dpre_x)
    split(lambda rows: du[rows, :], res_out)
    res_go, res_end = over_frame(
        lambda d: res_out.at[pl.ds(4 * d, 4)], lambda d: result.at[:, d], o7s, o7r, o7l)
    reduce_to(1)

    def back_through(first_tile, count, x_ref):
        for j in range(count):
            i = first_tile + j
            tile_load(i).wait()

            def run(h, i=i, j=j):
                rows = at(h, 256)
                y = dot_nt(x_ref[:, j * TILE : (j + 1) * TILE], wt[i % SLOTS, rows, :])
                du[:, rows] = y if j == 0 else du[:, rows] + y

            each(TILE // 256, run)
            load((i + SLOTS,))

    back_through(16, 4, dpre)

    def store3(rows, dh):
        g = g2d[rows, :].astype(F32)
        d = g + dh
        after2[rows, :] = d
        low2[rows, :] = d.astype(BF16)
        sm[0, 14:15, :] += jnp.sum(g, 0, keepdims=True)

    norm_back(lambda rows: after2[rows, :], du, gain3, sm.at[0, pl.ds(12, 1)], sm.at[0, pl.ds(13, 1)], acc, store3)
    dafter = after2
    swap2o = share(2, mixed2, mix2_x, low2, low2_x)
    reduce_to(2)
    wait_all(swap3)
    wgrad(core, TILE // 8, unit3, unit3_x, dpre, dpre_x, gbuf.at[1], lt)
    offer(4)

    def put_mix(rows, y):
        dmix[:, rows] = y.astype(BF16)

    tile_load(20).wait()
    matmul_nt(low2, wt.at[0], 512, put_mix)
    load((24,))
    reduce_to(3)
    attention_back(qkv2, bias, dmix, dqkv)
    swap2 = share(3, unit2, unit2_x, dqkv, dqkv2_x)
    reduce_to(4)
    back_through(21, 3, dqkv)

    def store2(rows, dh):
        dafter[rows, :] = dafter[rows, :] + dh

    norm_back(lambda rows: base2[rows, :].astype(F32), du, gain2, sm.at[0, pl.ds(10, 1)], sm.at[0, pl.ds(11, 1)], acc, store2)
    split(lambda rows: dafter[rows, :], turn_out)

    back_go, back_end = over_both(
        lambda a, b: turn_out.at[4 * a + b], lambda a, b: turn_in.at[8 * b + a], back_s, back_r, back_l)
    start_all(back_go)
    wait_all(swap2o)
    wgrad(core, TILE // 8, mixed2, mix2_x, low2, low2_x, gbuf.at[2, pl.ds(0, 1)], lt)
    wait_all(swap2)
    wgrad(core, TILE // 8, unit2, unit2_x, dqkv, dqkv2_x, gbuf.at[2, pl.ds(1, 3)], lt)
    offer(4)
    reduce_to(5)
    wait_all(back_end)
    join(turn_in, low1)
    swap1o = share(4, mixed1, mix1_x, low1, low1_x)
    tile_load(24).wait()
    matmul_nt(low1, wt.at[0], 512, put_mix)
    reduce_to(6)
    attention_back(qkv1, None, dmix, dqkv)
    swap1 = share(5, unit1, unit1_x, dqkv, dqkv1_x)
    wait_all(swap1o)
    wgrad(core, TILE // 8, mixed1, mix1_x, low1, low1_x, gbuf.at[0, pl.ds(0, 1)], lt)
    offer(1)
    reduce_to(7)
    back_through(25, 3, dqkv)
    reduce_to(9)
    wait_all(swap1)
    wgrad(core, TILE // 8, unit1, unit1_x, dqkv, dqkv1_x, gbuf.at[0, pl.ds(1, 3)], lt)
    offer(6)
    emb[...] = jnp.zeros_like(emb)

    def store1(rows, dh):
        d = low1[rows, :].astype(F32) + dh
        low2[rows, :] = d.astype(BF16)
        emb[...] += fold(d)

    norm_back(lambda rows: base1[rows, :].astype(F32) + added[...], du, gain1, sm.at[0, pl.ds(8, 1)], sm.at[0, pl.ds(9, 1)], acc, store1)
    sm[0, 0:8, :] = hot * jnp.sum(emb[...], 0, keepdims=True)

    last_go, last_end = over_tile(lambda d: rows_of(low2, d), lambda d: tokens_grad.at[d], t3s, t3r, t3l)
    start_all(last_go)

    def small_copy(i, dev):
        return remote(sm.at[i], smr.at[i], sms.at[i], smrs.at[i], dev)

    def small_down():
        return remote(sm.at[5], smr.at[3], sms.at[5], smrs.at[3], to_z)

    hops = (to_sib, to_x, to_y)
    small_copy(0, to_sib).start()
    for i in range(3):
        reduce_to(state["step"] + 1)
        small_copy(i, hops[i]).wait()
        sm[i + 1] = sm[i] + smr[i]
        if i < 2:
            small_copy(i + 1, hops[i + 1]).start()

    @pl.when(leaf)
    def _():
        small_copy(3, to_z).start()

    reduce_to(state["step"] + 1)

    @pl.when(inner)
    def _():
        small_copy(3, to_z).wait_recv()
        sm[4] = sm[3] + smr[3]
        small_copy(4, to_peer).start()

    reduce_to(state["step"] + 1)

    @pl.when(inner)
    def _():
        small_copy(4, to_peer).wait()
        sm[5] = sm[4] + smr[4]
        small_down().start()
        small_out[...] = sm[5]

    reduce_to(n + 1)
    start_all(res_go)
    reduce_to(n + 5)

    @pl.when(leaf)
    def _():
        small_copy(3, to_z).wait()
        small_out[...] = smr[3]

    @pl.when(inner)
    def _():
        small_down().wait_send()

    wait_all(last_end)
    wait_all(res_end)
    for k in range(n_chunks):
        for kind in range(7):
            copy(k, kind).wait_send()


def layer(mats, tokens, grad4, actions, segments, frame_mask, embed, vecs):
    width = tokens.shape[2]
    rows = tokens.shape[0] * tokens.shape[1]
    ff = mats[4].shape[1]
    fulls = [(8 * m.shape[0], m.shape[1]) for m in mats]
    chunks = gather_chunks([m.shape for m in mats])
    by_mat = weight_tiles(fulls)
    order = (5, 4, 3, 2, 1, 0)
    tiles = by_mat + [x for a in order[1:] for x in by_mat if x[0] == a]
    whole = [
        (a, r, c) for a in order
        for r in range(0, mats[a].shape[0], 128) for c in range(0, mats[a].shape[1], TILE)
    ]
    units = []
    for i, (a, r, c) in enumerate(whole):
        step = 64 if i >= len(whole) - 3 else 128
        units += [(a, r + top, c, step, i, top) for top in range(0, 128, step)]
    n = len(units)
    n_chunks = len(chunks)
    dma = pltpu.SemaphoreType.DMA
    blocks = (32, 8, width)
    unit = (128, TILE)
    bf = lambda *s: pltpu.VMEM(s, BF16)
    fl = lambda *s: pltpu.VMEM(s, F32)
    half = width // 2
    scratch = [
        bf(rows, width), bf(rows, width), bf(rows, 3 * width), bf(rows, width),
        bf(rows, width), bf(rows, width), bf(rows, 3 * width), bf(rows, width),
        fl(rows, width), bf(rows, width), bf(rows, ff), bf(rows, width), bf(rows, ff),
        bf(SLOTS, TILE, TILE), bf(3, 4, 4, *unit), bf(RING, 2, *unit), bf(RING, *unit),
        bf(RING, *unit), bf(RING, *unit),
        bf(rows, ff // 2), bf(rows, width), bf(rows, ff), bf(rows, half),
        bf(rows, half), bf(rows, width), bf(rows, half), bf(rows, 3 * width),
        bf(rows, half), bf(rows, width), bf(rows, half), bf(rows, 3 * width),
        fl(rows, width), bf(rows, width), bf(rows, width), bf(rows, width), bf(rows, 3 * width),
        bf(*blocks), bf(*blocks), bf(*blocks), bf(*blocks), bf(*blocks), bf(*blocks),
        fl(rows, rows), fl(1, width),
        fl(6, 24, width), fl(5, 24, width), bf(512, 2 * rows), fl(2, 8, width), fl(8, width),
    ]
    sems = [
        (n_chunks, 7), (n_chunks, 7), (16,), (len(tiles),), (3,), (3,), (), (7,), (7,), (),
        (31,), (31,), (), (31,), (31,), (),
        (n, 2), (n, 2), (n,), (n,), (n,), (n,), (n,), (n,), (n,), (6,), (6,), (6, 5), (6, 5),
        (7,), (7,), (), (3,), (3,), (),
    ]
    return pl.pallas_call(
        functools.partial(layer_kernel, chunks, tiles, units),
        out_shape=[jax.ShapeDtypeStruct(s, BF16) for s in fulls]
        + [jax.ShapeDtypeStruct(m.shape, BF16) for m in mats]
        + [
            jax.ShapeDtypeStruct((24, width), F32),
            jax.ShapeDtypeStruct(tokens.shape, BF16),
            jax.ShapeDtypeStruct(grad4.shape, BF16),
        ],
        in_specs=[HBM_SPEC] * 8 + [VMEM_SPEC] * (4 + len(vecs)),
        out_specs=[HBM_SPEC] * 12 + [VMEM_SPEC] + [HBM_SPEC] * 2,
        scratch_shapes=scratch + [dma(s) if s else dma for s in sems],
        compiler_params=params(collective_id=0, has_side_effects=True),
        name="layer",
    )(*mats, tokens, grad4, actions, segments, frame_mask, embed, *vecs)


def widen_kernel(n_mats, *refs):
    mats, (small, grad, res) = refs[:n_mats], refs[n_mats : n_mats + 3]
    wide = refs[n_mats + 3 : 2 * n_mats + 3]
    embed_g, g1, s1, g2, s2, g3, s3, b_out, b_in, grad_out, res_out = refs[2 * n_mats + 3 : 2 * n_mats + 14]
    low = refs[2 * n_mats + 14 : 3 * n_mats + 14]
    high = refs[3 * n_mats + 14 : 4 * n_mats + 14]
    passing, isem, osem = refs[4 * n_mats + 14 :]
    ins = [pltpu.make_async_copy(m, v, isem.at[i]) for i, (m, v) in enumerate(zip(mats, low))]
    outs = [pltpu.make_async_copy(v, w, osem.at[i]) for i, (v, w) in enumerate(zip(high, wide))]
    for i, (a, b) in enumerate(((grad, grad_out), (res, res_out))):
        ins.append(pltpu.make_async_copy(a, passing.at[i], isem.at[n_mats + i]))
        outs.append(pltpu.make_async_copy(passing.at[i], b, osem.at[n_mats + i]))
    for c in ins:
        c.start()
    n_act = embed_g.shape[0]
    embed_g[...] = small[0:n_act, :]
    for i, ref in enumerate((g1, s1, g2, s2, g3, s3, b_out)):
        ref[...] = small[n_act + i : n_act + i + 1, :]
    width = small.shape[1]
    for i in range(b_in.shape[1] // width):
        b_in[:, i * width : (i + 1) * width] = small[n_act + 7 + i : n_act + 8 + i, :]
    for i in range(n_mats):
        ins[i].wait()

        def step(j, i=i):
            rows = at(j, 16)
            high[i][rows, :] = low[i][rows, :].astype(F32)

        each(low[i].shape[0] // 16, step)
        outs[i].start()
    for i in (n_mats, n_mats + 1):
        ins[i].wait()
        outs[i].start()
    for c in outs:
        c.wait()


def widen(mats, small, grad, res, n_act, ff):
    n = len(mats)
    width = small.shape[1]
    lines = [(n_act, width)] + [(1, width)] * 7 + [(1, ff)]
    res = res.reshape(grad.shape)
    return pl.pallas_call(
        functools.partial(widen_kernel, n),
        out_shape=[jax.ShapeDtypeStruct(m.shape, F32) for m in mats]
        + [jax.ShapeDtypeStruct(s, F32) for s in lines]
        + [jax.ShapeDtypeStruct(grad.shape, grad.dtype)] * 2,
        in_specs=[HBM_SPEC] * n + [VMEM_SPEC] + [HBM_SPEC] * 2,
        out_specs=[HBM_SPEC] * n + [VMEM_SPEC] * 9 + [HBM_SPEC] * 2,
        scratch_shapes=[pltpu.VMEM(m.shape, BF16) for m in mats]
        + [pltpu.VMEM(m.shape, F32) for m in mats]
        + [pltpu.VMEM((2,) + grad.shape, grad.dtype)]
        + [pltpu.SemaphoreType.DMA((n + 2,))] * 2,
        compiler_params=params(),
        name="widen",
    )(*mats, small, grad, res)


def plain_norm(h, gain, shift):
    cen = h - jnp.mean(h, -1, keepdims=True)
    inv = lax.rsqrt(jnp.mean(cen * cen, -1, keepdims=True) + EPS)
    return cen * inv * gain + shift


def attn_fwd_kernel(masked, base_ref, added_ref, gain_ref, shift_ref, wqkv_ref, wo_ref, *rest):
    if masked:
        bias_ref, unit_ref, qkv_ref, mixed_ref, after_ref = rest
    else:
        bias_ref = None
        unit_ref, qkv_ref, mixed_ref, after_ref = rest

    def load(rows):
        return base_ref[rows, :].astype(F32) + added_ref[...]

    norm_rows(load, gain_ref, shift_ref, unit_ref)

    def put_qkv(cols, y):
        qkv_ref[:, cols] = y.astype(BF16)

    matmul(unit_ref, wqkv_ref, 512, put_qkv)
    attention(qkv_ref, bias_ref, mixed_ref)

    def put_after(cols, y):
        y = y + base_ref[:, cols].astype(F32) + added_ref[:, cols]
        after_ref[:, cols] = y.astype(after_ref.dtype)

    matmul(mixed_ref, wo_ref, 512, put_after)


def attn_fwd(base, added, gain, shift, wqkv, wo, bias, out_type, name):
    rows, width = base.shape
    ins = [base, added, gain, shift, wqkv, wo] + ([bias] if bias is not None else [])
    shapes = [(width, BF16), (3 * width, BF16), (width, BF16), (width, out_type)]
    return pl.pallas_call(
        functools.partial(attn_fwd_kernel, bias is not None),
        out_shape=[jax.ShapeDtypeStruct((rows, w), d) for w, d in shapes],
        in_specs=[VMEM_SPEC] * len(ins),
        out_specs=[VMEM_SPEC] * 4,
        compiler_params=params(),
        name=name,
    )(*ins)


def attn_bwd_kernel(masked, base_ref, added_ref, gain_ref, wqkv_ref, wo_ref, dout_ref, qkv_ref, *rest):
    if masked:
        bias_ref, *rest = rest
    else:
        bias_ref = None
    dlow_ref, dqkv_ref, dbase_ref, dgain_ref, dshift_ref, dmix_ref, du_ref, acc_ref = rest

    def cast(i):
        rows = at(i, ROWS)
        dlow_ref[rows, :] = dout_ref[rows, :].astype(BF16)

    each(dlow_ref.shape[0] // ROWS, cast)

    def put_mix(rows, y):
        dmix_ref[:, rows] = y.astype(BF16)

    matmul_nt(dlow_ref, wo_ref, 512, put_mix)
    attention_back(qkv_ref, bias_ref, dmix_ref, dqkv_ref)

    def put_du(rows, y):
        du_ref[:, rows] = y

    matmul_nt(dqkv_ref, wqkv_ref, 256, put_du)

    def load(rows):
        return base_ref[rows, :].astype(F32) + added_ref[...]

    def store(rows, dh):
        dbase_ref[rows, :] = (dout_ref[rows, :].astype(F32) + dh).astype(dbase_ref.dtype)

    norm_back(load, du_ref, gain_ref, dgain_ref, dshift_ref, acc_ref, store)


def attn_bwd(base, added, gain, wqkv, wo, dout, qkv, bias, out_type, name):
    rows, width = base.shape
    ins = [base, added, gain, wqkv, wo, dout, qkv] + ([bias] if bias is not None else [])
    outs = [
        jax.ShapeDtypeStruct((rows, width), BF16),
        jax.ShapeDtypeStruct((rows, 3 * width), BF16),
        jax.ShapeDtypeStruct((rows, width), out_type),
        jax.ShapeDtypeStruct((1, width), F32),
        jax.ShapeDtypeStruct((1, width), F32),
    ]
    return pl.pallas_call(
        functools.partial(attn_bwd_kernel, bias is not None),
        out_shape=outs,
        in_specs=[VMEM_SPEC] * len(ins),
        out_specs=[VMEM_SPEC] * len(outs),
        scratch_shapes=[
            pltpu.VMEM((rows, width), BF16),
            pltpu.VMEM((rows, width), F32),
            pltpu.VMEM((2, 8, width), F32),
        ],
        compiler_params=params(),
        name=name,
    )(*ins)


def ffn_bwd_kernel(g_ref, slope_ref, after_ref, gain_ref, win_ref, wout_ref,
                   dslope_ref, dafter_ref, dgain_ref, dshift_ref, dbin_ref, dbout_ref, du_ref, acc_ref):
    def put_dpre(rows, y):
        d = (y * slope_ref[:, rows].astype(F32)).astype(BF16)
        dslope_ref[:, rows] = d
        dbin_ref[:, rows] = jnp.sum(d.astype(F32), 0, keepdims=True)

    matmul_nt(g_ref, wout_ref, 512, put_dpre)

    def put_du(rows, y):
        du_ref[:, rows] = y

    matmul_nt(dslope_ref, win_ref, 256, put_du)
    dbout_ref[...] = jnp.zeros_like(dbout_ref)

    def store(rows, dh):
        g = g_ref[rows, :].astype(F32)
        dafter_ref[rows, :] = g + dh
        dbout_ref[...] += jnp.sum(g, 0, keepdims=True)

    norm_back(lambda rows: after_ref[rows, :], du_ref, gain_ref, dgain_ref, dshift_ref, acc_ref, store)


def ffn_bwd(g, slope, after, gain, win, wout):
    rows, width = after.shape
    ff = win.shape[1]
    row = lambda n: jax.ShapeDtypeStruct((1, n), F32)
    return pl.pallas_call(
        ffn_bwd_kernel,
        out_shape=[
            jax.ShapeDtypeStruct((rows, ff), BF16),
            jax.ShapeDtypeStruct((rows, width), F32),
            row(width), row(width), row(ff), row(width),
        ],
        in_specs=[VMEM_SPEC] * 6,
        out_specs=[VMEM_SPEC] * 6,
        scratch_shapes=[pltpu.VMEM((rows, width), F32), pltpu.VMEM((2, 8, width), F32)],
        compiler_params=params(),
        name="ffn_backward",
    )(g, slope, after, gain, win, wout)


def per_device(on_boxes, tokens, out_grad, actions, segments, frame_mask, embed,
               ln1_gain, ln1_shift, spatial_qkv, spatial_out,
               ln2_gain, ln2_shift, temporal_qkv, temporal_out,
               ln3_gain, ln3_shift, ffn_in, ffn_in_bias, ffn_out, ffn_out_bias):
    frames_dev, tile_tokens, width = tokens.shape
    n_frame = lax.axis_size("frame")
    n_tile = lax.axis_size("tile")
    f = lax.axis_index("frame")
    t = lax.axis_index("tile")
    frames = frames_dev * n_frame
    place = tile_tokens // n_frame
    rows = frames_dev * tile_tokens
    row = lambda v: v[None, :]

    mats = (spatial_qkv, spatial_out, temporal_qkv, temporal_out, ffn_in, ffn_out)

    grad4 = out_grad.reshape(frames_dev, n_frame, place, width)
    blocks = n_frame * n_tile

    def turn(x, forward):
        x = x.reshape(blocks, rows // blocks, width)
        if forward:
            y = x.reshape(n_tile, n_frame, -1, width).transpose(1, 0, 2, 3)
            y = lax.all_to_all(y.reshape(x.shape), ("frame", "tile"), 0, 0, tiled=True)
        else:
            y = lax.all_to_all(x, ("frame", "tile"), 0, 0, tiled=True)
            y = y.reshape(n_frame, n_tile, -1, width).transpose(1, 0, 2, 3)
        return y.reshape(rows, width)

    vecs = [row(v) for v in (ln1_gain, ln1_shift, ln2_gain, ln2_shift, ln3_gain, ln3_shift, ffn_in_bias, ffn_out_bias)]
    if on_boxes:
        *rest, small, tokens_grad, result = layer(
            mats, tokens, grad4, row(actions), row(segments), row(frame_mask), embed, vecs)
        summed = rest[6:]
        *outs, tokens_grad, result = widen(
            summed, small, tokens_grad, result, embed.shape[0], ffn_in_bias.shape[0])
        summed, d_embed = outs[:6], outs[6]
        dg1, ds1, dg2, ds2, dg3, ds3, d_bout, d_bin = (x[0] for x in outs[7:])
    else:
        action = lax.dynamic_index_in_dim(actions, t, keepdims=False)
        added = lax.dynamic_slice_in_dim(embed, action, 1, 0)
        one_hot = (action == jnp.arange(embed.shape[0], dtype=jnp.int32)).astype(F32)[:, None]
        number = jnp.arange(rows, dtype=jnp.int32)
        of_frame, of_place = number // place, number % place
        seg_row = jnp.repeat(segments, place)
        open_row = jnp.repeat(frame_mask, place)
        allowed = (
            (seg_row[:, None] == seg_row[None, :])
            & (of_place[:, None] == of_place[None, :])
            & (of_frame[None, :] <= of_frame[:, None])
            & ((open_row[None, :] == 1) | (of_frame[None, :] == of_frame[:, None]))
        )
        bias = jnp.where(allowed, 0.0, -1e30).astype(F32)
        nothing = jnp.zeros((1, width), F32)
        w_qs, w_os, w_qt, w_ot, w_in, w_out = (lax.all_gather(m, "frame", axis=0, tiled=True) for m in mats)
        base1 = lax.all_to_all(tokens, "tile", 0, 0, tiled=True).reshape(rows, width)
        g = lax.all_to_all(grad4.transpose(1, 0, 2, 3), "frame", 0, 0, tiled=True).reshape(rows, width)
        unit1, qkv1, mixed1, after1 = attn_fwd(
            base1, added, vecs[0], vecs[1], w_qs, w_os, None, BF16, "spatial_forward")
        base2 = turn(after1, True)
        unit2, qkv2, mixed2, after2 = attn_fwd(
            base2, nothing, vecs[2], vecs[3], w_qt, w_ot, bias, F32, "temporal_forward")
        unit3 = plain_norm(after2, ln3_gain, ln3_shift).astype(BF16)
        pre = jnp.dot(unit3, w_in, preferred_element_type=F32) + ffn_in_bias
        th = jnp.tanh(GELU_A * (pre + GELU_B * pre * pre * pre))
        act = (0.5 * pre * (1.0 + th)).astype(BF16)
        slope = 0.5 * (1.0 + th) + 0.5 * pre * (1.0 - th * th) * GELU_A * (1.0 + 3.0 * GELU_B * pre * pre)
        slope = slope.astype(BF16)
        result = after2 + jnp.dot(act, w_out, preferred_element_type=F32) + ffn_out_bias
        result = result.astype(BF16).reshape(n_frame, frames_dev, place, width)
        result = lax.all_to_all(result, "frame", 0, 0, tiled=True).transpose(1, 0, 2, 3)
        d_pre, d_after2, dg3, ds3, d_bin, d_bout = ffn_bwd(g, slope, after2, vecs[4], w_in, w_out)
        low2, d_qkv2, d_after1, dg2, ds2 = attn_bwd(
            base2, nothing, vecs[2], w_qt, w_ot, d_after2, qkv2, bias, BF16, "temporal_backward")
        d_out1 = turn(d_after1, False)
        low1, d_qkv1, d_start, dg1, ds1 = attn_bwd(
            base1, added, vecs[0], w_qs, w_os, d_out1, qkv1, None, F32, "spatial_backward")
        tokens_grad = d_start.astype(BF16).reshape(n_tile, tile_tokens, width)
        tokens_grad = lax.all_to_all(tokens_grad, "tile", 0, 0, tiled=True)
        d_embed = one_hot * jnp.sum(d_start, 0, keepdims=True)
        pairs = ((unit1, d_qkv1), (mixed1, low1), (unit2, d_qkv2), (mixed2, low2), (unit3, d_pre), (act, g))
        summed = []
        for a, b in pairs:
            part = lax.dot_general(a, b, (((0,), (0,)), ((), ())), preferred_element_type=F32)
            part = lax.psum_scatter(part, "frame", scatter_dimension=0, tiled=True)
            summed.append(lax.psum(part.astype(BF16), "tile").astype(F32))
        d_embed, dg1, ds1, dg2, ds2, dg3, ds3, d_bin, d_bout = lax.psum(
            (d_embed, dg1[0], ds1[0], dg2[0], ds2[0], dg3[0], ds3[0], d_bin[0], d_bout[0]), ("frame", "tile"))

    result = result.reshape(tokens.shape)
    return (result, tokens_grad, d_embed, dg1, ds1, summed[0], summed[1], dg2, ds2, summed[2], summed[3],
            dg3, ds3, summed[4], d_bin, summed[5], d_bout)


def solution(mesh):
    shard = P("frame", "tile", None)
    mat = P("frame", None)
    rep = P()
    in_specs = (shard, shard, P("frame"), rep, rep, rep, rep, rep, mat, mat, rep, rep, mat, mat,
                rep, rep, mat, rep, mat, rep)
    out_specs = (shard, shard, rep, rep, rep, mat, mat, rep, rep, mat, mat, rep, rep, mat, rep, mat, rep)
    on_boxes = mesh.shape["frame"] == 8 and mesh.shape["tile"] == 4
    return jax.shard_map(
        functools.partial(per_device, on_boxes),
        mesh=mesh, in_specs=in_specs, out_specs=out_specs, check_vma=False)
```

```python
import functools

import jax
import jax.numpy as jnp
from jax import lax
from jax.experimental import pallas as pl
from jax.experimental.pallas import tpu as pltpu
from jax.sharding import PartitionSpec as P

HD = 64
LANES = 128
EPS = 1e-5
MESH = pl.DeviceIdType.MESH
F32 = jnp.float32
BF16 = jnp.bfloat16
VMEM_SPEC = pl.BlockSpec(memory_space=pltpu.VMEM)
HBM_SPEC = pl.BlockSpec(memory_space=pltpu.HBM)


def params(**kw):
    return pltpu.CompilerParams(vmem_limit_bytes=60 * 1024 * 1024, **kw)


def at(j, size):
    return pl.ds(pl.multiple_of(j * size, size), size)


def each(n, fn):
    def step(i, carry):
        fn(i)
        return carry

    lax.fori_loop(0, n, step, 0)


def dot(a, b):
    return jnp.dot(a, b, preferred_element_type=F32)


def dot_nt(a, b):
    return lax.dot_general(a, b, (((1,), (1,)), ((), ())), preferred_element_type=F32)


def dot_tn(a, b):
    return lax.dot_general(a, b, (((0,), (0,)), ((), ())), preferred_element_type=F32)


def normed(h):
    cen = h - jnp.mean(h, -1, keepdims=True)
    inv = lax.rsqrt(jnp.mean(cen * cen, -1, keepdims=True) + EPS)
    return cen * inv, inv


ROWS = 32


def norm_rows(load, gain_ref, shift_ref, unit_ref):
    def step(i):
        rows = at(i, ROWS)
        xhat, _ = normed(load(rows))
        unit_ref[rows, :] = (xhat * gain_ref[...] + shift_ref[...]).astype(BF16)

    each(unit_ref.shape[0] // ROWS, step)


def fold(x):
    return jnp.sum(x.reshape(x.shape[0] // 8, 8, x.shape[1]), 0)


def norm_back(load, du_ref, gain_ref, dgain_ref, dshift_ref, acc_ref, store):
    acc_ref[...] = jnp.zeros_like(acc_ref)

    def step(i):
        rows = at(i, ROWS)
        xhat, inv = normed(load(rows))
        du = du_ref[rows, :]
        acc_ref[0] += fold(du * xhat)
        acc_ref[1] += fold(du)
        dx = du * gain_ref[...]
        dh = inv * (
            dx - jnp.mean(dx, -1, keepdims=True) - xhat * jnp.mean(dx * xhat, -1, keepdims=True)
        )
        store(rows, dh)

    each(du_ref.shape[0] // ROWS, step)
    dgain_ref[...] = jnp.sum(acc_ref[0], 0, keepdims=True)
    dshift_ref[...] = jnp.sum(acc_ref[1], 0, keepdims=True)


def head_masks():
    lane = lax.broadcasted_iota(jnp.int32, (1, LANES), 1)
    low = jnp.where(lane < HD, 1.0, 0.0)
    return low.astype(BF16), (1.0 - low).astype(BF16)


def head_probs(qm, k, bias_ref):
    s = dot_nt(qm, k) * (HD**-0.5)
    if bias_ref is not None:
        s = s + bias_ref[...]
    e = jnp.exp(s - jnp.max(s, -1, keepdims=True))
    return e * (1.0 / jnp.sum(e, -1, keepdims=True))


def attention(qkv_ref, bias_ref, mixed_ref, part=0, parts=1):
    width = mixed_ref.shape[1]
    per = width // LANES
    count = per // parts
    masks = head_masks()

    def pair(p):
        p = p + part * count
        q, k, v = (qkv_ref[:, at(p + i * per, LANES)] for i in range(3))
        out = 0.0
        for m in masks:
            out = out + dot(head_probs(q * m, k, bias_ref).astype(BF16), v * m)
        mixed_ref[:, at(p, LANES)] = out.astype(BF16)

    each(count, pair)


def attention_back(qkv_ref, bias_ref, dmix_ref, dqkv_ref):
    width = dmix_ref.shape[1]
    per = width // LANES
    masks = head_masks()
    scale = HD**-0.5

    def pair(p):
        q, k, v = (qkv_ref[:, at(p + i * per, LANES)] for i in range(3))
        dm = dmix_ref[:, at(p, LANES)]
        dq = dk = dv = 0.0
        for m in masks:
            qm = q * m
            dmm = dm * m
            probs = head_probs(qm, k, bias_ref)
            dp = dot_nt(dmm, v)
            ds = probs * (dp - jnp.sum(probs * dp, -1, keepdims=True))
            ds = ds.astype(BF16)
            dq = dq + dot(ds, k * m)
            dk = dk + dot_tn(ds, qm)
            dv = dv + dot_tn(probs.astype(BF16), dmm)
        dqkv_ref[:, at(p, LANES)] = (dq * scale).astype(BF16)
        dqkv_ref[:, at(p + per, LANES)] = (dk * scale).astype(BF16)
        dqkv_ref[:, at(p + 2 * per, LANES)] = dv.astype(BF16)

    each(per, pair)


def matmul(x_ref, w_ref, block, store):
    def step(j):
        cols = at(j, block)
        store(cols, dot(x_ref[...], w_ref[:, cols]))

    each(w_ref.shape[1] // block, step)


def matmul_nt(x_ref, w_ref, block, store):
    def step(j):
        rows = at(j, block)
        store(rows, dot_nt(x_ref[...], w_ref[rows, :]))

    each(w_ref.shape[0] // block, step)


def wgrad(core, shard, left, left_x, right, right_x, out, lt):
    tok = left.shape[0]
    col_blocks = right.shape[1] // TILE
    lt = lt.at[:, pl.ds(0, 2 * tok)]
    for rb in range(shard // 128):
        for q in range(4):
            cols = pl.ds(pl.multiple_of((2 * q + core) * shard + rb * 128, 128), 128)
            lt[q * 128 : (q + 1) * 128, :tok] = left[:, cols].T
            cols = pl.ds(q * shard + rb * 128, 128)
            lt[q * 128 : (q + 1) * 128, tok:] = left_x[:, cols].T

        def step(j, rb=rb):
            cols = at(j, TILE)
            y = dot(lt[:, :tok], right[:, cols]) + dot(lt[:, tok:], right_x[:, cols])
            y = y.astype(BF16)
            for q in range(4):
                out[rb * col_blocks + j, q] = y[q * 128 : (q + 1) * 128]

        each(col_blocks, step)


GELU_A = 0.7978845608
GELU_B = 0.044715


def xor(a, b):
    bit = lax.rem(a // b, 2)
    return a + b - 2 * b * bit


def greet(partners):
    barrier = pltpu.get_barrier_semaphore()
    for p in partners:
        pl.semaphore_signal(barrier, inc=1, device_id=p, device_id_type=MESH)
    pl.semaphore_wait(barrier, len(partners))


def remote(src, dst, ssem, rsem, dev):
    return pltpu.make_async_remote_copy(
        src_ref=src, dst_ref=dst, send_sem=ssem, recv_sem=rsem, device_id=dev, device_id_type=MESH
    )


def xor_any(a, bits):
    for b in (1, 2, 4, 8, 16):
        if bits & b:
            a = xor(a, b)
    return a


TILE = 1024
SLOTS = 4
AHEAD = 3
AHEAD2 = 3
PRE = 512
LAG = 2
PACE = (6, 7, 8, 10, 12, 13, 13, 14, 14, 16, 18)
DEEP = 3
RING = 6


def gather_chunks(shapes):
    out = []
    for i, (rows, cols) in enumerate(shapes):
        step = rows
        while step * cols > (128 if i < 4 else 64) * 1024 and step % 32 == 0:
            step //= 2
        out += [(i, r, step) for r in range(0, rows, step)]
    return out


def weight_tiles(shapes):
    return [
        (i, r, c)
        for i, (rows, cols) in enumerate(shapes)
        for r in range(0, rows, TILE)
        for c in range(0, cols, TILE)
    ]


def add_into(dst, a, b):
    def step(i):
        r = at(i, 16)
        dst[r, :] = (a[r, :].astype(F32) + b[r, :].astype(F32)).astype(dst.dtype)

    each(dst.shape[0] // 16, step)


def layer_kernel(chunks, tiles, units, *refs):
    shards = refs[:6]
    (tokens, grad4, actions, segments, frame_mask, embed,
     gain1, shift1, gain2, shift2, gain3, shift3, b_in, b_out) = refs[6:20]
    full = refs[20:26]
    outs = refs[26:32]
    small_out, tokens_grad, result = refs[32:35]
    (base1, unit1, qkv1, mixed1, base2, unit2, qkv2, mixed2, after2, unit3, slope, g2d, act,
     wt, gbuf, r1, r2, zin, zpeer, zin2, zpeer2, act_x, g_x, dpre_x, unit3_x, mix2_x, low2_x, unit2_x, dqkv2_x,
     mix1_x, low1_x, unit1_x, du, y_own, y_in, du_in, low2, low1, dmix, dqkv,
     out1, in2, g_in, res_out, turn_in, bias, added, b_half, db_half, sm, smr, lt, acc, emb,
     ssem, rsem, bsem, tsem, z3s, z3r, z3l, f7s, f7r, f7l, turn_s, turn_r, turn_l, back_s, back_r, back_l,
     s1s, s1r, s2s, s2r, zs, zr, zps, zpr, zs2, zr2, zps2, zpr2, osem, sms, smrs, xs, xr, pairs, pairr,
     o7s, o7r, o7l, t3s, t3r, t3l) = refs[35:]
    turn_out, dqkv1_x = out1, qkv2
    f = lax.axis_index("frame")
    t = lax.axis_index("tile")
    core = lax.rem(f, 2)
    chip = f // 2
    odd = lax.rem(t, 2)
    leaf = (t == 0) | (t == 3)
    inner = jnp.logical_not(leaf)
    fx, fy, sib = xor(f, 2), xor(f, 4), xor(f, 1)
    first = fx + (fy - fx) * odd
    second = fy + (fx - fy) * odd
    diag = xor_any(f, 6)
    cx, cy, cd = xor(chip, 1), xor(chip, 2), xor_any(chip, 3)
    to_sib, to_first, to_second = (sib, t), (first, t), (second, t)
    to_x, to_y, to_z, to_peer = (fx, t), (fy, t), (f, xor(t, 1)), (f, 3 - t)
    others = [(a, b) for a in range(8) for b in range(4) if a or b]
    greet([(xor_any(f, a), xor_any(t, b)) for a, b in others])

    def split_ffn(a):
        return a >= 4

    def shard_rows(a):
        return full[a].shape[0] // 8

    def piece(k, owner):
        a, r, rows = chunks[k]
        return full[a].at[pl.ds(pl.multiple_of(owner * shard_rows(a) + r, 16), rows)]

    def own(k):
        a, r, rows = chunks[k]
        return piece(k, f) if split_ffn(a) else shards[a].at[pl.ds(r, rows)]

    def ways(k):
        if split_ffn(chunks[k][0]) and k % 2:
            return second, to_second, first, to_first
        return first, to_first, second, to_second

    def copy(k, kind):
        one, to_one, other, to_other = ways(k)
        direct = split_ffn(chunks[k][0])
        dev = (to_one, to_other, to_other if direct else to_z, to_sib, to_sib, to_sib, to_sib)[kind]
        owner = (f, one, f if direct else one, f, one, diag, other)[kind]
        src = own(k) if kind in (0, 3) or (kind == 2 and direct) else piece(k, owner)
        return remote(src, piece(k, owner), ssem.at[k, kind], rsem.at[k, kind], dev)

    def arrived(k, kind):
        one, _, other, _ = ways(k)
        owner = (one, diag, other, sib, xor(one, 1), xor(diag, 1), xor(other, 1))[kind]
        dst = piece(k, owner)
        remote(dst, dst, ssem.at[k, kind], rsem.at[k, kind], to_sib).wait_recv()

    n_chunks = len(chunks)
    progress = [0, 0, AHEAD]

    def relay_to(k):
        while progress[1] < min(k, progress[0]):
            k1 = progress[1]
            progress[1] += 1
            for kind in (1, 2):
                arrived(k1, kind)
                copy(k1, kind + 4).start()

    def advance(hops, lag=LAG):
        while progress[0] < min(hops, n_chunks):
            k = progress[0]
            progress[0] += 1
            early = (3, 2) if split_ffn(chunks[k][0]) else (3,)
            for kind in early:
                copy(k, kind).start()
            arrived(k, 0)
            ahead = AHEAD if k < 9 else AHEAD2
            while progress[2] < min(k + 1 + ahead, n_chunks):
                copy(progress[2], 0).start()
                progress[2] += 1
            for kind in (1, 2, 4):
                if kind not in early:
                    copy(k, kind).start()
            relay_to(k + 1 - lag)

    def complete(a):
        ks = [k for k in range(n_chunks) if chunks[k][0] == a]
        advance(ks[-1] + 2)
        relay_to(ks[-1] + 1)
        for k in ks:
            for kind in (3, 4, 5, 6):
                arrived(k, kind)

    bounce = []
    for a, shard in enumerate(shards):
        for r in range(0, shard_rows(a), 128):
            for c in range(0, full[a].shape[1], TILE):
                i = len(bounce)
                via = wt.at[2 + i // 8, pl.ds(i % 8 * 128, 128)]
                if a == 4:
                    cuts = [(r, (c // 256 + b) * 512 + 256 * odd, 256, b * 256) for b in range(4)]
                else:
                    cuts = [(r + 256 * odd if a == 5 else r, c, TILE, 0)]
                bounce.append((a, r, c, via, cuts))

    def bounce_in(i):
        a, _, _, via, cuts = bounce[i]
        return [
            pltpu.make_async_copy(
                shards[a].at[pl.ds(row if isinstance(row, int) else pl.multiple_of(row, 128), 128),
                             pl.ds(col if isinstance(col, int) else pl.multiple_of(col, 256), wide)],
                via.at[:, pl.ds(place, wide)], bsem.at[i, b])
            for b, (row, col, wide, place) in enumerate(cuts)
        ]

    def bounce_out(i):
        a, r, c, via, _ = bounce[i]
        row = pl.multiple_of(f * shard_rows(a) + r, 128)
        return pltpu.make_async_copy(via, full[a].at[pl.ds(row, 128), pl.ds(c, TILE)], bsem.at[i, 0])

    def tile_load(i):
        a, r, c = tiles[i]
        src = full[a].at[pl.ds(r, TILE), pl.ds(c, TILE)]
        return pltpu.make_async_copy(src, wt.at[slot_of(i)], tsem.at[i])

    def slot_of(i):
        return i % SLOTS if i < 12 else (i + 2) % SLOTS

    def load(ids):
        for i in ids:
            if i < len(tiles):
                tile_load(i).start()

    n = len(units)

    def hop(u):
        return (to_x, cx, to_y, cy) if u % 2 == 0 else (to_y, cy, to_x, cx)

    def part(u, p):
        _, _, _, rows, unit, top = units[u]
        return gbuf.at[unit // 4 % 2, unit % 4, p, pl.ds(top, rows)]

    def slot(ref, u, *more):
        return ref.at[(u % RING, *more, pl.ds(0, units[u][3]))]

    def step1(u):
        dev1, p1, _, _ = hop(u)
        return (
            remote(part(u, cd), slot(r1, u, 1), s1s.at[u, 1], s1r.at[u, 1], dev1),
            remote(part(u, p1), slot(r1, u, 0), s1s.at[u, 0], s1r.at[u, 0], dev1),
        )

    def step2(u):
        _, _, dev2, p2 = hop(u)
        return remote(part(u, p2), slot(r2, u), s2s.at[u], s2r.at[u], dev2)

    def along(u):
        return remote(part(u, chip), slot(zin, u), zs.at[u], zr.at[u], to_z)

    def across(u):
        return remote(part(u, chip), slot(zpeer, u), zps.at[u], zpr.at[u], to_peer)

    def halves(u):
        return split_ffn(units[u][0])

    def across2(u):
        return remote(slot(zin, u), zpeer2.at[u], zps2.at[u], zpr2.at[u], to_peer)

    def along2(u):
        return remote(slot(zin, u), zin2.at[u], zs2.at[u], zr2.at[u], to_z)

    def emit(u, src, half=None, k=0):
        a, r, c, rows, _, _ = units[u]
        if a == 5:
            row = pl.multiple_of(r + 256 * half, 128)
            return [pltpu.make_async_copy(src, outs[a].at[pl.ds(row, rows), pl.ds(c, TILE)], osem.at[u, k])]
        if a == 4:
            return [
                pltpu.make_async_copy(
                    src.at[:, pl.ds(b * 256, 256)],
                    outs[a].at[pl.ds(r, rows), pl.ds(pl.multiple_of((c // 256 + b) * 512 + 256 * half, 256), 256)],
                    osem.at[u, k + b])
                for b in range(4)
            ]
        return [pltpu.make_async_copy(src, outs[a].at[pl.ds(r, rows), pl.ds(c, TILE)], osem.at[u, k])]

    state = {"ready": 0, "issued": 0, "done": 0, "step": 0}

    def issue():
        while state["issued"] < min(state["ready"], state["done"] + DEEP):
            for c in step1(state["issued"]):
                c.start()
            state["issued"] += 1

    def offer(count):
        state["ready"] += count
        issue()

    def reduce_step():
        s = state["step"]
        state["step"] += 1
        u = s
        if u < n:
            assert u < state["issued"]
            p2 = hop(u)[3]
            far, near = step1(u)
            far.wait_recv()
            add_into(part(u, p2), part(u, p2), slot(r1, u, 1))
            step2(u).start()
            near.wait_recv()
            add_into(part(u, chip), part(u, chip), slot(r1, u, 0))
            state["done"] += 1
            issue()
        u = s - 1
        if 0 <= u < n:
            step2(u).wait_recv()
            add_into(part(u, chip), part(u, chip), slot(r2, u))

            @pl.when(leaf)
            def _(u=u):
                along(u).start()

        u = s - 2
        if 0 <= u < n:
            @pl.when(inner)
            def _(u=u):
                along(u).wait_recv()
                if halves(u):
                    across2(u).start()
                else:
                    add_into(part(u, chip), part(u, chip), slot(zin, u))
                across(u).start()

        u = s - 5
        if 0 <= u < n:
            for c in step1(u):
                c.wait_send()
            step2(u).wait_send()

            @pl.when(inner)
            def _(u=u):
                along(u).wait_send()
                if halves(u):
                    along2(u).wait_send()

            if halves(u):
                wait_all(emit(u, part(u, chip), odd, 0))
                wait_all(emit(u, slot(zin, u), odd, 4))
            else:
                wait_all(emit(u, part(u, chip)))

        u = s - 3
        if 0 <= u < n:
            @pl.when(inner)
            def _(u=u):
                across(u).wait()
                if halves(u):
                    across2(u).wait()
                    add_into(part(u, chip), part(u, chip), zpeer2.at[u])
                    add_into(slot(zin, u), slot(zin, u), slot(zpeer, u))
                    along2(u).start()
                    start_all(emit(u, part(u, chip), odd, 0))
                    start_all(emit(u, slot(zin, u), 1 - odd, 4))
                else:
                    add_into(part(u, chip), part(u, chip), slot(zpeer, u))
                    start_all(emit(u, part(u, chip)))
                along(u).start()

        u = s - 4
        if 0 <= u < n:
            @pl.when(leaf)
            def _(u=u):
                along(u).wait()
                if halves(u):
                    along2(u).wait_recv()
                    start_all(emit(u, slot(zin, u), 1 - odd, 0))
                    start_all(emit(u, zin2.at[u], odd, 4))
                else:
                    start_all(emit(u, slot(zin, u)))

    def reduce_to(s):
        while state["step"] < s:
            reduce_step()

    def share(i, left, left_x, right, right_x):
        shard = left.shape[1] // 8
        copies = [
            remote(left.at[:, pl.ds(pl.multiple_of((2 * p + 1 - core) * shard, shard), shard)],
                   left_x.at[:, pl.ds(p * shard, shard)], xs.at[i, p], xr.at[i, p], to_sib)
            for p in range(4)
        ]
        copies.append(remote(right, right_x, xs.at[i, 4], xr.at[i, 4], to_sib))
        for c in copies:
            c.start()
        return copies

    def wait_all(copies):
        for c in copies:
            c.wait()

    def rows_of(ref, i):
        return ref.at[pl.ds(pl.multiple_of(i * 64, 64), 64)]

    def over_tile(src, dst, ssems, rsems, lsem):
        ds = [xor_any(t, i) for i in (1, 2, 3)]
        own = pltpu.make_async_copy(src(t), dst(t), lsem)
        go = [remote(src(d), dst(t), ssems.at[i], rsems.at[i], (f, d)) for i, d in enumerate(ds)]
        end = [remote(src(d), dst(d), ssems.at[i], rsems.at[i], (f, d)) for i, d in enumerate(ds)]
        return [own] + go, [own] + end

    def over_frame(src, dst, ssems, rsems, lsem):
        ds = [xor_any(f, i) for i in range(1, 8)]
        own = pltpu.make_async_copy(src(f), dst(f), lsem)
        go = [remote(src(d), dst(f), ssems.at[i], rsems.at[i], (d, t)) for i, d in enumerate(ds)]
        end = [remote(src(d), dst(d), ssems.at[i], rsems.at[i], (d, t)) for i, d in enumerate(ds)]
        return [own] + go, [own] + end

    def over_both(src, dst, ssems, rsems, lsem):
        ds = [(xor_any(f, a), xor_any(t, b)) for a, b in others]
        own = pltpu.make_async_copy(src(f, t), dst(f, t), lsem)
        go = [remote(src(*d), dst(f, t), ssems.at[i], rsems.at[i], d) for i, d in enumerate(ds)]
        end = [remote(src(*d), dst(*d), ssems.at[i], rsems.at[i], d) for i, d in enumerate(ds)]
        return [own] + go, [own] + end

    def start_all(copies):
        for c in copies:
            c.start()

    def split(load_rows, dst):
        def step(i):
            dst[pl.ds(4 * i, 4)] = load_rows(at(i, ROWS)).reshape(4, 8, TILE).astype(BF16)

        each(dst.shape[0] // 4, step)

    def join(src, dst):
        def step(i):
            dst[at(i, ROWS), :] = src[pl.ds(4 * i, 4)].astype(F32).reshape(ROWS, TILE).astype(BF16)

        each(src.shape[0] // 4, step)

    def to_pair(i, src, dst):
        return remote(src, dst, pairs.at[i], pairr.at[i], to_z)

    tok_go, tok_end = over_tile(lambda d: tokens.at[d], lambda d: rows_of(base1, d), z3s, z3r, z3l)
    start_all(tok_go)
    for k in range(AHEAD):
        copy(k, 0).start()
    for i in range(len(bounce)):
        start_all(bounce_in(i))
    grad_go, grad_end = over_frame(
        lambda d: grad4.at[:, d], lambda d: g_in.at[pl.ds(4 * d, 4)], f7s, f7r, f7l)

    which = jnp.sum(jnp.where(lax.broadcasted_iota(jnp.int32, (1, 4), 1) == t, actions[...], 0), -1, keepdims=True)
    hot = jnp.where(lax.broadcasted_iota(jnp.int32, (8, 1), 0) == which, 1.0, 0.0)
    added[...] = jnp.sum(hot * embed[...], 0, keepdims=True)
    n_frames = segments.shape[1]
    n_rows = bias.shape[0]
    place = n_rows // n_frames

    def column(ref):
        a = lax.broadcasted_iota(jnp.int32, (n_frames, n_frames), 0)
        b = lax.broadcasted_iota(jnp.int32, (n_frames, n_frames), 1)
        return jnp.sum(jnp.where(a == b, ref[...].astype(F32), 0.0), 1, keepdims=True)

    by_row = lax.broadcasted_iota(jnp.int32, (n_rows, n_frames), 0) // place
    by_row = by_row == lax.broadcasted_iota(jnp.int32, (n_rows, n_frames), 1)
    by_col = lax.broadcasted_iota(jnp.int32, (n_frames, n_rows), 1) // place
    by_col = by_col == lax.broadcasted_iota(jnp.int32, (n_frames, n_rows), 0)
    seg_q = jnp.sum(jnp.where(by_row, segments[...].astype(F32), 0.0), 1, keepdims=True)
    seg_k = jnp.sum(jnp.where(by_col, column(segments), 0.0), 0, keepdims=True)
    open_k = jnp.sum(jnp.where(by_col, column(frame_mask), 0.0), 0, keepdims=True)
    row_q = lax.broadcasted_iota(jnp.int32, (n_rows, n_rows), 0)
    row_k = lax.broadcasted_iota(jnp.int32, (n_rows, n_rows), 1)
    allowed = (
        (seg_q == seg_k)
        & (lax.rem(row_q, place) == lax.rem(row_k, place))
        & (row_k // place <= row_q // place)
        & ((open_k == 1.0) | (row_k == row_q))
    )
    bias[...] = jnp.where(allowed, 0.0, -1e30)

    for b in range(8):
        b_half[:, b * 256 : (b + 1) * 256] = b_in[:, pl.ds(pl.multiple_of(b * 512 + 256 * odd, 256), 256)]
    advance(1)
    for i in range(len(bounce)):
        wait_all(bounce_in(i))
        bounce_out(i).start()
    wait_all(tok_end)
    norm_rows(lambda rows: base1[rows, :].astype(F32) + added[...], gain1, shift1, unit1)
    start_all(grad_go)
    for i in range(len(bounce)):
        bounce_out(i).wait()

    def project(unit, ids, out_ref):
        for j, i in enumerate(ids):
            tile_load(i).wait()

            def put(cols, y, j=j):
                out_ref[:, j * TILE : (j + 1) * TILE] = y.astype(BF16)

            matmul(unit, wt.at[i % SLOTS], TILE, put)

    complete(0)
    load((0, 1, 2))
    project(unit1, (0, 1, 2), qkv1)
    advance(PACE[0])
    complete(1)
    load((3,))
    attention(qkv1, None, mixed1, 0, 2)
    advance(PACE[1])
    attention(qkv1, None, mixed1, 1, 2)
    advance(PACE[2])
    tile_load(3).wait()

    def put_after1(cols, y):
        du[:, cols] = y + base1[:, cols].astype(F32) + added[:, cols]

    matmul(mixed1, wt.at[3], TILE, put_after1)
    split(lambda rows: du[rows, :], out1)

    turn_go, turn_end = over_both(
        lambda a, b: out1.at[8 * b + a], lambda a, b: in2.at[4 * a + b], turn_s, turn_r, turn_l)
    start_all(turn_go)
    advance(PACE[3])
    complete(2)
    load((4, 5, 6))
    complete(3)
    load((7,))
    advance(PACE[4])
    wait_all(turn_end)
    join(in2, base2)
    wait_all(grad_end)
    join(g_in, g2d.at[pl.ds(0, n_rows)])
    g_pair = to_pair(0, g2d.at[pl.ds(0, n_rows)], g2d.at[pl.ds(n_rows, n_rows)])
    g_pair.start()
    norm_rows(lambda rows: base2[rows, :].astype(F32), gain2, shift2, unit2)
    advance(PACE[5])
    project(unit2, (4, 5, 6), qkv2)
    advance(PACE[6])
    attention(qkv2, bias, mixed2, 0, 2)
    advance(PACE[7])
    attention(qkv2, bias, mixed2, 1, 2)
    advance(PACE[8])
    tile_load(7).wait()

    def put_after2(cols, y):
        after2[:, cols] = y + base2[:, cols].astype(F32)

    matmul(mixed2, wt.at[3], TILE, put_after2)
    mine, theirs = pl.ds(0, n_rows), pl.ds(n_rows, n_rows)
    norm_rows(lambda rows: after2[rows, :], gain3, shift3, unit3.at[mine])
    unit_pair = to_pair(1, unit3.at[mine], unit3.at[theirs])
    unit_pair.start()
    complete(4)
    load((8, 9))

    for side in (0, 1):
        if side:
            unit_pair.wait()
            advance(PACE[9])
        for j in range(2):
            if side == 0:
                tile_load(8 + j).wait()

            def put_pre(cols, y, j=j, side=side):
                cols = pl.ds(pl.multiple_of(cols.start + j * TILE, PRE), PRE)
                rows = theirs if side else mine
                v = y + b_half[:, cols]
                th = jnp.tanh(GELU_A * (v + GELU_B * v * v * v))
                act[rows, cols] = (0.5 * v * (1.0 + th)).astype(BF16)
                rise = 0.5 * (1.0 + th) + 0.5 * v * (1.0 - th * th) * GELU_A * (1.0 + 3.0 * GELU_B * v * v)
                slope[rows, cols] = rise.astype(BF16)

            matmul(unit3.at[theirs if side else mine], wt.at[j], PRE, put_pre)

    g_pair.wait()
    swap4 = share(0, act, act_x, g2d, g_x)
    advance(PACE[10])
    wait_all(swap4)
    wgrad(core, act.shape[1] // 8, act, act_x, g2d, g_x, gbuf.at[0, pl.ds(0, 2)], lt)
    complete(5)
    load((10, 11))
    offer(2)

    sm[0] = jnp.zeros_like(sm[0])
    for j in range(2):
        tile_load(10 + j).wait()

        def put_dpre(rows, y, j=j):
            cols = pl.ds(pl.multiple_of(rows.start + j * TILE, 512), 512)
            d = (y * slope[:, cols].astype(F32)).astype(BF16)
            slope[:, cols] = d
            db_half[:, cols] = jnp.sum(d.astype(F32), 0, keepdims=True)

        matmul_nt(g2d, wt.at[2 + j], 512, put_dpre)
    dpre = slope
    swap3 = share(1, unit3, unit3_x, dpre, dpre_x)
    for b in range(8):
        place_b = pl.ds(pl.multiple_of(b % 2 * 512 + 256 * odd, 256), 256)
        sm[0, 15 + b // 2 : 16 + b // 2, place_b] = db_half[:, b * 256 : (b + 1) * 256]

    def back_in(side, store):
        def run(h):
            rows = at(h, 512)
            who = theirs if side else mine
            y = dot_nt(dpre[who, :TILE], wt[0, rows, :]) + dot_nt(dpre[who, TILE:], wt[1, rows, :])
            store(rows, y)

        each(TILE // 512, run)

    def put_theirs(rows, y):
        dmix[:, rows] = y.astype(BF16)

    def put_mine(rows, y):
        du[:, rows] = y

    back_in(1, put_theirs)
    du_pair = to_pair(2, dmix, du_in)
    du_pair.start()
    back_in(0, put_mine)
    load((14, 15))

    def forward_out(side, store):
        def run(h):
            cols = at(h, 512)
            who = theirs if side else mine
            store(cols, dot(act[who, :TILE], wt[2, :, cols]) + dot(act[who, TILE:], wt[3, :, cols]))

        each(TILE // 512, run)

    def put_y_theirs(cols, y):
        low1[:, cols] = y.astype(BF16)

    def put_y_mine(cols, y):
        y_own[:, cols] = y + after2[:, cols] + b_out[:, cols]

    forward_out(1, put_y_theirs)
    y_pair = to_pair(3, low1, y_in)
    y_pair.start()
    forward_out(0, put_y_mine)
    load((12, 13))
    res_go, res_end = over_frame(
        lambda d: res_out.at[pl.ds(4 * d, 4)], lambda d: result.at[:, d], o7s, o7r, o7l)
    reduce_to(1)
    du_pair.wait()

    def add_du(i):
        rows = at(i, ROWS)
        du[rows, :] = du[rows, :] + du_in[rows, :].astype(F32)

    each(n_rows // ROWS, add_du)

    def store3(rows, dh):
        g = g2d[rows, :].astype(F32)
        d = g + dh
        after2[rows, :] = d
        low2[rows, :] = d.astype(BF16)
        sm[0, 14:15, :] += jnp.sum(g, 0, keepdims=True)

    norm_back(lambda rows: after2[rows, :], du, gain3, sm.at[0, pl.ds(12, 1)], sm.at[0, pl.ds(13, 1)], acc, store3)
    dafter = after2
    swap2o = share(2, mixed2, mix2_x, low2, low2_x)
    wait_all(swap3)
    wgrad(core, TILE // 8, unit3, unit3_x, dpre, dpre_x, gbuf.at[0, pl.ds(2, 2)], lt)
    offer(2)
    reduce_to(2)
    y_pair.wait()
    split(lambda rows: y_own[rows, :] + y_in[rows, :].astype(F32), res_out)

    def back_through(first_tile, count, x_ref):
        ids = range(first_tile, first_tile + count)
        for i in ids:
            tile_load(i).wait()

        def run(h):
            rows = at(h, 512)
            parts = [
                dot_nt(x_ref[:, j * TILE : (j + 1) * TILE], wt[slot_of(i), rows, :]) for j, i in enumerate(ids)
            ]
            du[:, rows] = sum(parts[1:], parts[0])

        each(TILE // 512, run)
        load([i + SLOTS for i in ids])

    def put_mix(rows, y):
        dmix[:, rows] = y.astype(BF16)

    tile_load(12).wait()
    matmul_nt(low2, wt.at[slot_of(12)], TILE, put_mix)
    load((16,))
    reduce_to(3)
    attention_back(qkv2, bias, dmix, dqkv)
    swap2 = share(3, unit2, unit2_x, dqkv, dqkv2_x)
    reduce_to(4)
    back_through(13, 3, dqkv)

    def store2(rows, dh):
        dafter[rows, :] = dafter[rows, :] + dh

    norm_back(lambda rows: base2[rows, :].astype(F32), du, gain2, sm.at[0, pl.ds(10, 1)], sm.at[0, pl.ds(11, 1)], acc, store2)
    split(lambda rows: dafter[rows, :], turn_out)

    back_go, back_end = over_both(
        lambda a, b: turn_out.at[4 * a + b], lambda a, b: turn_in.at[8 * b + a], back_s, back_r, back_l)
    start_all(back_go)
    wait_all(swap2o)
    wgrad(core, TILE // 8, mixed2, mix2_x, low2, low2_x, gbuf.at[1, pl.ds(0, 1)], lt)
    wait_all(swap2)
    wgrad(core, TILE // 8, unit2, unit2_x, dqkv, dqkv2_x, gbuf.at[1, pl.ds(1, 3)], lt)
    offer(4)
    reduce_to(5)
    wait_all(back_end)
    join(turn_in, low1)
    swap1o = share(4, mixed1, mix1_x, low1, low1_x)
    tile_load(16).wait()
    matmul_nt(low1, wt.at[slot_of(16)], TILE, put_mix)
    reduce_to(6)
    attention_back(qkv1, None, dmix, dqkv)
    swap1 = share(5, unit1, unit1_x, dqkv, dqkv1_x)
    wait_all(swap1o)
    wgrad(core, TILE // 8, mixed1, mix1_x, low1, low1_x, gbuf.at[0, pl.ds(0, 1)], lt)
    offer(1)
    reduce_to(7)
    back_through(17, 3, dqkv)
    reduce_to(9)
    wait_all(swap1)
    wgrad(core, TILE // 8, unit1, unit1_x, dqkv, dqkv1_x, gbuf.at[0, pl.ds(1, 3)], lt)
    offer(6)
    emb[...] = jnp.zeros_like(emb)

    def store1(rows, dh):
        d = low1[rows, :].astype(F32) + dh
        low2[rows, :] = d.astype(BF16)
        emb[...] += fold(d)

    norm_back(lambda rows: base1[rows, :].astype(F32) + added[...], du, gain1, sm.at[0, pl.ds(8, 1)], sm.at[0, pl.ds(9, 1)], acc, store1)
    sm[0, 0:8, :] = hot * jnp.sum(emb[...], 0, keepdims=True)

    last_go, last_end = over_tile(lambda d: rows_of(low2, d), lambda d: tokens_grad.at[d], t3s, t3r, t3l)
    start_all(last_go)

    def small_copy(i, dev):
        return remote(sm.at[i], smr.at[i], sms.at[i], smrs.at[i], dev)

    def small_down():
        return remote(sm.at[5], smr.at[3], sms.at[5], smrs.at[3], to_z)

    hops = (to_sib, to_x, to_y)
    small_copy(0, to_sib).start()
    for i in range(3):
        reduce_to(state["step"] + 1)
        small_copy(i, hops[i]).wait()
        sm[i + 1] = sm[i] + smr[i]
        if i < 2:
            small_copy(i + 1, hops[i + 1]).start()

    @pl.when(leaf)
    def _():
        small_copy(3, to_z).start()

    reduce_to(state["step"] + 1)

    @pl.when(inner)
    def _():
        small_copy(3, to_z).wait_recv()
        sm[4] = sm[3] + smr[3]
        small_copy(4, to_peer).start()

    reduce_to(state["step"] + 1)

    @pl.when(inner)
    def _():
        small_copy(4, to_peer).wait()
        sm[5] = sm[4] + smr[4]
        small_down().start()
        small_out[...] = sm[5]

    reduce_to(n + 1)
    start_all(res_go)
    reduce_to(n + 5)

    @pl.when(leaf)
    def _():
        small_copy(3, to_z).wait()
        small_out[...] = smr[3]

    @pl.when(inner)
    def _():
        small_down().wait_send()

    wait_all(last_end)
    wait_all(res_end)
    for k in range(n_chunks):
        for kind in range(7):
            copy(k, kind).wait_send()


def layer(mats, tokens, grad4, actions, segments, frame_mask, embed, vecs):
    width = tokens.shape[2]
    rows = tokens.shape[0] * tokens.shape[1]
    ff = mats[4].shape[1]
    kept = [m.shape for m in mats[:4]] + [(mats[4].shape[0], ff // 2), (mats[5].shape[0] // 2, width)]
    fulls = [(8 * r, c) for r, c in kept]
    chunks = gather_chunks(kept)
    by_mat = weight_tiles(fulls)
    order = (5, 4, 3, 2, 1, 0)
    tiles = by_mat + [x for a in order[2:] for x in by_mat if x[0] == a]
    whole = [
        (a, r, c) for a in order
        for r in range(0, kept[a][0], 128) for c in range(0, kept[a][1], TILE)
    ]
    units = []
    for i, (a, r, c) in enumerate(whole):
        step = 64 if i >= len(whole) - 3 else 128
        units += [(a, r + top, c, step, i, top) for top in range(0, 128, step)]
    n = len(units)
    n_chunks = len(chunks)
    dma = pltpu.SemaphoreType.DMA
    blocks = (32, 8, width)
    unit = (128, TILE)
    bf = lambda *s: pltpu.VMEM(s, BF16)
    fl = lambda *s: pltpu.VMEM(s, F32)
    half = width // 2
    scratch = [
        bf(rows, width), bf(rows, width), bf(rows, 3 * width), bf(rows, width),
        bf(rows, width), bf(rows, width), bf(rows, 3 * width), bf(rows, width),
        fl(rows, width), bf(2 * rows, width), bf(2 * rows, ff // 2), bf(2 * rows, width), bf(2 * rows, ff // 2),
        bf(SLOTS, TILE, TILE), bf(2, 4, 4, *unit), bf(RING, 2, *unit), bf(RING, *unit),
        bf(RING, *unit), bf(RING, *unit), bf(4, *unit), bf(4, *unit),
        bf(2 * rows, ff // 4), bf(2 * rows, width), bf(2 * rows, ff // 2), bf(2 * rows, half),
        bf(rows, half), bf(rows, width), bf(rows, half), bf(rows, 3 * width),
        bf(rows, half), bf(rows, width), bf(rows, half),
        fl(rows, width), fl(rows, width), bf(rows, width), bf(rows, width),
        bf(rows, width), bf(rows, width), bf(rows, width), bf(rows, 3 * width),
        bf(*blocks), bf(*blocks), bf(*blocks), bf(*blocks), bf(*blocks),
        fl(rows, rows), fl(1, width), fl(1, ff // 2), fl(1, ff // 2),
        fl(6, 24, width), fl(5, 24, width), bf(512, 4 * rows), fl(2, 8, width), fl(8, width),
    ]
    sems = [
        (n_chunks, 7), (n_chunks, 7), (12, 4), (len(tiles),), (3,), (3,), (), (7,), (7,), (),
        (31,), (31,), (), (31,), (31,), (),
        (n, 2), (n, 2), (n,), (n,), (n,), (n,), (n,), (n,), (4,), (4,), (4,), (4,), (n, 8), (6,), (6,), (6, 5), (6, 5),
        (4,), (4,),
        (7,), (7,), (), (3,), (3,), (),
    ]
    return pl.pallas_call(
        functools.partial(layer_kernel, chunks, tiles, units),
        out_shape=[jax.ShapeDtypeStruct(s, BF16) for s in fulls]
        + [jax.ShapeDtypeStruct(m.shape, BF16) for m in mats]
        + [
            jax.ShapeDtypeStruct((24, width), F32),
            jax.ShapeDtypeStruct(tokens.shape, BF16),
            jax.ShapeDtypeStruct(grad4.shape, BF16),
        ],
        in_specs=[HBM_SPEC] * 8 + [VMEM_SPEC] * (4 + len(vecs)),
        out_specs=[HBM_SPEC] * 12 + [VMEM_SPEC] + [HBM_SPEC] * 2,
        scratch_shapes=scratch + [dma(s) if s else dma for s in sems],
        compiler_params=params(collective_id=0, has_side_effects=True),
        name="layer",
    )(*mats, tokens, grad4, actions, segments, frame_mask, embed, *vecs)


def widen_kernel(n_mats, *refs):
    mats, (small, grad, res) = refs[:n_mats], refs[n_mats : n_mats + 3]
    wide = refs[n_mats + 3 : 2 * n_mats + 3]
    embed_g, g1, s1, g2, s2, g3, s3, b_out, b_in, grad_out, res_out = refs[2 * n_mats + 3 : 2 * n_mats + 14]
    low = refs[2 * n_mats + 14 : 3 * n_mats + 14]
    high = refs[3 * n_mats + 14 : 4 * n_mats + 14]
    passing, isem, osem = refs[4 * n_mats + 14 :]
    ins = [pltpu.make_async_copy(m, v, isem.at[i]) for i, (m, v) in enumerate(zip(mats, low))]
    outs = [pltpu.make_async_copy(v, w, osem.at[i]) for i, (v, w) in enumerate(zip(high, wide))]
    for i, (a, b) in enumerate(((grad, grad_out), (res, res_out))):
        ins.append(pltpu.make_async_copy(a, passing.at[i], isem.at[n_mats + i]))
        outs.append(pltpu.make_async_copy(passing.at[i], b, osem.at[n_mats + i]))
    for c in ins:
        c.start()
    n_act = embed_g.shape[0]
    embed_g[...] = small[0:n_act, :]
    for i, ref in enumerate((g1, s1, g2, s2, g3, s3, b_out)):
        ref[...] = small[n_act + i : n_act + i + 1, :]
    width = small.shape[1]
    for i in range(b_in.shape[1] // width):
        b_in[:, i * width : (i + 1) * width] = small[n_act + 7 + i : n_act + 8 + i, :]
    for i in range(n_mats):
        ins[i].wait()

        def step(j, i=i):
            rows = at(j, 16)
            high[i][rows, :] = low[i][rows, :].astype(F32)

        each(low[i].shape[0] // 16, step)
        outs[i].start()
    for i in (n_mats, n_mats + 1):
        ins[i].wait()
        outs[i].start()
    for c in outs:
        c.wait()


def widen(mats, small, grad, res, n_act, ff):
    n = len(mats)
    width = small.shape[1]
    lines = [(n_act, width)] + [(1, width)] * 7 + [(1, ff)]
    res = res.reshape(grad.shape)
    return pl.pallas_call(
        functools.partial(widen_kernel, n),
        out_shape=[jax.ShapeDtypeStruct(m.shape, F32) for m in mats]
        + [jax.ShapeDtypeStruct(s, F32) for s in lines]
        + [jax.ShapeDtypeStruct(grad.shape, grad.dtype)] * 2,
        in_specs=[HBM_SPEC] * n + [VMEM_SPEC] + [HBM_SPEC] * 2,
        out_specs=[HBM_SPEC] * n + [VMEM_SPEC] * 9 + [HBM_SPEC] * 2,
        scratch_shapes=[pltpu.VMEM(m.shape, BF16) for m in mats]
        + [pltpu.VMEM(m.shape, F32) for m in mats]
        + [pltpu.VMEM((2,) + grad.shape, grad.dtype)]
        + [pltpu.SemaphoreType.DMA((n + 2,))] * 2,
        compiler_params=params(),
        name="widen",
    )(*mats, small, grad, res)


def plain_norm(h, gain, shift):
    cen = h - jnp.mean(h, -1, keepdims=True)
    inv = lax.rsqrt(jnp.mean(cen * cen, -1, keepdims=True) + EPS)
    return cen * inv * gain + shift


def attn_fwd_kernel(masked, base_ref, added_ref, gain_ref, shift_ref, wqkv_ref, wo_ref, *rest):
    if masked:
        bias_ref, unit_ref, qkv_ref, mixed_ref, after_ref = rest
    else:
        bias_ref = None
        unit_ref, qkv_ref, mixed_ref, after_ref = rest

    def load(rows):
        return base_ref[rows, :].astype(F32) + added_ref[...]

    norm_rows(load, gain_ref, shift_ref, unit_ref)

    def put_qkv(cols, y):
        qkv_ref[:, cols] = y.astype(BF16)

    matmul(unit_ref, wqkv_ref, 512, put_qkv)
    attention(qkv_ref, bias_ref, mixed_ref)

    def put_after(cols, y):
        y = y + base_ref[:, cols].astype(F32) + added_ref[:, cols]
        after_ref[:, cols] = y.astype(after_ref.dtype)

    matmul(mixed_ref, wo_ref, 512, put_after)


def attn_fwd(base, added, gain, shift, wqkv, wo, bias, out_type, name):
    rows, width = base.shape
    ins = [base, added, gain, shift, wqkv, wo] + ([bias] if bias is not None else [])
    shapes = [(width, BF16), (3 * width, BF16), (width, BF16), (width, out_type)]
    return pl.pallas_call(
        functools.partial(attn_fwd_kernel, bias is not None),
        out_shape=[jax.ShapeDtypeStruct((rows, w), d) for w, d in shapes],
        in_specs=[VMEM_SPEC] * len(ins),
        out_specs=[VMEM_SPEC] * 4,
        compiler_params=params(),
        name=name,
    )(*ins)


def attn_bwd_kernel(masked, base_ref, added_ref, gain_ref, wqkv_ref, wo_ref, dout_ref, qkv_ref, *rest):
    if masked:
        bias_ref, *rest = rest
    else:
        bias_ref = None
    dlow_ref, dqkv_ref, dbase_ref, dgain_ref, dshift_ref, dmix_ref, du_ref, acc_ref = rest

    def cast(i):
        rows = at(i, ROWS)
        dlow_ref[rows, :] = dout_ref[rows, :].astype(BF16)

    each(dlow_ref.shape[0] // ROWS, cast)

    def put_mix(rows, y):
        dmix_ref[:, rows] = y.astype(BF16)

    matmul_nt(dlow_ref, wo_ref, 512, put_mix)
    attention_back(qkv_ref, bias_ref, dmix_ref, dqkv_ref)

    def put_du(rows, y):
        du_ref[:, rows] = y

    matmul_nt(dqkv_ref, wqkv_ref, 256, put_du)

    def load(rows):
        return base_ref[rows, :].astype(F32) + added_ref[...]

    def store(rows, dh):
        dbase_ref[rows, :] = (dout_ref[rows, :].astype(F32) + dh).astype(dbase_ref.dtype)

    norm_back(load, du_ref, gain_ref, dgain_ref, dshift_ref, acc_ref, store)


def attn_bwd(base, added, gain, wqkv, wo, dout, qkv, bias, out_type, name):
    rows, width = base.shape
    ins = [base, added, gain, wqkv, wo, dout, qkv] + ([bias] if bias is not None else [])
    outs = [
        jax.ShapeDtypeStruct((rows, width), BF16),
        jax.ShapeDtypeStruct((rows, 3 * width), BF16),
        jax.ShapeDtypeStruct((rows, width), out_type),
        jax.ShapeDtypeStruct((1, width), F32),
        jax.ShapeDtypeStruct((1, width), F32),
    ]
    return pl.pallas_call(
        functools.partial(attn_bwd_kernel, bias is not None),
        out_shape=outs,
        in_specs=[VMEM_SPEC] * len(ins),
        out_specs=[VMEM_SPEC] * len(outs),
        scratch_shapes=[
            pltpu.VMEM((rows, width), BF16),
            pltpu.VMEM((rows, width), F32),
            pltpu.VMEM((2, 8, width), F32),
        ],
        compiler_params=params(),
        name=name,
    )(*ins)


def ffn_bwd_kernel(g_ref, slope_ref, after_ref, gain_ref, win_ref, wout_ref,
                   dslope_ref, dafter_ref, dgain_ref, dshift_ref, dbin_ref, dbout_ref, du_ref, acc_ref):
    def put_dpre(rows, y):
        d = (y * slope_ref[:, rows].astype(F32)).astype(BF16)
        dslope_ref[:, rows] = d
        dbin_ref[:, rows] = jnp.sum(d.astype(F32), 0, keepdims=True)

    matmul_nt(g_ref, wout_ref, 512, put_dpre)

    def put_du(rows, y):
        du_ref[:, rows] = y

    matmul_nt(dslope_ref, win_ref, 256, put_du)
    dbout_ref[...] = jnp.zeros_like(dbout_ref)

    def store(rows, dh):
        g = g_ref[rows, :].astype(F32)
        dafter_ref[rows, :] = g + dh
        dbout_ref[...] += jnp.sum(g, 0, keepdims=True)

    norm_back(lambda rows: after_ref[rows, :], du_ref, gain_ref, dgain_ref, dshift_ref, acc_ref, store)


def ffn_bwd(g, slope, after, gain, win, wout):
    rows, width = after.shape
    ff = win.shape[1]
    row = lambda n: jax.ShapeDtypeStruct((1, n), F32)
    return pl.pallas_call(
        ffn_bwd_kernel,
        out_shape=[
            jax.ShapeDtypeStruct((rows, ff), BF16),
            jax.ShapeDtypeStruct((rows, width), F32),
            row(width), row(width), row(ff), row(width),
        ],
        in_specs=[VMEM_SPEC] * 6,
        out_specs=[VMEM_SPEC] * 6,
        scratch_shapes=[pltpu.VMEM((rows, width), F32), pltpu.VMEM((2, 8, width), F32)],
        compiler_params=params(),
        name="ffn_backward",
    )(g, slope, after, gain, win, wout)


def per_device(on_boxes, tokens, out_grad, actions, segments, frame_mask, embed,
               ln1_gain, ln1_shift, spatial_qkv, spatial_out,
               ln2_gain, ln2_shift, temporal_qkv, temporal_out,
               ln3_gain, ln3_shift, ffn_in, ffn_in_bias, ffn_out, ffn_out_bias):
    frames_dev, tile_tokens, width = tokens.shape
    n_frame = lax.axis_size("frame")
    n_tile = lax.axis_size("tile")
    f = lax.axis_index("frame")
    t = lax.axis_index("tile")
    frames = frames_dev * n_frame
    place = tile_tokens // n_frame
    rows = frames_dev * tile_tokens
    row = lambda v: v[None, :]

    mats = (spatial_qkv, spatial_out, temporal_qkv, temporal_out, ffn_in, ffn_out)

    grad4 = out_grad.reshape(frames_dev, n_frame, place, width)
    blocks = n_frame * n_tile

    def turn(x, forward):
        x = x.reshape(blocks, rows // blocks, width)
        if forward:
            y = x.reshape(n_tile, n_frame, -1, width).transpose(1, 0, 2, 3)
            y = lax.all_to_all(y.reshape(x.shape), ("frame", "tile"), 0, 0, tiled=True)
        else:
            y = lax.all_to_all(x, ("frame", "tile"), 0, 0, tiled=True)
            y = y.reshape(n_frame, n_tile, -1, width).transpose(1, 0, 2, 3)
        return y.reshape(rows, width)

    vecs = [row(v) for v in (ln1_gain, ln1_shift, ln2_gain, ln2_shift, ln3_gain, ln3_shift, ffn_in_bias, ffn_out_bias)]
    if on_boxes:
        *rest, small, tokens_grad, result = layer(
            mats, tokens, grad4, row(actions), row(segments), row(frame_mask), embed, vecs)
        summed = rest[6:]
        *outs, tokens_grad, result = widen(
            summed, small, tokens_grad, result, embed.shape[0], ffn_in_bias.shape[0])
        summed, d_embed = outs[:6], outs[6]
        dg1, ds1, dg2, ds2, dg3, ds3, d_bout, d_bin = (x[0] for x in outs[7:])
    else:
        action = lax.dynamic_index_in_dim(actions, t, keepdims=False)
        added = lax.dynamic_slice_in_dim(embed, action, 1, 0)
        one_hot = (action == jnp.arange(embed.shape[0], dtype=jnp.int32)).astype(F32)[:, None]
        number = jnp.arange(rows, dtype=jnp.int32)
        of_frame, of_place = number // place, number % place
        seg_row = jnp.repeat(segments, place)
        open_row = jnp.repeat(frame_mask, place)
        allowed = (
            (seg_row[:, None] == seg_row[None, :])
            & (of_place[:, None] == of_place[None, :])
            & (of_frame[None, :] <= of_frame[:, None])
            & ((open_row[None, :] == 1) | (of_frame[None, :] == of_frame[:, None]))
        )
        bias = jnp.where(allowed, 0.0, -1e30).astype(F32)
        nothing = jnp.zeros((1, width), F32)
        w_qs, w_os, w_qt, w_ot, w_in, w_out = (lax.all_gather(m, "frame", axis=0, tiled=True) for m in mats)
        base1 = lax.all_to_all(tokens, "tile", 0, 0, tiled=True).reshape(rows, width)
        g = lax.all_to_all(grad4.transpose(1, 0, 2, 3), "frame", 0, 0, tiled=True).reshape(rows, width)
        unit1, qkv1, mixed1, after1 = attn_fwd(
            base1, added, vecs[0], vecs[1], w_qs, w_os, None, BF16, "spatial_forward")
        base2 = turn(after1, True)
        unit2, qkv2, mixed2, after2 = attn_fwd(
            base2, nothing, vecs[2], vecs[3], w_qt, w_ot, bias, F32, "temporal_forward")
        unit3 = plain_norm(after2, ln3_gain, ln3_shift).astype(BF16)
        pre = jnp.dot(unit3, w_in, preferred_element_type=F32) + ffn_in_bias
        th = jnp.tanh(GELU_A * (pre + GELU_B * pre * pre * pre))
        act = (0.5 * pre * (1.0 + th)).astype(BF16)
        slope = 0.5 * (1.0 + th) + 0.5 * pre * (1.0 - th * th) * GELU_A * (1.0 + 3.0 * GELU_B * pre * pre)
        slope = slope.astype(BF16)
        result = after2 + jnp.dot(act, w_out, preferred_element_type=F32) + ffn_out_bias
        result = result.astype(BF16).reshape(n_frame, frames_dev, place, width)
        result = lax.all_to_all(result, "frame", 0, 0, tiled=True).transpose(1, 0, 2, 3)
        d_pre, d_after2, dg3, ds3, d_bin, d_bout = ffn_bwd(g, slope, after2, vecs[4], w_in, w_out)
        low2, d_qkv2, d_after1, dg2, ds2 = attn_bwd(
            base2, nothing, vecs[2], w_qt, w_ot, d_after2, qkv2, bias, BF16, "temporal_backward")
        d_out1 = turn(d_after1, False)
        low1, d_qkv1, d_start, dg1, ds1 = attn_bwd(
            base1, added, vecs[0], w_qs, w_os, d_out1, qkv1, None, F32, "spatial_backward")
        tokens_grad = d_start.astype(BF16).reshape(n_tile, tile_tokens, width)
        tokens_grad = lax.all_to_all(tokens_grad, "tile", 0, 0, tiled=True)
        d_embed = one_hot * jnp.sum(d_start, 0, keepdims=True)
        pairs = ((unit1, d_qkv1), (mixed1, low1), (unit2, d_qkv2), (mixed2, low2), (unit3, d_pre), (act, g))
        summed = []
        for a, b in pairs:
            part = lax.dot_general(a, b, (((0,), (0,)), ((), ())), preferred_element_type=F32)
            part = lax.psum_scatter(part, "frame", scatter_dimension=0, tiled=True)
            summed.append(lax.psum(part.astype(BF16), "tile").astype(F32))
        d_embed, dg1, ds1, dg2, ds2, dg3, ds3, d_bin, d_bout = lax.psum(
            (d_embed, dg1[0], ds1[0], dg2[0], ds2[0], dg3[0], ds3[0], d_bin[0], d_bout[0]), ("frame", "tile"))

    result = result.reshape(tokens.shape)
    return (result, tokens_grad, d_embed, dg1, ds1, summed[0], summed[1], dg2, ds2, summed[2], summed[3],
            dg3, ds3, summed[4], d_bin, summed[5], d_bout)


def solution(mesh):
    shard = P("frame", "tile", None)
    mat = P("frame", None)
    rep = P()
    in_specs = (shard, shard, P("frame"), rep, rep, rep, rep, rep, mat, mat, rep, rep, mat, mat,
                rep, rep, mat, rep, mat, rep)
    out_specs = (shard, shard, rep, rep, rep, mat, mat, rep, rep, mat, mat, rep, rep, mat, rep, mat, rep)
    on_boxes = mesh.shape["frame"] == 8 and mesh.shape["tile"] == 4
    return jax.shard_map(
        functools.partial(per_device, on_boxes),
        mesh=mesh, in_specs=in_specs, out_specs=out_specs, check_vma=False)
```
